32 devices in a mesh: dp: 8 (over z, y), tensor: 4 (over x, core).
Axes of the slice: x: 2, y: 2, z: 4, core: 2. Of those that a mesh axis runs over, the one named last changes fastest.
Arguments:
- text_in: bfloat16 [32, 512, 768], P('dp', 'tensor'), may hold values from -20 to 20, as said below
- layout_in: bfloat16 [32, 98304], P('dp', 'tensor'), may hold values from -20 to 20, as said below
- segment_ids: int32 [32, 512], P('dp', 'tensor'), may hold values from 0 to 3, never falling along the last dimension, each value on 1 to 256 neighbouring positions
- box_bins: int32 [32, 1024], P('dp', 'tensor'), may hold values from 0 to 1023
- text_cot: bfloat16 [32, 512, 768], P('dp', 'tensor'), may hold values from -20 to 20, as said below
- layout_cot: bfloat16 [32, 98304], P('dp', 'tensor'), may hold values from -20 to 20, as said below
- attend_text: float32 [768, 4, 768], P('dp', None, 'tensor'), as said below
- attend_text_mean: float32 [768, 4, 768], P('dp', None, 'tensor'), may hold values from -0.00024414062 to 0.00024414062
- attend_text_square: float32 [768, 4, 768], P('dp', None, 'tensor'), may hold values from 1.2939316e-10 to 5.1757265e-10
- feed_text: float32 [768, 2, 3072], P('dp', None, 'tensor'), as said below
- feed_text_mean: float32 [768, 2, 3072], P('dp', None, 'tensor'), may hold values from -0.00024414062 to 0.00024414062
- feed_text_square: float32 [768, 2, 3072], P('dp', None, 'tensor'), may hold values from 1.2939316e-10 to 5.1757265e-10
- attend_layout: float32 [192, 4, 192], P('dp', None, 'tensor'), as said below
- attend_layout_mean: float32 [192, 4, 192], P('dp', None, 'tensor'), may hold values from -0.00024414062 to 0.00024414062
- attend_layout_square: float32 [192, 4, 192], P('dp', None, 'tensor'), may hold values from 1.2939316e-10 to 5.1757265e-10
- feed_layout: float32 [192, 2, 768], P('dp', None, 'tensor'), as said below
- feed_layout_mean: float32 [192, 2, 768], P('dp', None, 'tensor'), may hold values from -0.00024414062 to 0.00024414062
- feed_layout_square: float32 [192, 2, 768], P('dp', None, 'tensor'), may hold values from 1.2939316e-10 to 5.1757265e-10
- vectors: float32 [11520], replicated, as said below
- vectors_mean: float32 [11520], replicated, may hold values from -0.00024414062 to 0.00024414062
- vectors_square: float32 [11520], replicated, may hold values from 1.2939316e-10 to 5.1757265e-10
- tables: float32 [196608], replicated, may hold values from -3 to 3
- tables_mean: float32 [196608], replicated, may hold values from -7.6293945e-06 to 7.6293945e-06
- tables_square: float32 [196608], replicated, may hold values from 1.2636051e-13 to 5.0544204e-13
Outputs:
- out_text: bfloat16 [32, 512, 768], P('dp', 'tensor')
- out_layout: bfloat16 [32, 98304], P('dp', 'tensor')
- grad_text: float32 [32, 512, 768], P('dp', 'tensor')
- grad_layout: float32 [32, 98304], P('dp', 'tensor')
- new_attend_text: float32 [768, 4, 768], P('dp', None, 'tensor')
- new_attend_text_mean: float32 [768, 4, 768], P('dp', None, 'tensor')
- new_attend_text_square: float32 [768, 4, 768], P('dp', None, 'tensor')
- new_feed_text: float32 [768, 2, 3072], P('dp', None, 'tensor')
- new_feed_text_mean: float32 [768, 2, 3072], P('dp', None, 'tensor')
- new_feed_text_square: float32 [768, 2, 3072], P('dp', None, 'tensor')
- new_attend_layout: float32 [192, 4, 192], P('dp', None, 'tensor')
- new_attend_layout_mean: float32 [192, 4, 192], P('dp', None, 'tensor')
- new_attend_layout_square: float32 [192, 4, 192], P('dp', None, 'tensor')
- new_feed_layout: float32 [192, 2, 768], P('dp', None, 'tensor')
- new_feed_layout_mean: float32 [192, 2, 768], P('dp', None, 'tensor')
- new_feed_layout_square: float32 [192, 2, 768], P('dp', None, 'tensor')
- new_vectors: float32 [11520], replicated
- new_vectors_mean: float32 [11520], replicated
- new_vectors_square: float32 [11520], replicated
- new_tables: float32 [196608], replicated
- new_tables_mean: float32 [196608], replicated
- new_tables_square: float32 [196608], replicated
- clip_norm: float32 [], replicated
The draws below stay inside these ranges and needn't reach their ends.
Inputs may be any that keep to these rules, and one draw needn't show every extreme that they name: `text_in`: entries are independent and of order one. `layout_in`: entries are independent and of order one. `text_cot`: entries are independent and of order one. `layout_cot`: entries are independent and of order one. `attend_text`: entries are independent; the query, key, value slots have spread of order 1 / sqrt of the width, the output projection slot a larger one. `attend_layout`: entries are independent; the query, key, value slots have spread of order 1 / sqrt of the width, the output projection slot a larger one. `feed_text`: entries are independent with spread of order 1 / sqrt of the fan-in. `feed_layout`: entries are independent with spread of order 1 / sqrt of the fan-in. `vectors`: gains near one, biases of both signs.
All inputs are finite; a program needn't handle non-finite values.
Results may differ from the reference program's by a relative error of at most 0.017.
The reference program's roundings to bfloat16 on the way count: a program that leaves them out, or rounds other values in their place, can miss the bound.
Values may be sent and summed in bfloat16 or wider, within the bound.
No kernel may reach another device: no remote copies, remote signals or barrier semaphores. Data moves between devices by JAX's collectives and lax.ppermute only.
A program may use at most 128 MiB of HBM per device.

```python
import math
import jax
import jax.numpy as jnp
import numpy as np
from jax import lax

HEADS = 12
HD = 64
LHD = 16
FF = 3072
LF = 768
BINS = 1024
PAGE = 512
STEP = 10
D = 768
L = 192
PAGES = 32
NV = 11520
PTOT = 7728384


def stacked_normal(key, dims_shape, scales):
    values = jax.random.truncated_normal(key, -4.0, 4.0, dims_shape, jnp.float32)
    return values * jnp.array(scales, jnp.float32)[None, :, None]


def column_rows(key, dims_shape, column_pos, width_now):
    ratio = column_pos.astype(jnp.float32) / (width_now - 1)
    entries = jax.random.truncated_normal(key, -4.0, 4.0, dims_shape, jnp.float32)
    scales = jnp.exp(ratio * jnp.log(3.0))
    return entries * scales


def draw_text_in(key, part):
    own_key = jax.random.fold_in(key, 11)
    column_pos = jnp.arange(D)[None, None, :]
    return column_rows(own_key, (PAGES, PAGE, D), column_pos, D).astype(jnp.bfloat16)


def draw_text_cot(key, part):
    own_key = jax.random.fold_in(key, 12)
    column_pos = jnp.arange(D)[None, None, :]
    return column_rows(own_key, (PAGES, PAGE, D), column_pos, D).astype(jnp.bfloat16)


def draw_layout_in(key, part):
    own_key = jax.random.fold_in(key, 13)
    column_pos = (jnp.arange(PAGE * L) % L)[None, :]
    return column_rows(own_key, (PAGES, PAGE * L), column_pos, L).astype(jnp.bfloat16)


def draw_layout_cot(key, part):
    own_key = jax.random.fold_in(key, 14)
    column_pos = (jnp.arange(PAGE * L) % L)[None, :]
    return column_rows(own_key, (PAGES, PAGE * L), column_pos, L).astype(jnp.bfloat16)


def draw_attend_text(key, part):
    inner = D ** (-0.5)
    return stacked_normal(jax.random.fold_in(key, 21), (D, 4, D), [inner, inner, inner, (64.0 / D) ** 0.5])


def draw_attend_layout(key, part):
    inner = L ** (-0.5)
    return stacked_normal(jax.random.fold_in(key, 22), (L, 4, L), [inner, inner, inner, (64.0 / L) ** 0.5])


def draw_feed_text(key, part):
    return stacked_normal(jax.random.fold_in(key, 23), (D, 2, FF), [D ** (-0.5), FF ** (-0.5)])


def draw_feed_layout(key, part):
    return stacked_normal(jax.random.fold_in(key, 24), (L, 2, LF), [L ** (-0.5), LF ** (-0.5)])


def draw_vectors(key, part):
    positions = jnp.arange(NV)
    base_draw = jax.random.truncated_normal(jax.random.fold_in(key, 25), -4.0, 4.0, (NV,), jnp.float32)
    text_slot = positions // D
    layout_pos = positions - (8 * D + FF)
    layout_slot = layout_pos // L
    in_text = positions < 8 * D
    in_layout = (layout_pos >= 0) & (layout_pos < 8 * L)
    text_gain = in_text & ((text_slot == 3) | (text_slot == 6))
    layout_gain = in_layout & ((layout_slot == 3) | (layout_slot == 6))
    return jnp.where(text_gain | layout_gain, 1.0 + 0.15 * base_draw, 0.3 * base_draw)


def place_ends(values, stream_key, least, high):
    extent = values.shape
    index_at = [jax.random.randint(jax.random.fold_in(stream_key, axis), (), 0, extent[axis]) for axis in range(len(extent))]
    values = values.at[tuple(index_at)].set(least)
    longest = extent.index(max(extent))
    index_at[longest] = (index_at[longest] + 1) % extent[longest]
    return values.at[tuple(index_at)].set(high)


def shard_levels(key, extent, shards, smallest, largest):
    loudness, own = 1.0, jax.random.fold_in(key, 6)
    for dim, parts in shards:
        heights = jnp.exp(jax.random.uniform(jax.random.fold_in(own, dim), (parts,), jnp.float32, smallest / len(shards), largest / len(shards)))
        loudness = loudness * jnp.repeat(heights, extent[dim] // parts).reshape([-1 if axis == dim else 1 for axis in range(len(extent))])
    return loudness


def length_profile(amount, total, reach, slope):
    portions = [(1 << 20) // math.isqrt(grade ** slope) + 1 for grade in range(2, amount + 1)]
    surplus, counts = total - reach - (amount - 1), [1] * (amount - 1)
    while surplus > 0:
        movable = [i for i in range(amount - 1) if counts[i] < reach]
        whole, left = sum([portions[i] for i in movable]), surplus
        for i in movable:
            addition = min(reach - counts[i], max(1, left * portions[i] // whole), surplus)
            counts[i] = counts[i] + addition
            surplus = surplus - addition
    return np.array([reach] + counts)


def uneven_parts(key, number_of, total, reach, lean):
    if number_of == 2:
        one = jax.random.randint(key, (), max(1, total - reach), min(reach, total - 1) + 1)
        return jnp.stack([one, total - one])
    lengths = jnp.asarray(length_profile(number_of, total, reach, lean), jnp.int32)
    pairs = (number_of - 1) // 2
    source_of, sink = lengths[1:1 + 2 * pairs:2], lengths[2:2 + 2 * pairs:2]
    margin = jnp.minimum(source_of - 1, reach - sink)
    moved = jax.random.randint(jax.random.fold_in(key, 1), (pairs,), 0, 1 << 20) % (margin + 1)
    lengths = lengths.at[1:1 + 2 * pairs:2].set(source_of - moved).at[2:2 + 2 * pairs:2].set(sink + moved)
    return lengths[jax.random.permutation(jax.random.fold_in(key, 2), number_of)]


def bell_draw(rng, shape, deviation, most, shards=(), dtype=jnp.bfloat16):
    drawn = deviation * jax.random.normal(rng, shape, jnp.float32)
    if shards:
        drawn = drawn * shard_levels(rng, shape, shards, -0.22, 0.18)
    return jnp.clip(drawn, -most, most).astype(dtype)


def setup_inputs(seed: int = 0) -> dict:
    key_list = jax.random.split(jax.random.key(seed), 25)
    text_in = draw_text_in(jax.random.fold_in(key_list[24], 71), 0)
    layout_in = draw_layout_in(jax.random.fold_in(key_list[24], 71), 0)
    segment_ids = jax.vmap(lambda own: jnp.searchsorted(jnp.cumsum(uneven_parts(own, 4, PAGE, PAGE // 2, 1)), jnp.arange(PAGE), side="right"))(jax.random.split(key_list[2], PAGES)).reshape((PAGES, PAGE)).astype(jnp.int32)
    box_bins = place_ends(jax.random.randint(key_list[3], (PAGES, PAGE * 2), 0, BINS), jax.random.fold_in(key_list[3], 1), 0, BINS - 1).astype(jnp.int32)
    text_cot = draw_text_cot(jax.random.fold_in(key_list[24], 71), 0)
    layout_cot = draw_layout_cot(jax.random.fold_in(key_list[24], 71), 0)
    attend_text = draw_attend_text(jax.random.fold_in(key_list[24], 71), 0)
    attend_text_mean = bell_draw(key_list[7], (D, 4, D), (0.11 / PTOT ** 0.5), 0.00024414062, ((0, 8), (2, 4)), jnp.float32)
    attend_text_square = jnp.clip(jnp.exp(math.log(5.175726514039525e-10) - 1.3862944 * jax.random.uniform(key_list[8], (D, 4, D), jnp.float32) ** shard_levels(key_list[8], (D, 4, D), ((0, 8), (2, 4)), -0.2, 0.2)), 1.2939316285098812e-10, 5.175726514039525e-10)
    feed_text = draw_feed_text(jax.random.fold_in(key_list[24], 71), 0)
    feed_text_mean = bell_draw(key_list[10], (D, 2, FF), (0.11 / PTOT ** 0.5), 0.00024414062, ((0, 8), (2, 4)), jnp.float32)
    feed_text_square = jnp.clip(jnp.exp(math.log(5.175726514039525e-10) - 1.3862944 * jax.random.uniform(key_list[11], (D, 2, FF), jnp.float32) ** shard_levels(key_list[11], (D, 2, FF), ((0, 8), (2, 4)), -0.2, 0.2)), 1.2939316285098812e-10, 5.175726514039525e-10)
    attend_layout = draw_attend_layout(jax.random.fold_in(key_list[24], 71), 0)
    attend_layout_mean = bell_draw(key_list[13], (L, 4, L), (0.11 / PTOT ** 0.5), 0.00024414062, ((0, 8), (2, 4)), jnp.float32)
    attend_layout_square = jnp.clip(jnp.exp(math.log(5.175726514039525e-10) - 1.3862944 * jax.random.uniform(key_list[14], (L, 4, L), jnp.float32) ** shard_levels(key_list[14], (L, 4, L), ((0, 8), (2, 4)), -0.2, 0.2)), 1.2939316285098812e-10, 5.175726514039525e-10)
    feed_layout = draw_feed_layout(jax.random.fold_in(key_list[24], 71), 0)
    feed_layout_mean = bell_draw(key_list[16], (L, 2, LF), (0.11 / PTOT ** 0.5), 0.00024414062, ((0, 8), (2, 4)), jnp.float32)
    feed_layout_square = jnp.clip(jnp.exp(math.log(5.175726514039525e-10) - 1.3862944 * jax.random.uniform(key_list[17], (L, 2, LF), jnp.float32) ** shard_levels(key_list[17], (L, 2, LF), ((0, 8), (2, 4)), -0.2, 0.2)), 1.2939316285098812e-10, 5.175726514039525e-10)
    vectors = draw_vectors(jax.random.fold_in(key_list[24], 71), 0)
    vectors_mean = bell_draw(key_list[19], (NV,), (0.11 / PTOT ** 0.5), 0.00024414062, (), jnp.float32)
    vectors_square = jnp.clip(jnp.exp(jax.random.uniform(key_list[20], (NV,), jnp.float32, math.log(1.2939316285098812e-10), math.log(5.175726514039525e-10))), 1.2939316285098812e-10, 5.175726514039525e-10)
    tables = bell_draw(key_list[21], (BINS * L,), 0.5, 3.0, (), jnp.float32)
    tables_mean = bell_draw(key_list[22], (BINS * L,), (0.11 / (PTOT * BINS) ** 0.5), 7.62939453125e-06, (), jnp.float32)
    tables_square = jnp.clip(jnp.exp(jax.random.uniform(key_list[23], (BINS * L,), jnp.float32, math.log(1.2636051059666809e-13), math.log(5.054420423866723e-13))), 1.2636051059666809e-13, 5.054420423866723e-13)
    return {"text_in": text_in, "layout_in": layout_in, "segment_ids": segment_ids, "box_bins": box_bins, "text_cot": text_cot, "layout_cot": layout_cot, "attend_text": attend_text, "attend_text_mean": attend_text_mean, "attend_text_square": attend_text_square, "feed_text": feed_text, "feed_text_mean": feed_text_mean, "feed_text_square": feed_text_square, "attend_layout": attend_layout, "attend_layout_mean": attend_layout_mean, "attend_layout_square": attend_layout_square, "feed_layout": feed_layout, "feed_layout_mean": feed_layout_mean, "feed_layout_square": feed_layout_square, "vectors": vectors, "vectors_mean": vectors_mean, "vectors_square": vectors_square, "tables": tables, "tables_mean": tables_mean, "tables_square": tables_square}


@jax.custom_vjp
def low(v):
    return lax.optimization_barrier(v.astype(jnp.bfloat16)).astype(jnp.float32)

@jax.custom_vjp
def low_back(v):
    return v

def low_keep(v):
    return (low(v), None)

def low_pass(kept, grad):
    return (grad,)

def back_keep(v):
    return (v, None)

def back_low(kept, grad):
    return (low(grad),)
low.defvjp(low_keep, low_pass)
low_back.defvjp(back_keep, back_low)
PRECISE = lax.Precision.HIGHEST
NORM_EPS = 1e-05
NEG_FILL = -1000000000.0
CLIP_NORM = 1.0
LEARN_RATES = (0.3, 0.05, 0.3, 0.05, 0.3, 0.3)
BETA_ONE = 0.9
BETA_TWO = 0.999
ADAM_EPS = 1e-08
WEIGHT_DECAY = 0.01

def split_vectors(packed):
    widths = (D, L)
    hidden = (FF, LF)
    result = []
    offset = 0
    for stream in range(2):
        width_now = widths[stream]
        pieces = [packed[offset + slot_index * width_now:offset + (slot_index + 1) * width_now] for slot_index in range(8)]
        offset = offset + 8 * width_now
        result.append((pieces, packed[offset:offset + hidden[stream]]))
        offset = offset + hidden[stream]
    return result

def layer_norm(residual, gain_vec, shift_vec):
    centered = residual - lax.optimization_barrier(jnp.mean(residual, axis=-1, keepdims=True))
    variance = lax.optimization_barrier(jnp.mean(centered * centered, axis=-1, keepdims=True))
    return centered * lax.rsqrt(variance + NORM_EPS) * gain_vec + shift_vec

def softmax_rows(scores_in):
    top_score = lax.optimization_barrier(jnp.max(scores_in, axis=-1, keepdims=True))
    exponent = jnp.exp(scores_in - top_score)
    return exponent / lax.optimization_barrier(jnp.sum(exponent, axis=-1, keepdims=True))

def lookup(tables_flat, bins_in):
    half_width = L // 2
    tables_low = tables_flat.reshape(BINS, L)
    return jnp.concatenate([tables_low[:, :half_width][bins_in[..., 0]], tables_low[:, half_width:][bins_in[..., 1]]], axis=-1)

def attention_inputs(rows_low, weight, bias_q, bias_v, head_dim):
    projected = jnp.einsum('bpd,dcn->bpcn', rows_low, weight[:, :3], precision=PRECISE)
    queries = low(low_back(projected[:, :, 0]) + bias_q)
    key_rows = low(low_back(projected[:, :, 1]))
    values = low(low_back(projected[:, :, 2]) + bias_v)
    head_shape = queries.shape[:2] + (HEADS, head_dim)
    return (queries.reshape(head_shape), key_rows.reshape(head_shape), values.reshape(head_shape))

def head_scores(queries, key_rows, head_dim):
    return jnp.einsum('bqhd,bkhd->bhqk', queries, key_rows, precision=PRECISE) * (1.0 / math.sqrt(head_dim))

def mix_values(probs_in, values):
    mixed = jnp.einsum('bhqk,bkhd->bqhd', low(probs_in), values, precision=PRECISE)
    return low_back(low(mixed)).reshape(mixed.shape[:2] + (-1,))

def branch_tail(residual_in, context, weight_low, feed_low, vector_list, bias_in):
    attended = low_back(jnp.einsum('bpn,dn->bpd', context, weight_low[:, 3], precision=PRECISE))
    first_norm = layer_norm(residual_in + attended + vector_list[2], vector_list[3], vector_list[4])
    gate_in = low_back(jnp.einsum('bpd,df->bpf', low(first_norm), feed_low[:, 0], precision=PRECISE)) + bias_in
    activated = low(jax.nn.gelu(gate_in, approximate=False))
    feed_out = low_back(jnp.einsum('bpf,df->bpd', activated, feed_low[:, 1], precision=PRECISE))
    return layer_norm(first_norm + feed_out + vector_list[5], vector_list[6], vector_list[7])

def forward(params, frozen, text_rows, layout_hidden, segments, bins_in):
    attend_t, feed_t, attend_l, feed_l, packed, tables_in = params
    frozen_attend, frozen_packed, frozen_tables, frozen_hidden = frozen
    text_parts, layout_parts = split_vectors(packed)
    frozen_parts = split_vectors(frozen_packed)[1][0]
    weight_text = low(attend_t)
    weight_layout = low(attend_l)
    layout_rows = layout_hidden + lookup(low(tables_in), bins_in)
    frozen_rows = frozen_hidden + lookup(low(frozen_tables), bins_in)
    q_text, k_text, v_text = attention_inputs(low(text_rows), weight_text, text_parts[0][0], text_parts[0][1], HD)
    q_lay, k_lay, v_lay = attention_inputs(low(layout_rows), weight_layout, layout_parts[0][0], layout_parts[0][1], LHD)
    q_frozen, k_frozen, v_frozen = attention_inputs(low(frozen_rows), low(frozen_attend), frozen_parts[0], frozen_parts[1], LHD)
    same_doc = (segments[:, :, None] == segments[:, None, :])[:, None]
    s_text = low_back(head_scores(q_text, k_text, HD))
    s_lay = low_back(head_scores(q_lay, k_lay, LHD))
    s_frozen = head_scores(q_frozen, k_frozen, LHD)
    p_text = softmax_rows(jnp.where(same_doc, s_text + s_frozen, NEG_FILL))
    p_lay = softmax_rows(jnp.where(same_doc, s_lay + s_text, NEG_FILL))
    out_text = branch_tail(text_rows, mix_values(p_text, v_text), weight_text, low(feed_t), text_parts[0], text_parts[1])
    out_layout = branch_tail(layout_rows, mix_values(p_lay, v_lay), weight_layout, low(feed_l), layout_parts[0], layout_parts[1])
    return (out_text, out_layout)

def adamw_step(weight, moment, square, gradient, decay_rate, rate_now):
    new_moment = BETA_ONE * moment + (1.0 - BETA_ONE) * gradient
    new_square = BETA_TWO * square + (1.0 - BETA_TWO) * gradient * gradient
    moment_hat = new_moment / (1.0 - BETA_ONE ** STEP)
    square_hat = new_square / (1.0 - BETA_TWO ** STEP)
    new_weight = weight - rate_now * (moment_hat / (jnp.sqrt(square_hat) + ADAM_EPS) + decay_rate * weight)
    return (new_weight, new_moment, new_square)

def reference(text_in, layout_in, segment_ids, box_bins, text_cot, layout_cot, attend_text, attend_text_mean, attend_text_square, feed_text, feed_text_mean, feed_text_square, attend_layout, attend_layout_mean, attend_layout_square, feed_layout, feed_layout_mean, feed_layout_square, vectors, vectors_mean, vectors_square, tables, tables_mean, tables_square):
    layout_in = layout_in.reshape(PAGES, PAGE, L)
    layout_cot = layout_cot.reshape(PAGES, PAGE, L)
    box_bins = box_bins.reshape(PAGES, PAGE, 2)
    params = tuple((array_in.astype(jnp.float32) for array_in in (attend_text, feed_text, attend_layout, feed_layout, vectors, tables)))
    block_pages = math.gcd(PAGES, 4)

    def blocks(array_in):
        return array_in.reshape((PAGES // block_pages, block_pages) + array_in.shape[1:])

    def scan_step(totals, block_item):
        text_block, layout_block, seg_block, bins_block, cot_text, cot_layout = block_item
        layout_full = layout_block.astype(jnp.float32)
        frozen = (params[2], params[4], params[5], layout_full)

        def run_layer(weights_in, text_full, layout_arg):
            return forward(weights_in, frozen, text_full, layout_arg, seg_block, bins_block)
        outputs, pullback = jax.vjp(run_layer, params, text_block.astype(jnp.float32), layout_full)
        gradients, grad_text_block, grad_layout_block = pullback((cot_text.astype(jnp.float32), cot_layout.astype(jnp.float32)))
        totals = jax.tree.map(jnp.add, totals, gradients)
        return (totals, (outputs[0].astype(jnp.bfloat16), outputs[1].astype(jnp.bfloat16), grad_text_block, grad_layout_block))
    zero_grads = jax.tree.map(jnp.zeros_like, params)
    inputs_blocked = tuple((blocks(array_in) for array_in in (text_in, layout_in, segment_ids, box_bins, text_cot, layout_cot)))
    gradients, stacked = lax.scan(scan_step, zero_grads, inputs_blocked)

    def unblock(array_in):
        return array_in.reshape((PAGES,) + array_in.shape[2:])
    out_text = unblock(stacked[0])
    out_layout = unblock(stacked[1]).reshape(PAGES, PAGE * L)
    grad_text = unblock(stacked[2])
    grad_layout = unblock(stacked[3]).reshape(PAGES, PAGE * L)
    total_sq = sum((jnp.sum(member_grad * member_grad) for member_grad in gradients))
    clip_norm = jnp.sqrt(total_sq)
    factor = jnp.minimum(1.0, CLIP_NORM / (clip_norm + 1e-06))
    moments = (attend_text_mean, feed_text_mean, attend_layout_mean, feed_layout_mean, vectors_mean, tables_mean)
    seconds = (attend_text_square, feed_text_square, attend_layout_square, feed_layout_square, vectors_square, tables_square)
    decays = (WEIGHT_DECAY, WEIGHT_DECAY, WEIGHT_DECAY, WEIGHT_DECAY, 0.0, 0.0)
    updated = [adamw_step(params[which_param], moments[which_param], seconds[which_param], gradients[which_param] * factor, decays[which_param], LEARN_RATES[which_param]) for which_param in range(6)]
    return (out_text, out_layout, grad_text, grad_layout, updated[0][0], updated[0][1], updated[0][2], updated[1][0], updated[1][1], updated[1][2], updated[2][0], updated[2][1], updated[2][2], updated[3][0], updated[3][1], updated[3][2], updated[4][0], updated[4][1], updated[4][2], updated[5][0], updated[5][1], updated[5][2], clip_norm)
```

```python
import functools
import math

import jax
import jax.numpy as jnp
from jax import lax
from jax.experimental import pallas as pl
from jax.experimental.pallas import tpu as pltpu
from jax.sharding import PartitionSpec as P

HD = 64
LHD = 16
STEP = 10

NORM_EPS = 1e-05
NEG_FILL = -1000000000.0
CLIP_NORM = 1.0
LEARN_RATES = (0.3, 0.05, 0.3, 0.05, 0.3, 0.3)
BETA_ONE = 0.9
BETA_TWO = 0.999
ADAM_EPS = 1e-08
WEIGHT_DECAY = 0.01
AXES = ("dp", "tensor")
LAY_ROWS = 32
F32 = jnp.float32
BF16 = jnp.bfloat16


def to_low(values):
    return values.astype(BF16)


def xor_send(values, total, distance):
    return lax.ppermute(values, AXES, [(i, i ^ distance) for i in range(total)])


def split_vectors(packed, widths, hidden):
    result = []
    offset = 0
    for stream in range(2):
        width_now = widths[stream]
        pieces = [packed[offset + k * width_now : offset + (k + 1) * width_now] for k in range(8)]
        offset = offset + 8 * width_now
        result.append((pieces, packed[offset : offset + hidden[stream]]))
        offset = offset + hidden[stream]
    return result


def norm_forward(residual, gain_vec, shift_vec):
    centered = residual - jnp.mean(residual, axis=-1, keepdims=True)
    inv_std = lax.rsqrt(jnp.mean(centered * centered, axis=-1, keepdims=True) + NORM_EPS)
    normed = centered * inv_std
    return (normed * gain_vec + shift_vec, normed, inv_std)


def norm_backward(gradient, normed, inv_std, gain_vec):
    scaled = gradient * gain_vec
    d_resid = inv_std * (
        scaled
        - jnp.mean(scaled, axis=-1, keepdims=True)
        - normed * jnp.mean(scaled * normed, axis=-1, keepdims=True)
    )
    return (d_resid, jnp.sum(gradient * normed, axis=0), jnp.sum(gradient, axis=0))


def gelu_exact(values):
    return jax.nn.gelu(values, approximate=False)


def gelu_backward(gate_in, gradient):
    return jax.vjp(gelu_exact, gate_in)[1](gradient)[0]


def page_logits(q_text, k_text, q_lay, k_lay, segments):
    s_text = jnp.einsum("qhd,khd->hqk", q_text, k_text, preferred_element_type=F32) * (
        1.0 / math.sqrt(HD)
    )
    s_lay = jnp.einsum("qhd,khd->hqk", q_lay, k_lay, preferred_element_type=F32) * (
        1.0 / math.sqrt(LHD)
    )
    same_doc = (segments[:, None] == segments[None, :])[None]
    return jnp.where(same_doc, s_text + s_lay, NEG_FILL)


def page_forward(q_text, k_text, v_text, q_lay, k_lay, v_lay, segments):
    logits = page_logits(q_text, k_text, q_lay, k_lay, segments)
    top_score = jnp.max(logits, axis=-1, keepdims=True)
    exponent = jnp.exp(logits - top_score)
    row_total = jnp.sum(exponent, axis=-1, keepdims=True)
    probs_low = to_low(exponent / row_total)
    ctx_text = to_low(jnp.einsum("hqk,khd->qhd", probs_low, v_text, preferred_element_type=F32))
    ctx_lay = to_low(jnp.einsum("hqk,khd->qhd", probs_low, v_lay, preferred_element_type=F32))
    return (ctx_text, ctx_lay, top_score + jnp.log(row_total))


def page_backward(
    q_text, k_text, v_text, q_lay, k_lay, v_lay, segments, log_total, d_ctx_text, d_ctx_lay
):
    probs_full = jnp.exp(page_logits(q_text, k_text, q_lay, k_lay, segments) - log_total)
    probs_low = to_low(probs_full)

    def softmax_back(d_context, values):
        d_probs = jnp.einsum("qhd,khd->hqk", d_context, values, preferred_element_type=F32)
        d_values = jnp.einsum("hqk,qhd->khd", probs_low, d_context, preferred_element_type=F32)
        d_logits = probs_full * (d_probs - jnp.sum(probs_full * d_probs, axis=-1, keepdims=True))
        return (d_logits, d_values)

    dz_text, dv_text = softmax_back(d_ctx_text, v_text)
    dz_lay, dv_lay = softmax_back(d_ctx_lay, v_lay)
    ds_text = to_low(dz_text + dz_lay)
    ds_lay = to_low(dz_lay)
    scale_text = 1.0 / math.sqrt(HD)
    scale_lay = 1.0 / math.sqrt(LHD)
    dq_text = jnp.einsum("hqk,khd->qhd", ds_text, k_text, preferred_element_type=F32) * scale_text
    dk_text = jnp.einsum("hqk,qhd->khd", ds_text, q_text, preferred_element_type=F32) * scale_text
    dq_lay = jnp.einsum("hqk,khd->qhd", ds_lay, k_lay, preferred_element_type=F32) * scale_lay
    dk_lay = jnp.einsum("hqk,qhd->khd", ds_lay, q_lay, preferred_element_type=F32) * scale_lay
    return (dq_text, dk_text, dv_text, dq_lay, dk_lay, dv_lay)


def adamw_step(weight, moment, square, gradient, decay_rate, rate_now):
    new_moment = BETA_ONE * moment + (1.0 - BETA_ONE) * gradient
    new_square = BETA_TWO * square + (1.0 - BETA_TWO) * gradient * gradient
    moment_hat = new_moment / (1.0 - BETA_ONE**STEP)
    square_hat = new_square / (1.0 - BETA_TWO**STEP)
    new_weight = weight - rate_now * (
        moment_hat / (jnp.sqrt(square_hat) + ADAM_EPS) + decay_rate * weight
    )
    return (new_weight, new_moment, new_square)


def reorder(blocks, own_index):
    def body(own_ref, in_ref, out_ref):
        out_ref[...] = in_ref[...]

    count, rows, cols = blocks.shape
    return pl.pallas_call(
        body,
        grid_spec=pltpu.PrefetchScalarGridSpec(
            num_scalar_prefetch=1,
            grid=(count,),
            in_specs=[pl.BlockSpec((1, rows, cols), lambda i, own: (i, 0, 0))],
            out_specs=pl.BlockSpec((1, rows, cols), lambda i, own: (i ^ own[0], 0, 0)),
        ),
        out_shape=jax.ShapeDtypeStruct(blocks.shape, blocks.dtype),
    )(own_index, blocks)


def gather_shards(shard, total):
    far = total // 8
    rows, cols = shard.shape
    half = rows // 2
    stacked = jnp.stack([shard] + [xor_send(shard, total, 8 * r) for r in range(1, far)])

    def two_more(part, first, second):
        part = jnp.stack([part, xor_send(part, total, first)])
        return jnp.stack([part, xor_send(part, total, second)])

    low_half = two_more(stacked[:, :half], 2, 4)
    high_half = two_more(stacked[:, half:], 4, 2)
    both = (low_half, xor_send(low_half, total, 1), high_half, xor_send(high_half, total, 1))
    low_all = jnp.stack([both[0], both[1]])
    high_all = jnp.stack([both[2], both[3]])
    low_all = low_all.transpose(3, 1, 2, 0, 4, 5).reshape(total, half, cols)
    high_all = high_all.transpose(3, 2, 1, 0, 4, 5).reshape(total, rows - half, cols)
    return jnp.concatenate([low_all, high_all], axis=1)


def reduce_shards(blocks, total):
    far = total // 8
    rows, cols = blocks.shape[1:]
    half = rows // 2
    parts = blocks.reshape(far, 2, 2, 2, rows, cols)

    def add(mine, theirs):
        return to_low(mine.astype(F32) + theirs.astype(F32))

    chip = add(parts[:, :, :, 0], xor_send(parts[:, :, :, 1], total, 1))
    low, high = chip[..., :half, :], chip[..., half:, :]
    low = add(low[:, :, 0], xor_send(low[:, :, 1], total, 2))
    high = add(high[:, 0], xor_send(high[:, 1], total, 4))
    low = add(low[:, 0], xor_send(low[:, 1], total, 4))
    high = add(high[:, 0], xor_send(high[:, 1], total, 2))
    line = jnp.concatenate([low, high], axis=1)
    out = line[0].astype(F32)
    for r in range(1, far):
        out = out + xor_send(line[r], total, 8 * r).astype(F32)
    return out


def sum_everywhere(values, total):
    distance = 1
    while distance < total:
        values = values + xor_send(values, total, distance)
        distance = distance * 2
    return values


def reduce_small(values, total):
    me = lax.axis_index("dp") * lax.axis_size("tensor") + lax.axis_index("tensor")
    distance = 1
    sizes = []
    while distance < total:
        half = values.shape[0] // 2
        bit = (me // distance) % 2
        mine = lax.dynamic_slice_in_dim(values, bit * half, half)
        other = lax.dynamic_slice_in_dim(values, (1 - bit) * half, half)
        values = mine + xor_send(to_low(other), total, distance).astype(F32)
        sizes.append(distance)
        distance = distance * 2
    square_sum = jnp.sum(values * values)
    for distance in reversed(sizes):
        bit = (me // distance) % 2
        other = xor_send(values, total, distance)
        values = jnp.where(
            bit == 0, jnp.concatenate([values, other]), jnp.concatenate([other, values])
        )
    return values, square_sum


def on_device(
    text_in,
    layout_in,
    segment_ids,
    box_bins,
    text_cot,
    layout_cot,
    attend_text,
    attend_text_mean,
    attend_text_square,
    feed_text,
    feed_text_mean,
    feed_text_square,
    attend_layout,
    attend_layout_mean,
    attend_layout_square,
    feed_layout,
    feed_layout_mean,
    feed_layout_square,
    vectors,
    vectors_mean,
    vectors_square,
    tables,
    tables_mean,
    tables_square,
):
    n_dp, n_t = lax.axis_size("dp"), lax.axis_size("tensor")
    total = n_dp * n_t
    t_pos = lax.axis_index("tensor")
    me = lax.axis_index("dp") * n_t + t_pos
    me_arr = me.astype(jnp.int32).reshape(1)
    pages, quarter, wt = text_in.shape
    wl = layout_in.shape[1] // quarter
    rows = quarter * n_t
    widths = [wt, wl]
    head_dims = [HD, LHD]
    d_own, dl_own = attend_text.shape[0], attend_layout.shape[0]
    ct, cl = attend_text.shape[2], attend_layout.shape[2]
    ht, hl = feed_text.shape[2], feed_layout.shape[2]

    def page_of(values):
        take = lambda r: lax.dynamic_index_in_dim(values, t_pos ^ r, 0, keepdims=False)
        return jnp.concatenate([take(0)] + [xor_send(take(r), total, r) for r in range(1, n_t)])

    def pages_of(page):
        blocks = page.reshape(n_t, quarter, page.shape[-1])
        parts = [blocks[0]] + [xor_send(blocks[r], total, r) for r in range(1, n_t)]
        out = jnp.zeros((n_t,) + parts[0].shape, parts[0].dtype)
        for r in range(n_t):
            out = lax.dynamic_update_slice(out, parts[r][None], (t_pos ^ r, 0, 0))
        return out

    lay_pack = jnp.concatenate(
        [
            to_low(attend_layout).reshape(dl_own, 4 * cl),
            to_low(feed_layout).reshape(dl_own, 2 * hl),
        ],
        axis=1,
    )
    lay_cols = lay_pack.shape[1]
    lay_pack = jnp.pad(lay_pack, ((0, LAY_ROWS - dl_own), (0, 4 * ct - lay_cols)))
    attend_pack = jnp.concatenate([to_low(attend_text).reshape(d_own, 4 * ct), lay_pack])
    feed_pack = to_low(feed_text).transpose(1, 0, 2).reshape(2 * d_own, ht)
    attend_all = reorder(gather_shards(attend_pack, total), me_arr)
    feed_all = reorder(gather_shards(feed_pack, total), me_arr)
    attend_all = attend_all.reshape(n_dp, n_t, d_own + LAY_ROWS, 4 * ct)
    w_text = attend_all[:, :, :d_own].reshape(n_dp, n_t, d_own, 4, ct)
    w_text = w_text.transpose(0, 2, 3, 1, 4).reshape(wt, 4, n_t * ct)
    w_lay = attend_all[:, :, d_own : d_own + dl_own, : 4 * cl].reshape(n_dp, n_t, dl_own, 4, cl)
    w_lay = w_lay.transpose(0, 2, 3, 1, 4).reshape(wl, 4, n_t * cl)
    f_lay = attend_all[:, :, d_own : d_own + dl_own, 4 * cl : lay_cols]
    f_lay = f_lay.reshape(n_dp, n_t, dl_own, 2, hl).transpose(0, 2, 3, 1, 4)
    f_lay = f_lay.reshape(wl, 2, n_t * hl)
    f_text = feed_all.reshape(n_dp, n_t, 2, d_own, ht).transpose(0, 3, 2, 1, 4)
    f_text = f_text.reshape(wt, 2, n_t * ht)
    attend = [w_text, w_lay]
    feeds = [f_text, f_lay]

    text_page = page_of(text_in)
    lay_page = page_of(layout_in.reshape(pages, quarter, wl))
    ints = page_of(
        jnp.concatenate([segment_ids[:, :, None], box_bins.reshape(pages, quarter, 2)], axis=2)
    )
    segments, bins = ints[:, 0], ints[:, 1:]
    cots = [page_of(text_cot), page_of(layout_cot.reshape(pages, quarter, wl))]

    parts = split_vectors(vectors, widths, [n_t * ht, n_t * hl])
    half_width = wl // 2
    table_rows = to_low(tables.reshape(-1, wl))
    levels = jnp.arange(table_rows.shape[0], dtype=jnp.int32)[None, :]
    hots = [(bins[:, k : k + 1] == levels).astype(BF16) for k in range(2)]
    embedded = jnp.concatenate(
        [
            jnp.dot(hots[0], table_rows[:, :half_width], preferred_element_type=F32),
            jnp.dot(hots[1], table_rows[:, half_width:], preferred_element_type=F32),
        ],
        axis=1,
    )
    own_rows = [text_page.astype(F32), lay_page.astype(F32) + embedded]
    rows_low = [text_page, to_low(own_rows[1])]
    qkv = []
    for s in range(2):
        raw = jnp.einsum("rd,dcn->rcn", rows_low[s], attend[s][:, :3], preferred_element_type=F32)
        qkv.append(
            [
                to_low(member).reshape(rows, -1, head_dims[s])
                for member in (raw[:, 0] + parts[s][0][0], raw[:, 1], raw[:, 2] + parts[s][0][1])
            ]
        )
    ctx_text, ctx_lay, log_total = page_forward(*qkv[0], *qkv[1], segments)
    contexts = [ctx_text.reshape(rows, -1), ctx_lay.reshape(rows, -1)]
    attend_grads, feed_grads, input_grads, vector_grads, outs = [], [], [], [], []
    first, d_first, d_ctx, out_proj = [], [], [], []
    for s in range(2):
        vec, bias_in = parts[s]
        attended = jnp.einsum(
            "rn,dn->rd", contexts[s], attend[s][:, 3], preferred_element_type=F32
        )
        h1, n1, inv1 = norm_forward(own_rows[s] + attended + vec[2], vec[3], vec[4])
        h1_low = to_low(h1)
        gate = jnp.dot(h1_low, feeds[s][:, 0], preferred_element_type=F32) + bias_in
        active = to_low(gelu_exact(gate))
        f_out = jnp.einsum("rf,df->rd", active, feeds[s][:, 1], preferred_element_type=F32)
        o, n2, inv2 = norm_forward(h1 + f_out + vec[5], vec[6], vec[7])
        outs.append(to_low(o))
        d_r2, g_gain2, g_shift2 = norm_backward(cots[s].astype(F32), n2, inv2, vec[6])
        df = to_low(d_r2)
        down = jnp.einsum("rd,rf->df", df, active, preferred_element_type=F32)
        d_active = jnp.dot(df, feeds[s][:, 1], preferred_element_type=F32)
        d_gate = gelu_backward(gate, d_active)
        d_gate_low = to_low(d_gate)
        up = jnp.einsum("rd,rf->df", h1_low, d_gate_low, preferred_element_type=F32)
        feed_grads.append(jnp.stack([to_low(up), to_low(down)], axis=1))
        d_h1 = d_r2 + jnp.einsum(
            "rf,df->rd", d_gate_low, feeds[s][:, 0], preferred_element_type=F32
        )
        d_r1, g_gain1, g_shift1 = norm_backward(d_h1, n1, inv1, vec[3])
        da = to_low(d_r1)
        out_proj.append(jnp.einsum("rd,rn->dn", da, contexts[s], preferred_element_type=F32))
        d_ctx.append(
            to_low(jnp.dot(da, attend[s][:, 3], preferred_element_type=F32)).reshape(
                rows, -1, head_dims[s]
            )
        )
        d_first.append(d_r1)
        vector_grads.append(
            [
                None,
                None,
                jnp.sum(d_r1, axis=0),
                g_gain1,
                g_shift1,
                jnp.sum(d_r2, axis=0),
                g_gain2,
                g_shift2,
                jnp.sum(d_gate, axis=0),
            ]
        )
    heads = page_backward(*qkv[0], *qkv[1], segments, log_total, d_ctx[0], d_ctx[1])
    for s in range(2):
        pieces = [heads[3 * s + k].reshape(rows, -1) for k in range(3)]
        vector_grads[s][0] = jnp.sum(pieces[0], axis=0)
        vector_grads[s][1] = jnp.sum(pieces[2], axis=0)
        d_proj = jnp.stack([to_low(piece) for piece in pieces], axis=1)
        qkv_grad = jnp.einsum("rd,rcn->dcn", rows_low[s], d_proj, preferred_element_type=F32)
        attend_grads.append(
            to_low(jnp.concatenate([qkv_grad, out_proj[s][:, None]], axis=1))
        )
        input_grads.append(
            d_first[s]
            + jnp.einsum("rcn,dcn->rd", d_proj, attend[s][:, :3], preferred_element_type=F32)
        )
    g_lay = input_grads[1]
    g_high = to_low(g_lay)
    g_rest = to_low(g_lay - g_high.astype(F32))

    def bin_sum(hot, high, rest):
        both = jnp.einsum(
            "rb,rl->bl", hot, jnp.concatenate([high, rest], axis=1), preferred_element_type=F32
        )
        return both[:, : high.shape[1]] + both[:, high.shape[1] :]

    table_grad = jnp.concatenate(
        [
            bin_sum(hots[0], g_high[:, :half_width], g_rest[:, :half_width]),
            bin_sum(hots[1], g_high[:, half_width:], g_rest[:, half_width:]),
        ],
        axis=1,
    )
    table_grad, _ = reduce_small(table_grad, total)
    vector_grad = sum_everywhere(
        jnp.concatenate([member for stream in vector_grads for member in stream]), total
    )

    def by_owner(grad, own, cols):
        return grad.reshape(n_dp, own, grad.shape[1], n_t, cols).transpose(0, 3, 1, 2, 4)

    g_feed = by_owner(feed_grads[0], d_own, ht).transpose(0, 1, 3, 2, 4)
    g_feed = g_feed.reshape(total, 2 * d_own, ht)
    g_at = by_owner(attend_grads[0], d_own, ct).reshape(total, d_own, 4 * ct)
    g_al = by_owner(attend_grads[1], dl_own, cl).reshape(total, dl_own, 4 * cl)
    g_fl = by_owner(feed_grads[1], dl_own, hl).reshape(total, dl_own, 2 * hl)
    g_lay_pack = jnp.pad(
        jnp.concatenate([g_al, g_fl], axis=2),
        ((0, 0), (0, LAY_ROWS - dl_own), (0, 4 * ct - lay_cols)),
    )
    g_attend = jnp.concatenate([g_at, g_lay_pack], axis=1)
    feed_sum = reduce_shards(reorder(g_feed, me_arr), total)
    attend_sum = reduce_shards(reorder(g_attend, me_arr), total)
    shared_sq = sum_everywhere(
        (jnp.sum(feed_sum * feed_sum) + jnp.sum(attend_sum * attend_sum)).reshape(1), total
    )[0]
    clip_norm = jnp.sqrt(
        shared_sq + jnp.sum(vector_grad * vector_grad) + jnp.sum(table_grad * table_grad)
    )
    factor = jnp.minimum(1.0, CLIP_NORM / (clip_norm + 1e-06))
    lay_sum = attend_sum[d_own : d_own + dl_own]
    states = [
        (
            attend_text,
            attend_text_mean,
            attend_text_square,
            attend_sum[:d_own].reshape(d_own, 4, ct),
            WEIGHT_DECAY,
        ),
        (
            feed_text,
            feed_text_mean,
            feed_text_square,
            feed_sum.reshape(2, d_own, ht).transpose(1, 0, 2),
            WEIGHT_DECAY,
        ),
        (
            attend_layout,
            attend_layout_mean,
            attend_layout_square,
            lay_sum[:, : 4 * cl].reshape(dl_own, 4, cl),
            WEIGHT_DECAY,
        ),
        (
            feed_layout,
            feed_layout_mean,
            feed_layout_square,
            lay_sum[:, 4 * cl : lay_cols].reshape(dl_own, 2, hl),
            WEIGHT_DECAY,
        ),
        (vectors, vectors_mean, vectors_square, vector_grad, 0.0),
        (tables, tables_mean, tables_square, table_grad.reshape(-1), 0.0),
    ]
    updated = []
    for k in range(6):
        updated.extend(
            adamw_step(
                states[k][0],
                states[k][1],
                states[k][2],
                states[k][3] * factor,
                states[k][4],
                LEARN_RATES[k],
            )
        )
    return (
        pages_of(outs[0]),
        pages_of(outs[1]).reshape(pages, quarter * wl),
        pages_of(to_low(input_grads[0])).astype(F32),
        pages_of(to_low(input_grads[1])).astype(F32).reshape(pages, quarter * wl),
        *updated,
        clip_norm,
    )


def solution(mesh):
    rows3, rows2, cols3 = P("dp", "tensor", None), P("dp", "tensor"), P("dp", None, "tensor")
    in_specs = (rows3, rows2, rows2, rows2, rows3, rows2) + (cols3,) * 12 + (P(),) * 6
    out_specs = (rows3, rows2, rows3, rows2) + (cols3,) * 12 + (P(),) * 7
    return jax.shard_map(
        on_device, mesh=mesh, in_specs=in_specs, out_specs=out_specs, check_vma=False
    )
```

```python
import functools
import math

import jax
import jax.numpy as jnp
from jax import lax
from jax.experimental import pallas as pl
from jax.experimental.pallas import tpu as pltpu
from jax.sharding import PartitionSpec as P

HD = 64
LHD = 16
STEP = 10

NORM_EPS = 1e-05
NEG_FILL = -1000000000.0
CLIP_NORM = 1.0
LEARN_RATES = (0.3, 0.05, 0.3, 0.05, 0.3, 0.3)
BETA_ONE = 0.9
BETA_TWO = 0.999
ADAM_EPS = 1e-08
WEIGHT_DECAY = 0.01
AXES = ("dp", "tensor")
LAY_ROWS = 32
F32 = jnp.float32
BF16 = jnp.bfloat16


def to_low(values):
    return values.astype(BF16)


def xor_send(values, total, distance):
    return lax.ppermute(values, AXES, [(i, i ^ distance) for i in range(total)])


def split_vectors(packed, widths, hidden):
    result = []
    offset = 0
    for stream in range(2):
        width_now = widths[stream]
        pieces = [packed[offset + k * width_now : offset + (k + 1) * width_now] for k in range(8)]
        offset = offset + 8 * width_now
        result.append((pieces, packed[offset : offset + hidden[stream]]))
        offset = offset + hidden[stream]
    return result


def adamw_step(weight, moment, square, gradient, decay_rate, rate_now):
    new_moment = BETA_ONE * moment + (1.0 - BETA_ONE) * gradient
    new_square = BETA_TWO * square + (1.0 - BETA_TWO) * gradient * gradient
    moment_hat = new_moment / (1.0 - BETA_ONE**STEP)
    square_hat = new_square / (1.0 - BETA_TWO**STEP)
    new_weight = weight - rate_now * (
        moment_hat / (jnp.sqrt(square_hat) + ADAM_EPS) + decay_rate * weight
    )
    return (new_weight, new_moment, new_square)


def lane_mean(values):
    return jnp.sum(values, axis=-1, keepdims=True) * (1.0 / values.shape[-1])


def norm_parts(residual):
    centered = residual - lane_mean(residual)
    inv_std = lax.rsqrt(lane_mean(centered * centered) + NORM_EPS)
    return centered * inv_std, inv_std


def norm_back(gradient, normed, inv_std, gain_vec):
    scaled = gradient * gain_vec
    d_resid = inv_std * (
        scaled - lane_mean(scaled) - normed * lane_mean(scaled * normed)
    )
    return d_resid


def col_sum(values):
    return jnp.sum(values, axis=0, keepdims=True)


def dot(a, b, da=1, db=0):
    return lax.dot_general(a, b, (((da,), (db,)), ((), ())), preferred_element_type=F32)


def round_up(count, step):
    return -(-count // step) * step


class Plan:
    def __init__(self, n_dp, n_t, quarter, wt, wl, ct, cl, ht, hl):
        self.n_dp, self.n_t, self.total = n_dp, n_t, n_dp * n_t
        self.far = self.total // 8
        self.quarter, self.rows = quarter, quarter * n_t
        self.wt, self.wl, self.ct, self.cl, self.ht, self.hl = wt, wl, ct, cl, ht, hl
        self.d_own, self.dl_own = wt // n_dp, wl // n_dp
        self.ra, self.rl = round_up(self.d_own, 16), round_up(self.dl_own, 16)
        self.cols = 4 * ct
        self.half_a = (self.ra + self.rl) // 2
        self.heads = ct // HD
        self.hw = HD + LHD
        self.lay_cols = 4 * cl + 2 * hl

    def spread(self, own, padded):
        out = jnp.arange(own * self.n_dp, dtype=jnp.int32)
        place = (out // own) * padded + out % own
        return (place[:, None] == jnp.arange(padded * self.n_dp, dtype=jnp.int32)[None]).astype(BF16)


VMEM_LIMIT = 60 * 2**20
COST = 10 * 10**9
ANY = pl.BlockSpec(memory_space=pl.ANY)
VM = pl.BlockSpec(memory_space=pltpu.VMEM)
SM = pl.BlockSpec(memory_space=pltpu.SMEM)


def kernel_call(body, outs, in_specs, out_specs, scratch, args):
    return pl.pallas_call(
        body,
        out_shape=outs,
        in_specs=in_specs,
        out_specs=out_specs,
        scratch_shapes=scratch,
        compiler_params=pltpu.CompilerParams(vmem_limit_bytes=VMEM_LIMIT),
        cost_estimate=pl.CostEstimate(flops=COST, bytes_accessed=2**20, transcendentals=0),
    )(*args)


def shape(dims, kind):
    return jax.ShapeDtypeStruct(tuple(dims), kind)


def wait_for(ref, sem):
    pltpu.make_async_copy(ref, ref, sem).wait()


def attend_forward(p, me2, core, rows_in, bias_t, bias_l, vec_t, vec_l, spread_t, spread_l, pieces):
    rows, hw, nh = p.rows, p.hw, p.heads
    padded_t, padded_l = p.n_dp * p.ra, p.n_dp * p.rl
    exact_t = p.ra == p.d_own
    first = core == 0
    nb = p.n_t // 2
    n_in = len(rows_in)

    def body(*refs):
        (me_ref, bt, bl, vt, vl, spt, spl), refs = refs[:7], refs[7:]
        in_refs, refs = refs[:n_in], refs[n_in:]
        piece_refs, refs = refs[:4], refs[4:]
        n_out = 12 if first else 11
        outs, scratch = refs[:n_out], refs[n_out:]
        wt_out, wl_out, qkv, ctx, lse_ref = outs[:5]
        wpad, lpad, acc_t, acc_l, ctx_rows, ctx_lay, sem_t, sem_l, sem_out = scratch
        my_dp, my_t = me_ref[0], me_ref[1]
        for k in range(nb):
            for y in range(2):
                low, high = piece_refs[y].at[k], piece_refs[2 + k].at[y]
                for z in range(p.far):
                    at = (z * 2 + y) ^ my_dp
                    row = pl.multiple_of(at * p.ra, 16)
                    lrow = pl.multiple_of(at * p.rl, 16)
                    pltpu.make_async_copy(
                        low.at[z], wpad.at[k, pl.ds(row, p.half_a)], sem_t.at[k]
                    ).start()
                    rest = p.ra - p.half_a
                    if rest:
                        pltpu.make_async_copy(
                            high.at[z, pl.ds(0, rest)],
                            wpad.at[k, pl.ds(pl.multiple_of(row + p.half_a, 16), rest)],
                            sem_t.at[k],
                        ).start()
                    pltpu.make_async_copy(
                        high.at[z, pl.ds(rest, p.rl)], lpad.at[k, pl.ds(lrow, p.rl)], sem_l
                    ).start()
        if first:
            x0, x1, x2, x3, tab = in_refs
            xt_ref, lay_low, lay_ref, ints_ref, intst_ref, acc_t_out, acc_l_out = outs[5:]
            for k, ref in enumerate((x0, x1, x2, x3)):
                xt_ref[pl.ds(k * p.quarter, p.quarter), :] = ref[:, : p.wt]
            x = xt_ref[...]
            side = jnp.concatenate([ref[:, p.wt :] for ref in (x0, x1, x2, x3)], axis=0).astype(F32)
            digits = side[:, p.wl : p.wl + 8]
            ints_ref[...] = digits
            intst_ref[...] = digits.T
            half = p.wl // 2
            levels = lax.broadcasted_iota(jnp.int32, (1, tab.shape[0]), 1).astype(F32)
            hot_x = (digits[:, 1:2] * 128.0 + digits[:, 2:3] == levels).astype(F32).astype(BF16)
            hot_y = (digits[:, 3:4] * 128.0 + digits[:, 4:5] == levels).astype(F32).astype(BF16)
            emb = jnp.concatenate([dot(hot_x, tab[:, :half]), dot(hot_y, tab[:, half:])], axis=1)
            lay = side[:, : p.wl] + emb
            low_rows = lay.astype(BF16)
            lay_low[...] = low_rows
            lay_ref[...] = lay
            acc_t[...] = jnp.zeros_like(acc_t)
            acc_l[...] = jnp.zeros_like(acc_l)
        else:
            xt_ref, lay_low, lay_ref, ints_ref, intst_ref, acc_t_in, acc_l_in = in_refs
            n1t, i1t, ht, n1l, i1l, hl = outs[5:]
            x, low_rows = xt_ref[...], lay_low[...]
            acc_t[...] = acc_t_in[...]
            acc_l[...] = acc_l_in[...]
        seg_col = ints_ref[:, 0:1]
        seg_row = intst_ref[0:1, :]
        wait_for(lpad, sem_l)
        for k in range(nb):
            wl_out[k] = dot(spl[...], lpad[k]).astype(BF16)

        def block(k, carry):
            wait_for(wpad.at[k], sem_t.at[k])
            if not exact_t:
                wpad[k, pl.ds(0, p.wt)] = dot(spt[...], wpad[k]).astype(BF16)
            out_copy = pltpu.make_async_copy(wpad.at[k, pl.ds(0, p.wt)], wt_out.at[k], sem_out)
            out_copy.start()
            own_t = (2 * k + core) ^ my_t
            w = wpad[k, pl.ds(0, p.wt)]
            wl = wl_out[k]
            raw = (dot(x, w[:, : 3 * p.ct]) + bt[own_t]).T
            raw_l = (dot(low_rows, wl[:, : 3 * p.cl]) + bl[own_t]).T
            for c in range(3):
                for h in range(nh):
                    top = raw[c * p.ct + h * HD : c * p.ct + (h + 1) * HD]
                    bot = raw_l[c * p.cl + h * LHD : c * p.cl + (h + 1) * LHD]
                    top, bot = top.astype(BF16), bot.astype(BF16)
                    if c == 0:
                        top = top * jnp.asarray(1.0 / math.sqrt(HD), BF16)
                        bot = bot * jnp.asarray(1.0 / math.sqrt(LHD), BF16)
                    qkv[k, c * nh + h, pl.ds(0, HD)] = top
                    qkv[k, c * nh + h, pl.ds(HD, LHD)] = bot
            for h in range(nh):
                scores = dot(qkv[k, nh + h], qkv[k, h], 0, 0)
                scores = jnp.where(seg_col == seg_row, scores, NEG_FILL)
                top_score = jnp.max(scores, axis=0, keepdims=True)
                expo = jnp.exp(scores - top_score)
                row_total = jnp.sum(expo, axis=0, keepdims=True)
                probs = (expo * (1.0 / row_total)).astype(BF16)
                mixed = dot(qkv[k, 2 * nh + h], probs).astype(BF16)
                ctx[k, h] = mixed
                ctx_rows[pl.ds(h * HD, HD)] = mixed[:HD]
                ctx_lay[pl.ds(h * LHD, LHD)] = mixed[HD:]
                lse_ref[k, pl.ds(h, 1), :] = top_score + jnp.log(row_total)
            acc_t[...] += dot(w[:, 3 * p.ct :], ctx_rows[...])
            acc_l[...] += dot(wl[:, 3 * p.cl : 4 * p.cl], ctx_lay[...])
            out_copy.wait()
            return carry

        lax.fori_loop(0, nb, block, 0)
        if first:
            acc_t_out[...] = acc_t[...]
            acc_l_out[...] = acc_l[...]
        else:
            for residual, acc, vec, n_ref, i_ref, h_ref in (
                (x.astype(F32), acc_t, vt, n1t, i1t, ht),
                (lay_ref[...], acc_l, vl, n1l, i1l, hl),
            ):
                normed, inv = norm_parts(residual + acc[...].T + vec[2:3])
                n_ref[...] = normed
                i_ref[...] = inv
                h_ref[...] = (normed * vec[3:4] + vec[4:5]).astype(BF16)

    outs = [
        shape((nb, p.wt, p.cols), BF16),
        shape((nb, p.wl, p.cols), BF16),
        shape((nb, 3 * nh, hw, rows), BF16),
        shape((nb, nh, hw, rows), BF16),
        shape((nb, 8, rows), F32),
    ]
    if first:
        outs += [
            shape((rows, p.wt), BF16),
            shape((rows, p.wl), BF16),
            shape((rows, p.wl), F32),
            shape((rows, 8), F32),
            shape((8, rows), F32),
            shape((p.wt, rows), F32),
            shape((p.wl, rows), F32),
        ]
    else:
        outs += [
            shape((rows, p.wt), F32),
            shape((rows, 1), F32),
            shape((rows, p.wt), BF16),
            shape((rows, p.wl), F32),
            shape((rows, 1), F32),
            shape((rows, p.wl), BF16),
        ]
    scratch = [
        pltpu.VMEM((nb, padded_t, p.cols), BF16),
        pltpu.VMEM((nb, padded_l, p.cols), BF16),
        pltpu.VMEM((p.wt, rows), F32),
        pltpu.VMEM((p.wl, rows), F32),
        pltpu.VMEM((p.ct, rows), BF16),
        pltpu.VMEM((p.cl, rows), BF16),
        pltpu.SemaphoreType.DMA((nb,)),
        pltpu.SemaphoreType.DMA,
        pltpu.SemaphoreType.DMA,
    ]
    args = (me2, bias_t, bias_l, vec_t, vec_l, spread_t, spread_l, *rows_in, *pieces)
    return kernel_call(
        body,
        outs,
        [SM] + [VM] * (6 + n_in) + [ANY] * 4,
        [ANY] + [VM] * (len(outs) - 1),
        scratch,
        args,
    )


def feed_forward(p, me2, core, pieces, w_lay, h_t, h_l, bin_t, bin_l, spread_t, rest_in):
    rows = p.rows
    padded_t = p.n_dp * p.ra
    exact_t = p.ra == p.d_own
    root = 1.0 / math.sqrt(2.0)
    first = core == 0
    nb = p.n_t // 2
    n_rest = len(rest_in)

    def body(*refs):
        (me_ref, wl, ht, hl, bt, bl, spt), refs = refs[:7], refs[7:]
        rest_refs, refs = refs[:n_rest], refs[n_rest:]
        piece_refs, refs = refs[:4], refs[4:]
        n_out = 7 if first else 13
        outs, scratch = refs[:n_out], refs[n_out:]
        f_out, g_t, gp_t, g_l, gp_l = outs[:5]
        fpad, acc_t, acc_l, sem_t, sem_out = scratch
        my_dp, my_t = me_ref[0], me_ref[1]
        for k in range(nb):
            for m in range(2):
                for y in range(2):
                    src = piece_refs[y].at[k] if m == 0 else piece_refs[2 + k].at[y]
                    for z in range(p.far):
                        row = pl.multiple_of(((z * 2 + y) ^ my_dp) * p.ra, 16)
                        pltpu.make_async_copy(
                            src.at[z], fpad.at[k, m, pl.ds(row, p.ra)], sem_t.at[k]
                        ).start()
        if first:
            acc_t[...] = jnp.zeros_like(acc_t)
            acc_l[...] = jnp.zeros_like(acc_l)
        else:
            acc_t_in, acc_l_in, n1t_, n1l_, c0, c1, c2, c3, vt, vl = rest_refs
            acc_t[...] = acc_t_in[...]
            acc_l[...] = acc_l_in[...]

        def gelu(u, g_ref, gp_ref, k):
            cdf = 0.5 + 0.5 * lax.erf(u * root)
            low = (u * cdf).astype(BF16)
            g_ref[k] = low
            dens = jnp.exp(u * u * -0.5) * (1.0 / math.sqrt(2.0 * math.pi))
            gp_ref[k] = (cdf + u * dens).astype(gp_ref.dtype)
            return low

        def block(k, carry):
            wait_for(fpad.at[k], sem_t.at[k])
            if not exact_t:
                for m in range(2):
                    fpad[k, m, pl.ds(0, p.wt)] = dot(spt[...], fpad[k, m]).astype(BF16)
            out_copy = pltpu.make_async_copy(
                fpad.at[k, :, pl.ds(0, p.wt)], f_out.at[k], sem_out
            )
            out_copy.start()
            own_t = (2 * k + core) ^ my_t
            g = gelu(dot(ht[...], fpad[k, 0, pl.ds(0, p.wt)]) + bt[own_t], g_t, gp_t, k)
            acc_t[...] += dot(g, fpad[k, 1, pl.ds(0, p.wt)], 1, 1)
            w = wl[k]
            up = w[:, 4 * p.cl : 4 * p.cl + p.hl]
            down = w[:, 4 * p.cl + p.hl : p.lay_cols]
            g = gelu(dot(hl[...], up) + bl[own_t], g_l, gp_l, k)
            acc_l[...] += dot(g, down, 1, 1)
            out_copy.wait()
            return carry

        lax.fori_loop(0, nb, block, 0)
        if first:
            outs[5][...] = acc_t[...]
            outs[6][...] = acc_l[...]
        else:
            out_tl, dr_t, dr_l, df_t, df_l, gv_t, gv_l, _ = outs[5:]
            cot = jnp.concatenate([ref[...] for ref in (c0, c1, c2, c3)], axis=0).astype(F32)
            for n1, acc, vec, begin, dr_ref, df_ref, gv in (
                (n1t_, acc_t, vt, 0, dr_t, df_t, gv_t),
                (n1l_, acc_l, vl, p.wt, dr_l, df_l, gv_l),
            ):
                width = n1.shape[1]
                ct = cot[:, begin : begin + width]
                h1 = n1[...] * vec[3:4] + vec[4:5]
                n2, inv2 = norm_parts(h1 + acc[...] + vec[5:6])
                out_tl[:, pl.ds(begin, width)] = (n2 * vec[6:7] + vec[7:8]).astype(BF16)
                dr = norm_back(ct, n2, inv2, vec[6:7])
                dr_ref[...] = dr
                df_ref[...] = dr.astype(BF16)
                gv[...] = jnp.zeros_like(gv)
                gv[5:6] = col_sum(dr)
                gv[6:7] = col_sum(ct * n2)
                gv[7:8] = col_sum(ct)
            outs[12][...] = jnp.zeros_like(outs[12])

    outs = [
        shape((nb, 2, p.wt, p.ht), BF16),
        shape((nb, rows, p.ht), BF16),
        shape((nb, rows, p.ht), BF16),
        shape((nb, rows, p.hl), BF16),
        shape((nb, rows, p.hl), BF16),
    ]
    if first:
        outs += [shape((rows, p.wt), F32), shape((rows, p.wl), F32)]
    else:
        outs += [
            shape((rows, p.wt + p.wl), BF16),
            shape((rows, p.wt), F32),
            shape((rows, p.wl), F32),
            shape((rows, p.wt), BF16),
            shape((rows, p.wl), BF16),
            shape((8, p.wt), F32),
            shape((8, p.wl), F32),
            shape((8, 128), F32),
        ]
    scratch = [
        pltpu.VMEM((nb, 2, padded_t, p.ht), BF16),
        pltpu.VMEM((rows, p.wt), F32),
        pltpu.VMEM((rows, p.wl), F32),
        pltpu.SemaphoreType.DMA((nb,)),
        pltpu.SemaphoreType.DMA,
    ]
    args = (me2, w_lay, h_t, h_l, bin_t, bin_l, spread_t, *rest_in, *pieces)
    return kernel_call(
        body,
        outs,
        [SM] + [VM] * (6 + n_rest) + [ANY] * 4,
        [ANY] + [VM] * (len(outs) - 1),
        scratch,
        args,
    )


def store_slots(p, staged, slot_of, my_dp, sem, slices):
    for z in range(p.far):
        for y in range(2):
            at = (z * 2 + y) ^ my_dp
            for dst, per, begin, count, off in slices:
                pltpu.make_async_copy(
                    staged.at[pl.ds(pl.multiple_of(at * per + begin, 16), count)],
                    slot_of(dst, y, z).at[pl.ds(off, count)],
                    sem,
                ).start()


def feed_backward(p, me2, f_all, w_lay, h_t, h_l, df_t, df_l, g_t, gp_t, g_l, gp_l, spread_t, prev, last):
    n_t, rows = p.n_t, p.rows
    padded_t = p.n_dp * p.ra
    exact_t = p.ra == p.d_own
    blocks = [t for t in range(n_t) if t % 2 == (0 if last else 1)]

    def body(*refs):
        (me_ref, f_any, wl, ht, hl, dft, dfl, gt, gpt, gl, gpl, spt), refs = refs[:12], refs[12:]
        if last:
            (pt, pl_, drt, drl, n1t, i1t, n1l, i1l, vt, vl), refs = refs[:10], refs[10:]
            n_out = 11
        else:
            n_out = 7
        outs, scratch = refs[:n_out], refs[n_out:]
        low, high, gfl, dbt, dbl = outs[:5]
        f_in, staged, acc_t, acc_l, sem_in, sem_out = scratch
        my_dp, my_t = me_ref[0], me_ref[1]
        for k, t in enumerate(blocks):
            pltpu.make_async_copy(f_any.at[k], f_in.at[k], sem_in.at[k]).start()
        dfT, hT = dft[...].T, ht[...].T
        dfTl, hTl = dfl[...].T, hl[...].T
        if last:
            acc_t[...] = pt[...]
            acc_l[...] = pl_[...]
        else:
            acc_t[...] = jnp.zeros_like(acc_t)
            acc_l[...] = jnp.zeros_like(acc_l)
        for k, t in enumerate(blocks):
            wait_for(f_in.at[k], sem_in.at[k])
            du = dot(dft[...], f_in[k, 1]) * gpt[k].astype(F32)
            dbt[k] = col_sum(du)
            du_low = du.astype(BF16)
            grads = (dot(hT, du_low).astype(BF16), dot(dfT, gt[k]).astype(BF16))
            for m in range(2):
                value = grads[m]
                if not exact_t:
                    value = dot(spt[...], value, 0, 0).astype(BF16)
                staged[k, m] = value
                x = t // 2
                if m == 0:
                    store_slots(p, staged.at[k, m], lambda d, y, z: low.at[x, y, z], my_dp, sem_out, [(0, p.ra, 0, p.ra, 0)])
                else:
                    store_slots(p, staged.at[k, m], lambda d, y, z: high.at[y, x, z], my_dp, sem_out, [(0, p.ra, 0, p.ra, 0)])
            acc_t[...] += dot(du_low, f_in[k, 0], 1, 1)
            w = wl[k]
            up = w[:, 4 * p.cl : 4 * p.cl + p.hl]
            down = w[:, 4 * p.cl + p.hl : p.lay_cols]
            du = dot(dfl[...], down) * gpl[k].astype(F32)
            dbl[k] = col_sum(du)
            du_low = du.astype(BF16)
            gfl[k, :, pl.ds(0, p.hl)] = dot(hTl, du_low).astype(BF16)
            gfl[k, :, pl.ds(p.hl, p.hl)] = dot(dfTl, gl[k]).astype(BF16)
            acc_l[...] += dot(du_low, up, 1, 1)
        if last:
            dr1t, dr1l, dat, dal, gvt, gvl = outs[5:]
            for dr, acc, n1, i1, vec, o, low_o, gv in (
                (drt, acc_t, n1t, i1t, vt, dr1t, dat, gvt),
                (drl, acc_l, n1l, i1l, vl, dr1l, dal, gvl),
            ):
                dh = dr[...] + acc[...]
                n = n1[...]
                dr1 = norm_back(dh, n, i1[...], vec[3:4])
                o[...] = dr1
                low_o[...] = dr1.astype(BF16)
                gv[...] = jnp.zeros_like(gv)
                gv[2:3] = col_sum(dr1)
                gv[3:4] = col_sum(dh * n)
                gv[4:5] = col_sum(dh)
        else:
            outs[5][...] = acc_t[...]
            outs[6][...] = acc_l[...]
        wait_for(staged, sem_out)

    nb = len(blocks)
    outs = [
        shape((2, 2, p.far, p.ra, p.ht), BF16),
        shape((2, 2, p.far, p.ra, p.ht), BF16),
        shape((nb, p.wl, 2 * p.hl), BF16),
        shape((nb, 1, p.ht), F32),
        shape((nb, 1, p.hl), F32),
    ]
    args = [me2, f_all, w_lay, h_t, h_l, df_t, df_l, g_t, gp_t, g_l, gp_l, spread_t]
    if last:
        args += list(prev)
        outs += [
            shape((rows, p.wt), F32),
            shape((rows, p.wl), F32),
            shape((rows, p.wt), BF16),
            shape((rows, p.wl), BF16),
            shape((8, p.wt), F32),
            shape((8, p.wl), F32),
        ]
    else:
        outs += [shape((rows, p.wt), F32), shape((rows, p.wl), F32)]
    scratch = [
        pltpu.VMEM((nb, 2, p.wt, p.ht), BF16),
        pltpu.VMEM((nb, 2, padded_t, p.ht), BF16),
        pltpu.VMEM((rows, p.wt), F32),
        pltpu.VMEM((rows, p.wl), F32),
        pltpu.SemaphoreType.DMA((nb,)),
        pltpu.SemaphoreType.DMA,
    ]
    specs = [SM, ANY] + [VM] * (len(args) - 2)
    return kernel_call(
        body, outs, specs, [ANY, ANY] + [VM] * (len(outs) - 2), scratch, args
    )


def attend_backward(p, me2, w_all, w_lay, qkv, ctx, lse, x_low, lay_low, ints, ints_t, da_t, da_l, gfl, spread_t, spread_l, prev, last):
    n_t, rows, hw, nh = p.n_t, p.rows, p.hw, p.heads
    padded_t, padded_l = p.n_dp * p.ra, p.n_dp * p.rl
    exact_t = p.ra == p.d_own
    blocks = [t for t in range(n_t) if t % 2 == (0 if last else 1)]
    nb = len(blocks)

    def body(*refs):
        (me_ref, w_any, wl_ref, qkv_r, ctx_r, lse_r, xl, ll, ir, itr, dat, dal, gfl_r, spt, spl), refs = refs[:15], refs[15:]
        if last:
            (pt, pl_, dr1t, dr1l), refs = refs[:4], refs[4:]
        outs, scratch = refs[:8], refs[8:]
        low, high, gbq, gbv, gbql, gbvl, out_a, out_b = outs
        w_in, staged, staged_l, acc_t, acc_l, dctx, ctx_s, ctx_l, dp_t, dp_l, sem_in, sem_out = scratch
        my_dp = me_ref[0]
        for k, t in enumerate(blocks):
            pltpu.make_async_copy(w_any.at[k], w_in.at[k], sem_in.at[k]).start()
        xT, lT = xl[...].T, ll[...].T
        daT, dalT = dat[...].T, dal[...].T
        seg_col, seg_row = ir[:, 0:1], itr[0:1, :]
        if last:
            acc_t[...] = pt[...]
            acc_l[...] = pl_[...]
        else:
            acc_t[...] = jnp.zeros_like(acc_t)
            acc_l[...] = jnp.zeros_like(acc_l)
        gbq[...] = jnp.zeros_like(gbq)
        gbv[...] = jnp.zeros_like(gbv)
        gbql[...] = jnp.zeros_like(gbql)
        gbvl[...] = jnp.zeros_like(gbvl)
        for k, t in enumerate(blocks):
            wait_for(w_in.at[k], sem_in.at[k])
            w = w_in[k]
            wl = wl_ref[k]
            d_t = dot(dat[...], w[:, 3 * p.ct :]).T
            d_l = dot(dal[...], wl[:, 3 * p.cl : 4 * p.cl]).T
            for h in range(nh):
                dctx[h, pl.ds(0, HD)] = d_t[h * HD : (h + 1) * HD].astype(BF16)
                dctx[h, pl.ds(HD, LHD)] = d_l[h * LHD : (h + 1) * LHD].astype(BF16)
                ctx_s[pl.ds(h * HD, HD)] = ctx_r[k, h, pl.ds(0, HD)]
                ctx_l[pl.ds(h * LHD, LHD)] = ctx_r[k, h, pl.ds(HD, LHD)]

            for h in range(nh):
                q, key, val = qkv_r[k, h], qkv_r[k, nh + h], qkv_r[k, 2 * nh + h]
                dc = dctx[h]
                scores = dot(key, q, 0, 0)
                probs = jnp.exp(
                    jnp.where(seg_col == seg_row, scores, NEG_FILL) - lse_r[k, pl.ds(h, 1), :]
                )
                low_p = probs.astype(BF16)
                prod = dc.astype(F32) * ctx_r[k, h].astype(F32)
                sum_lay = jnp.sum(prod[HD:], axis=0, keepdims=True)
                sum_all = jnp.sum(prod[:HD], axis=0, keepdims=True) + sum_lay
                dz_all = probs * (dot(val, dc, 0, 0) - sum_all)
                dz_lay = probs * (dot(val[HD:], dc[HD:], 0, 0) - sum_lay)
                ds_t, ds_l = dz_all.astype(BF16), dz_lay.astype(BF16)
                dv = dot(dc, low_p, 1, 1)
                dq_t = dot(key[:HD], ds_t) * (1.0 / math.sqrt(HD))
                dq_l = dot(key[HD:], ds_l) * (1.0 / math.sqrt(LHD))
                dk_t = dot(q[:HD], ds_t, 1, 1)
                dk_l = dot(q[HD:], ds_l, 1, 1)
                for c, (top, bot) in enumerate(((dq_t, dq_l), (dk_t, dk_l), (dv[:HD], dv[HD:]))):
                    dp_t[pl.ds(c * p.ct + h * HD, HD)] = top.astype(BF16)
                    dp_l[pl.ds(c * p.cl + h * LHD, LHD)] = bot.astype(BF16)
                    if c != 1:
                        dst, dst_l = (gbq, gbql) if c == 0 else (gbv, gbvl)
                        dst[k, pl.ds(h * HD, HD)] = jnp.sum(top, axis=1, keepdims=True)
                        dst_l[k, pl.ds(h * LHD, LHD)] = jnp.sum(bot, axis=1, keepdims=True)
            acc_t[...] += dot(w[:, : 3 * p.ct], dp_t[...])
            acc_l[...] += dot(wl[:, : 3 * p.cl], dp_l[...])
            grad = jnp.concatenate(
                [dot(xT, dp_t[...], 1, 1), dot(daT, ctx_s[...], 1, 1)], axis=1
            ).astype(BF16)
            if not exact_t:
                grad = dot(spt[...], grad, 0, 0).astype(BF16)
            staged[k] = grad
            fill = p.cols - p.lay_cols
            grad_l = jnp.concatenate(
                [
                    dot(lT, dp_l[...], 1, 1),
                    dot(dalT, ctx_l[...], 1, 1),
                    gfl_r[k].astype(F32),
                    jnp.zeros((p.wl, fill), F32),
                ],
                axis=1,
            ).astype(BF16)
            staged_l[k] = dot(spl[...], grad_l, 0, 0).astype(BF16)
            x = t // 2
            rest = p.ra - p.half_a
            slot = lambda d, y, z: low.at[x, y, z] if d == 0 else high.at[y, x, z]
            slices = [(0, p.ra, 0, p.half_a, 0)]
            if rest:
                slices.append((1, p.ra, p.half_a, rest, 0))
            store_slots(p, staged.at[k], slot, my_dp, sem_out.at[0], slices)
            store_slots(p, staged_l.at[k], slot, my_dp, sem_out.at[1], [(1, p.rl, 0, p.rl, rest)])
        if last:
            gt = dr1t[...] + acc_t[...].T
            gl = dr1l[...] + acc_l[...].T
            out_a[:, pl.ds(0, p.wt)] = gt.astype(BF16)
            out_a[:, pl.ds(p.wt, p.wl)] = gl.astype(BF16)
            half = p.wl // 2
            bins = out_b.shape[0]
            levels = lax.broadcasted_iota(jnp.int32, (bins, 1), 0).astype(F32)
            for m in range(2):
                row = itr[1 + 2 * m : 2 + 2 * m, :] * 128.0 + itr[2 + 2 * m : 3 + 2 * m, :]
                hot = (levels == row).astype(F32).astype(BF16)
                part = gl[:, m * half : (m + 1) * half]
                top = part.astype(BF16)
                rest_part = (part - top.astype(F32)).astype(BF16)
                both = dot(hot, jnp.concatenate([top, rest_part], axis=1))
                out_b[:, pl.ds(m * half, half)] = both[:, :half] + both[:, half:]
        else:
            out_a[...] = acc_t[...]
            out_b[...] = acc_l[...]
        wait_for(staged, sem_out.at[0])
        wait_for(staged_l, sem_out.at[1])

    half_b = p.ra + p.rl - p.half_a
    outs = [
        shape((2, 2, p.far, p.half_a, p.cols), BF16),
        shape((2, 2, p.far, half_b, p.cols), BF16),
        shape((nb, p.ct, 1), F32),
        shape((nb, p.ct, 1), F32),
        shape((nb, p.cl, 1), F32),
        shape((nb, p.cl, 1), F32),
    ]
    args = [me2, w_all, w_lay, qkv, ctx, lse, x_low, lay_low, ints, ints_t, da_t, da_l, gfl, spread_t, spread_l]
    if last:
        *prev, bins = prev
        args += list(prev)
        outs += [shape((rows, p.wt + p.wl), BF16), shape((bins, p.wl), F32)]
    else:
        outs += [shape((p.wt, rows), F32), shape((p.wl, rows), F32)]
    scratch = [
        pltpu.VMEM((nb, p.wt, p.cols), BF16),
        pltpu.VMEM((nb, padded_t, p.cols), BF16),
        pltpu.VMEM((nb, padded_l, p.cols), BF16),
        pltpu.VMEM((p.wt, rows), F32),
        pltpu.VMEM((p.wl, rows), F32),
        pltpu.VMEM((nh, hw, rows), BF16),
        pltpu.VMEM((p.ct, rows), BF16),
        pltpu.VMEM((p.cl, rows), BF16),
        pltpu.VMEM((3 * p.ct, rows), BF16),
        pltpu.VMEM((3 * p.cl, rows), BF16),
        pltpu.SemaphoreType.DMA((nb,)),
        pltpu.SemaphoreType.DMA((2,)),
    ]
    specs = [SM, ANY] + [VM] * (len(args) - 2)
    return kernel_call(
        body, outs, specs, [ANY, ANY] + [VM] * (len(outs) - 2), scratch, args
    )


def tie(*groups):
    leaves, tree = jax.tree.flatten(groups)
    return jax.tree.unflatten(tree, lax.optimization_barrier(leaves))


def line_of(shard, total):
    return [shard] + [xor_send(shard, total, 8 * r) for r in range(1, total // 8)]


def halves_of(line, half):
    low = jnp.stack([member[:half] for member in line])
    high = jnp.stack([member[half:] for member in line])
    return low, high


def add_low(mine, theirs):
    return to_low(mine.astype(F32) + theirs.astype(F32))


def reduce_second(mine, got):
    send = [add_low(mine[k][1], got[k][1]) for k in range(2)]
    keep = [add_low(mine[k][0], got[k][0]) for k in range(2)]
    return send, keep


def reduce_last(keep, got, total):
    far = total // 8
    line = [
        jnp.concatenate([add_low(keep[k][z], got[k][z]) for k in range(2)], axis=0)
        for z in range(far)
    ]
    out = line[0].astype(F32)
    for z in range(1, far):
        out = out + xor_send(line[z], total, 8 * z).astype(F32)
    return out


def sum_everywhere(values, total):
    pair = values + xor_send(values, total, 1)
    chip = pair + xor_send(pair, total, 2)
    plane = chip + xor_send(chip, total, 4)
    distance = 8
    while distance < total:
        if 2 * distance < total:
            near, far, both = (xor_send(plane, total, distance * k) for k in (1, 2, 3))
            plane = (plane + near) + (far + both)
            distance = distance * 4
        else:
            plane = plane + xor_send(plane, total, distance)
            distance = distance * 2
    return plane


def reduce_small(values, total):
    me = lax.axis_index("dp") * lax.axis_size("tensor") + lax.axis_index("tensor")
    distance = 1
    sizes = []
    while distance < total:
        half = values.shape[0] // 2
        bit = (me // distance) % 2
        mine = lax.dynamic_slice_in_dim(values, bit * half, half)
        other = lax.dynamic_slice_in_dim(values, (1 - bit) * half, half)
        values = mine + xor_send(to_low(other), total, distance).astype(F32)
        sizes.append(distance)
        distance = distance * 2
    square_sum = jnp.sum(values * values)
    for distance in reversed(sizes):
        bit = (me // distance) % 2
        other = xor_send(values, total, distance)
        values = jnp.where(
            bit == 0, jnp.concatenate([values, other]), jnp.concatenate([other, values])
        )
    return values, square_sum


def on_device(
    text_in,
    layout_in,
    segment_ids,
    box_bins,
    text_cot,
    layout_cot,
    attend_text,
    attend_text_mean,
    attend_text_square,
    feed_text,
    feed_text_mean,
    feed_text_square,
    attend_layout,
    attend_layout_mean,
    attend_layout_square,
    feed_layout,
    feed_layout_mean,
    feed_layout_square,
    vectors,
    vectors_mean,
    vectors_square,
    tables,
    tables_mean,
    tables_square,
):
    n_dp, n_t = lax.axis_size("dp"), lax.axis_size("tensor")
    total = n_dp * n_t
    t_pos = lax.axis_index("tensor")
    pages, quarter, wt = text_in.shape
    wl = layout_in.shape[1] // quarter
    d_own, dl_own = attend_text.shape[0], attend_layout.shape[0]
    ct, cl = attend_text.shape[2], attend_layout.shape[2]
    ht, hl = feed_text.shape[2], feed_layout.shape[2]


    p = Plan(n_dp, n_t, quarter, wt, wl, ct, cl, ht, hl)
    me2 = jnp.stack([lax.axis_index("dp"), t_pos]).astype(jnp.int32)
    lay_cols = p.lay_cols

    def pad_rows(values, count):
        return jnp.pad(values, ((0, count - values.shape[0]), (0, 0)))

    lay_pack = jnp.concatenate(
        [
            to_low(attend_layout).reshape(dl_own, 4 * cl),
            to_low(feed_layout).reshape(dl_own, 2 * hl),
        ],
        axis=1,
    )
    lay_pack = jnp.pad(lay_pack, ((0, p.rl - dl_own), (0, p.cols - lay_cols)))
    attend_pack = jnp.concatenate(
        [pad_rows(to_low(attend_text).reshape(d_own, p.cols), p.ra), lay_pack]
    )
    low_feed = to_low(feed_text)
    feed_pack = jnp.concatenate(
        [pad_rows(low_feed[:, 0], p.ra), pad_rows(low_feed[:, 1], p.ra)]
    )
    bins = box_bins.reshape(pages, quarter, 2)
    digits = jnp.stack(
        [segment_ids, bins[..., 0] // 128, bins[..., 0] % 128, bins[..., 1] // 128, bins[..., 1] % 128],
        axis=-1,
    )
    packed_in = jnp.concatenate(
        [
            text_in,
            layout_in.reshape(pages, quarter, wl),
            jnp.pad(to_low(digits), ((0, 0), (0, 0), (0, 59))),
        ],
        axis=2,
    )
    packed_cot = jnp.concatenate([text_cot, layout_cot.reshape(pages, quarter, wl)], axis=2)

    def page_of(values):
        take = lambda r: lax.dynamic_index_in_dim(values, t_pos ^ r, 0, keepdims=False)
        return [take(0)] + [xor_send(take(r), total, r) for r in range(1, n_t)]

    def send_rows(page):
        blocks = page.reshape(n_t, quarter, page.shape[-1])
        return [blocks[0]] + [xor_send(blocks[r], total, r) for r in range(1, n_t)]

    def pages_of(blocks):
        out = jnp.zeros((n_t,) + blocks[0].shape, blocks[0].dtype)
        for r in range(n_t):
            out = lax.dynamic_update_slice(out, blocks[r][None], (t_pos ^ r, 0, 0))
        return out

    parts = split_vectors(vectors, [wt, wl], [n_t * ht, n_t * hl])
    biases, vecs, bins_in = [], [], []
    for s, width in ((0, ct), (1, cl)):
        vec, hidden = parts[s]
        biases.append(
            jnp.concatenate(
                [
                    vec[0].reshape(n_t, 1, width),
                    jnp.zeros((n_t, 1, width), F32),
                    vec[1].reshape(n_t, 1, width),
                ],
                axis=2,
            )
        )
        vecs.append(jnp.stack(vec))
        bins_in.append(hidden.reshape(n_t, 1, -1))
    table_rows = to_low(tables.reshape(-1, wl))
    spread_t = p.spread(d_own, p.ra) if p.ra != d_own else jnp.zeros((16, 128), BF16)
    spread_l = p.spread(dl_own, p.rl)

    send = lambda values, distance: xor_send(values, total, distance)

    line_a = line_of(attend_pack, total)
    xin = page_of(packed_in)
    line_a, feed_pack = tie(line_a, feed_pack)
    line_f = line_of(feed_pack, total)
    low, high = halves_of(line_a, p.half_a)
    low0, high0 = jnp.stack([low, send(low, 2)]), jnp.stack([high, send(high, 4)])
    low4, high2 = send(low0, 4), send(high0, 2)
    low1, high1 = send(low0, 1), send(high0, 1)
    pieces_a0 = [low0, low4, high0, high2]
    (low4, high2), line_f = tie((low4, high2), line_f)
    low5, high3 = send(low4, 1), send(high2, 1)
    flow, fhigh = halves_of(line_f, p.ra)
    flow_x, fhigh_y = send(flow, 2), send(fhigh, 4)
    xin, flow, fhigh = tie(xin, flow, fhigh)
    att_fix = (biases[0], biases[1], vecs[0], vecs[1], spread_t, spread_l)
    (w_all0, w_lay0, qkv0, ctx0, lse0, *row_state) = attend_forward(
        p, me2, 0, (*xin, table_rows), *att_fix, pieces_a0
    )
    row_state, (flow_x, fhigh_y) = tie(row_state, (flow_x, fhigh_y))
    flow0, fhigh0 = jnp.stack([flow, flow_x]), jnp.stack([fhigh, fhigh_y])
    flow4, fhigh2 = send(flow0, 4), send(fhigh0, 2)
    flow1, fhigh1 = send(flow0, 1), send(fhigh0, 1)
    row_state, flow0, fhigh0 = tie(row_state, flow0, fhigh0)
    (w_all1, w_lay1, qkv1, ctx1, lse1, n1t, i1t, h_t, n1l, i1l, h_l) = attend_forward(
        p, me2, 1, row_state, *att_fix, [low1, low5, high1, high3]
    )
    x_low, lay_low, _, ints, ints_t = row_state[:5]
    (flow4, fhigh2), h_t, packed_cot = tie((flow4, fhigh2), h_t, packed_cot)
    flow5, fhigh3 = send(flow4, 1), send(fhigh2, 1)
    cots = page_of(packed_cot)
    (f_all0, g_t0, gp_t0, g_l0, gp_l0, acc_t, acc_l) = feed_forward(
        p, me2, 0, [flow0, flow4, fhigh0, fhigh2], w_lay0, h_t, h_l, bins_in[0], bins_in[1], spread_t, ()
    )
    acc_t, flow5, fhigh3, cots = tie(acc_t, flow5, fhigh3, cots)
    (f_all1, g_t1, gp_t1, g_l1, gp_l1, out_rows, dr_t, dr_l, df_t, df_l, gv2t, gv2l, _) = feed_forward(
        p, me2, 1, [flow1, flow5, fhigh1, fhigh3], w_lay1, h_t, h_l, bins_in[0], bins_in[1], spread_t,
        (acc_t, acc_l, n1t, n1l, *cots, vecs[0], vecs[1]),
    )
    rows_out = send_rows(out_rows)
    (gf_low1, gf_high1, gfl1, dbt1, dbl1, acc_t, acc_l) = feed_backward(
        p, me2, f_all1, w_lay1, h_t, h_l, df_t, df_l, g_t1, gp_t1, g_l1, gp_l1, spread_t, None, False
    )
    acc_t, rows_out = tie(acc_t, rows_out)
    got = [send(gf_low1, 1), send(gf_high1, 1)]
    (gf_low0, gf_high0, gfl0, dbt0, dbl0, dr1t, dr1l, da_t, da_l, gv1t, gv1l) = feed_backward(
        p, me2, f_all0, w_lay0, h_t, h_l, df_t, df_l, g_t0, gp_t0, g_l0, gp_l0, spread_t,
        (acc_t, acc_l, dr_t, dr_l, n1t, i1t, n1l, i1l, vecs[0], vecs[1]), True
    )
    next_f, keep_f = reduce_second((gf_low0, gf_high0), got)
    next_f, keep_f, da_t = tie(next_f, keep_f, da_t)
    got_f = [send(next_f[0], 2), send(next_f[1], 4)]
    (ga_low1, ga_high1, bq1, bv1, bql1, bvl1, acc_t, acc_l) = attend_backward(
        p, me2, w_all1, w_lay1, qkv1, ctx1, lse1, x_low, lay_low, ints, ints_t, da_t, da_l,
        gfl1, spread_t, spread_l, None, False
    )
    got_f, acc_t = tie(got_f, acc_t)
    got = [send(ga_low1, 1), send(ga_high1, 1)]
    next_f, keep_f = reduce_second(keep_f, got_f)
    next_f, keep_f, acc_t = tie(next_f, keep_f, acc_t)
    got_f = [send(next_f[0], 4), send(next_f[1], 2)]
    (ga_low0, ga_high0, bq0, bv0, bql0, bvl0, grad_rows, table_grad) = attend_backward(
        p, me2, w_all0, w_lay0, qkv0, ctx0, lse0, x_low, lay_low, ints, ints_t, da_t, da_l,
        gfl0, spread_t, spread_l, (acc_t, acc_l, dr1t, dr1l, table_rows.shape[0]), True
    )
    got_f, got, grad_rows, table_grad, bq0 = tie(got_f, got, grad_rows, table_grad, bq0)
    next_a, keep_a = reduce_second((ga_low0, ga_high0), got)
    got_a = [send(next_a[0], 2), send(next_a[1], 4)]
    feed_sum = reduce_last(keep_f, got_f, total)
    next_a, keep_a = reduce_second(keep_a, got_a)
    got_a = [send(next_a[0], 4), send(next_a[1], 2)]
    attend_sum = reduce_last(keep_a, got_a, total)
    rows_grad = send_rows(grad_rows)

    def by_block(odd, even):
        both = jnp.stack([even[0], odd[0], even[1], odd[1]]).reshape(n_t, -1)
        order = jnp.arange(n_t) ^ t_pos
        hot = order[:, None] == jnp.arange(n_t)[None, :]
        return jnp.sum(jnp.where(hot[:, :, None], both[None], 0.0), axis=1).reshape(-1)

    gv_t, gv_l = gv2t + gv1t, gv2l + gv1l
    vector_grad = jnp.concatenate(
        [
            by_block(bq1, bq0),
            by_block(bv1, bv0),
            gv_t[2:].reshape(-1),
            by_block(dbt1, dbt0),
            by_block(bql1, bql0),
            by_block(bvl1, bvl0),
            gv_l[2:].reshape(-1),
            by_block(dbl1, dbl0),
        ]
    )
    small = jnp.concatenate([table_grad.reshape(-1), vector_grad])
    n_table, n_small = table_grad.size, small.shape[0]
    small_rows = round_up(-(-n_small // 128), 4 * total)
    small = jnp.pad(small, (0, small_rows * 128 - n_small)).reshape(small_rows, 128)
    small, small_sq = reduce_small(small, total)
    small = small.reshape(-1)
    table_grad, vector_grad = small[:n_table], small[n_table:n_small]
    shared_sq = sum_everywhere(
        (jnp.sum(feed_sum * feed_sum) + jnp.sum(attend_sum * attend_sum) + small_sq).reshape(1, 1),
        total,
    )[0, 0]
    clip_norm = jnp.sqrt(shared_sq)
    factor = jnp.minimum(1.0, CLIP_NORM / (clip_norm + 1e-06))
    lay_sum = attend_sum[p.ra : p.ra + dl_own]
    states = [
        (
            attend_text,
            attend_text_mean,
            attend_text_square,
            attend_sum[:d_own].reshape(d_own, 4, ct),
            WEIGHT_DECAY,
        ),
        (
            feed_text,
            feed_text_mean,
            feed_text_square,
            jnp.stack([feed_sum[:d_own], feed_sum[p.ra : p.ra + d_own]], axis=1),
            WEIGHT_DECAY,
        ),
        (
            attend_layout,
            attend_layout_mean,
            attend_layout_square,
            lay_sum[:, : 4 * cl].reshape(dl_own, 4, cl),
            WEIGHT_DECAY,
        ),
        (
            feed_layout,
            feed_layout_mean,
            feed_layout_square,
            lay_sum[:, 4 * cl : lay_cols].reshape(dl_own, 2, hl),
            WEIGHT_DECAY,
        ),
        (vectors, vectors_mean, vectors_square, vector_grad, 0.0),
        (tables, tables_mean, tables_square, table_grad, 0.0),
    ]
    updated = []
    for k in range(6):
        updated.extend(
            adamw_step(
                states[k][0],
                states[k][1],
                states[k][2],
                states[k][3] * factor,
                states[k][4],
                LEARN_RATES[k],
            )
        )
    rows_out, rows_grad = pages_of(rows_out), pages_of(rows_grad)
    return (
        rows_out[:, :, :wt],
        rows_out[:, :, wt:].reshape(pages, quarter * wl),
        rows_grad[:, :, :wt].astype(F32),
        rows_grad[:, :, wt:].astype(F32).reshape(pages, quarter * wl),
        *updated,
        clip_norm,
    )


def solution(mesh):
    rows3, rows2, cols3 = P("dp", "tensor", None), P("dp", "tensor"), P("dp", None, "tensor")
    in_specs = (rows3, rows2, rows2, rows2, rows3, rows2) + (cols3,) * 12 + (P(),) * 6
    out_specs = (rows3, rows2, rows3, rows2) + (cols3,) * 12 + (P(),) * 7
    return jax.shard_map(
        on_device, mesh=mesh, in_specs=in_specs, out_specs=out_specs, check_vma=False
    )
```

```python
import functools
import math

import jax
import jax.numpy as jnp
from jax import lax
from jax.experimental import pallas as pl
from jax.experimental.pallas import tpu as pltpu
from jax.sharding import PartitionSpec as P

HD = 64
LHD = 16
STEP = 10

NORM_EPS = 1e-05
NEG_FILL = -1000000000.0
CLIP_NORM = 1.0
LEARN_RATES = (0.3, 0.05, 0.3, 0.05, 0.3, 0.3)
BETA_ONE = 0.9
BETA_TWO = 0.999
ADAM_EPS = 1e-08
WEIGHT_DECAY = 0.01
AXES = ("dp", "tensor")
LAY_ROWS = 32
F32 = jnp.float32
BF16 = jnp.bfloat16


def to_low(values):
    return values.astype(BF16)


def xor_send(values, total, distance):
    return lax.ppermute(values, AXES, [(i, i ^ distance) for i in range(total)])


def split_vectors(packed, widths, hidden):
    result = []
    offset = 0
    for stream in range(2):
        width_now = widths[stream]
        pieces = [packed[offset + k * width_now : offset + (k + 1) * width_now] for k in range(8)]
        offset = offset + 8 * width_now
        result.append((pieces, packed[offset : offset + hidden[stream]]))
        offset = offset + hidden[stream]
    return result


def adamw_step(weight, moment, square, gradient, decay_rate, rate_now):
    new_moment = BETA_ONE * moment + (1.0 - BETA_ONE) * gradient
    new_square = BETA_TWO * square + (1.0 - BETA_TWO) * gradient * gradient
    moment_hat = new_moment / (1.0 - BETA_ONE**STEP)
    square_hat = new_square / (1.0 - BETA_TWO**STEP)
    new_weight = weight - rate_now * (
        moment_hat / (jnp.sqrt(square_hat) + ADAM_EPS) + decay_rate * weight
    )
    return (new_weight, new_moment, new_square)


def lane_mean(values):
    return jnp.sum(values, axis=-1, keepdims=True) * (1.0 / values.shape[-1])


def norm_parts(residual):
    centered = residual - lane_mean(residual)
    inv_std = lax.rsqrt(lane_mean(centered * centered) + NORM_EPS)
    return centered * inv_std, inv_std


def norm_back(gradient, normed, inv_std, gain_vec):
    scaled = gradient * gain_vec
    d_resid = inv_std * (
        scaled - lane_mean(scaled) - normed * lane_mean(scaled * normed)
    )
    return d_resid


def col_sum(values):
    return jnp.sum(values, axis=0, keepdims=True)


def dot(a, b, da=1, db=0):
    return lax.dot_general(a, b, (((da,), (db,)), ((), ())), preferred_element_type=F32)


def round_up(count, step):
    return -(-count // step) * step


class Plan:
    def __init__(self, n_dp, n_t, quarter, wt, wl, ct, cl, ht, hl, bins):
        self.n_dp, self.n_t, self.total = n_dp, n_t, n_dp * n_t
        self.far = self.total // 8
        self.quarter, self.rows = quarter, quarter * n_t
        self.wt, self.wl, self.ct, self.cl, self.ht, self.hl = wt, wl, ct, cl, ht, hl
        self.d_own, self.dl_own = wt // n_dp, wl // n_dp
        self.ra, self.rl = round_up(self.d_own, 16), round_up(self.dl_own, 16)
        self.cols = 4 * ct
        self.half_a = (self.ra + self.rl) // 2
        self.heads = ct // HD
        self.hw = HD + LHD
        self.lay_cols = 4 * cl + 2 * hl
        self.per = bins // self.total

    def spread(self, own, padded):
        out = jnp.arange(own * self.n_dp, dtype=jnp.int32)
        place = (out // own) * padded + out % own
        return (place[:, None] == jnp.arange(padded * self.n_dp, dtype=jnp.int32)[None]).astype(BF16)


VMEM_LIMIT = 60 * 2**20
COST = 10 * 10**9
ANY = pl.BlockSpec(memory_space=pl.ANY)
VM = pl.BlockSpec(memory_space=pltpu.VMEM)
SM = pl.BlockSpec(memory_space=pltpu.SMEM)


def kernel_call(body, outs, in_specs, out_specs, scratch, args):
    return pl.pallas_call(
        body,
        out_shape=outs,
        in_specs=in_specs,
        out_specs=out_specs,
        scratch_shapes=scratch,
        compiler_params=pltpu.CompilerParams(vmem_limit_bytes=VMEM_LIMIT),
        cost_estimate=pl.CostEstimate(flops=COST, bytes_accessed=2**20, transcendentals=0),
    )(*args)


def shape(dims, kind):
    return jax.ShapeDtypeStruct(tuple(dims), kind)


def wait_for(ref, sem):
    pltpu.make_async_copy(ref, ref, sem).wait()


def attend_forward(p, me2, core, rows_in, bias_t, bias_l, vec_t, vec_l, spread_t, spread_l, pieces):
    rows, hw, nh = p.rows, p.hw, p.heads
    padded_t, padded_l = p.n_dp * p.ra, p.n_dp * p.rl
    exact_t = p.ra == p.d_own
    first = core == 0
    nb = p.n_t // 2
    n_in = len(rows_in)

    def body(*refs):
        (me_ref, bt, bl, vt, vl, spt, spl), refs = refs[:7], refs[7:]
        in_refs, refs = refs[:n_in], refs[n_in:]
        piece_refs, refs = refs[:4], refs[4:]
        n_out = 12 if first else 11
        outs, scratch = refs[:n_out], refs[n_out:]
        wt_out, wl_out, qkv, ctx, lse_ref = outs[:5]
        wpad, lpad, acc_t, acc_l, ctx_rows, ctx_lay, sem_t, sem_l, sem_out = scratch
        my_dp, my_t = me_ref[0], me_ref[1]
        for k in range(nb):
            for y in range(2):
                low, high = piece_refs[y].at[k], piece_refs[2 + k].at[y]
                for z in range(p.far):
                    at = (z * 2 + y) ^ my_dp
                    row = pl.multiple_of(at * p.ra, 16)
                    lrow = pl.multiple_of(at * p.rl, 16)
                    pltpu.make_async_copy(
                        low.at[z], wpad.at[k, pl.ds(row, p.half_a)], sem_t.at[k]
                    ).start()
                    rest = p.ra - p.half_a
                    if rest:
                        pltpu.make_async_copy(
                            high.at[z, pl.ds(0, rest)],
                            wpad.at[k, pl.ds(pl.multiple_of(row + p.half_a, 16), rest)],
                            sem_t.at[k],
                        ).start()
                    pltpu.make_async_copy(
                        high.at[z, pl.ds(rest, p.rl)], lpad.at[k, pl.ds(lrow, p.rl)], sem_l
                    ).start()
        if first:
            x0, x1, x2, x3, tab = in_refs
            xt_ref, lay_low, lay_ref, ints_ref, intst_ref, acc_t_out, acc_l_out = outs[5:]
            for k, ref in enumerate((x0, x1, x2, x3)):
                xt_ref[pl.ds(k * p.quarter, p.quarter), :] = ref[:, : p.wt]
            x = xt_ref[...]
            side = jnp.concatenate([ref[:, p.wt :] for ref in (x0, x1, x2, x3)], axis=0).astype(F32)
            digits = side[:, p.wl : p.wl + 8]
            ints_ref[...] = digits
            intst_ref[...] = digits.T
            half = p.wl // 2
            levels = lax.broadcasted_iota(jnp.int32, (1, tab.shape[0]), 1).astype(F32)
            hot_x = (digits[:, 1:2] * 128.0 + digits[:, 2:3] == levels).astype(F32).astype(BF16)
            hot_y = (digits[:, 3:4] * 128.0 + digits[:, 4:5] == levels).astype(F32).astype(BF16)
            emb = jnp.concatenate([dot(hot_x, tab[:, :half]), dot(hot_y, tab[:, half:])], axis=1)
            lay = side[:, : p.wl] + emb
            low_rows = lay.astype(BF16)
            lay_low[...] = low_rows
            lay_ref[...] = lay
            acc_t[...] = jnp.zeros_like(acc_t)
            acc_l[...] = jnp.zeros_like(acc_l)
        else:
            xt_ref, lay_low, lay_ref, ints_ref, intst_ref, acc_t_in, acc_l_in = in_refs
            n1t, i1t, ht, n1l, i1l, hl = outs[5:]
            x, low_rows = xt_ref[...], lay_low[...]
            acc_t[...] = acc_t_in[...]
            acc_l[...] = acc_l_in[...]
        seg_col = ints_ref[:, 0:1]
        seg_row = intst_ref[0:1, :]
        wait_for(lpad, sem_l)
        for k in range(nb):
            wl_out[k] = dot(spl[...], lpad[k]).astype(BF16)

        def block(k, carry):
            wait_for(wpad.at[k], sem_t.at[k])
            if not exact_t:
                wpad[k, pl.ds(0, p.wt)] = dot(spt[...], wpad[k]).astype(BF16)
            out_copy = pltpu.make_async_copy(wpad.at[k, pl.ds(0, p.wt)], wt_out.at[k], sem_out)
            out_copy.start()
            own_t = (2 * k + core) ^ my_t
            w = wpad[k, pl.ds(0, p.wt)]
            wl = wl_out[k]
            raw = (dot(x, w[:, : 3 * p.ct]) + bt[own_t]).T
            raw_l = (dot(low_rows, wl[:, : 3 * p.cl]) + bl[own_t]).T
            for c in range(3):
                for h in range(nh):
                    top = raw[c * p.ct + h * HD : c * p.ct + (h + 1) * HD]
                    bot = raw_l[c * p.cl + h * LHD : c * p.cl + (h + 1) * LHD]
                    top, bot = top.astype(BF16), bot.astype(BF16)
                    if c == 0:
                        top = top * jnp.asarray(1.0 / math.sqrt(HD), BF16)
                        bot = bot * jnp.asarray(1.0 / math.sqrt(LHD), BF16)
                    qkv[k, c * nh + h, pl.ds(0, HD)] = top
                    qkv[k, c * nh + h, pl.ds(HD, LHD)] = bot
            for h in range(nh):
                scores = dot(qkv[k, nh + h], qkv[k, h], 0, 0)
                scores = jnp.where(seg_col == seg_row, scores, NEG_FILL)
                top_score = jnp.max(scores, axis=0, keepdims=True)
                expo = jnp.exp(scores - top_score)
                row_total = jnp.sum(expo, axis=0, keepdims=True)
                probs = (expo * (1.0 / row_total)).astype(BF16)
                mixed = dot(qkv[k, 2 * nh + h], probs).astype(BF16)
                ctx[k, h] = mixed
                ctx_rows[pl.ds(h * HD, HD)] = mixed[:HD]
                ctx_lay[pl.ds(h * LHD, LHD)] = mixed[HD:]
                lse_ref[k, pl.ds(h, 1), :] = top_score + jnp.log(row_total)
            acc_t[...] += dot(w[:, 3 * p.ct :], ctx_rows[...])
            acc_l[...] += dot(wl[:, 3 * p.cl : 4 * p.cl], ctx_lay[...])
            out_copy.wait()
            return carry

        lax.fori_loop(0, nb, block, 0)
        if first:
            acc_t_out[...] = acc_t[...]
            acc_l_out[...] = acc_l[...]
        else:
            for residual, acc, vec, n_ref, i_ref, h_ref in (
                (x.astype(F32), acc_t, vt, n1t, i1t, ht),
                (lay_ref[...], acc_l, vl, n1l, i1l, hl),
            ):
                normed, inv = norm_parts(residual + acc[...].T + vec[2:3])
                n_ref[...] = normed
                i_ref[...] = inv
                h_ref[...] = (normed * vec[3:4] + vec[4:5]).astype(BF16)

    outs = [
        shape((nb, p.wt, p.cols), BF16),
        shape((nb, p.wl, p.cols), BF16),
        shape((nb, 3 * nh, hw, rows), BF16),
        shape((nb, nh, hw, rows), BF16),
        shape((nb, 8, rows), F32),
    ]
    if first:
        outs += [
            shape((rows, p.wt), BF16),
            shape((rows, p.wl), BF16),
            shape((rows, p.wl), F32),
            shape((rows, 8), F32),
            shape((8, rows), F32),
            shape((p.wt, rows), F32),
            shape((p.wl, rows), F32),
        ]
    else:
        outs += [
            shape((rows, p.wt), F32),
            shape((rows, 1), F32),
            shape((rows, p.wt), BF16),
            shape((rows, p.wl), F32),
            shape((rows, 1), F32),
            shape((rows, p.wl), BF16),
        ]
    scratch = [
        pltpu.VMEM((nb, padded_t, p.cols), BF16),
        pltpu.VMEM((nb, padded_l, p.cols), BF16),
        pltpu.VMEM((p.wt, rows), F32),
        pltpu.VMEM((p.wl, rows), F32),
        pltpu.VMEM((p.ct, rows), BF16),
        pltpu.VMEM((p.cl, rows), BF16),
        pltpu.SemaphoreType.DMA((nb,)),
        pltpu.SemaphoreType.DMA,
        pltpu.SemaphoreType.DMA,
    ]
    args = (me2, bias_t, bias_l, vec_t, vec_l, spread_t, spread_l, *rows_in, *pieces)
    return kernel_call(
        body,
        outs,
        [SM] + [VM] * (6 + n_in) + [ANY] * 4,
        [ANY] + [VM] * (len(outs) - 1),
        scratch,
        args,
    )


def feed_forward(p, me2, core, pieces, w_lay, h_t, h_l, bin_t, bin_l, spread_t, rest_in):
    rows = p.rows
    padded_t = p.n_dp * p.ra
    exact_t = p.ra == p.d_own
    root = 1.0 / math.sqrt(2.0)
    first = core == 0
    nb = p.n_t // 2
    n_rest = len(rest_in)

    def body(*refs):
        (me_ref, wl, ht, hl, bt, bl, spt), refs = refs[:7], refs[7:]
        rest_refs, refs = refs[:n_rest], refs[n_rest:]
        piece_refs, refs = refs[:4], refs[4:]
        n_out = 7 if first else 13
        outs, scratch = refs[:n_out], refs[n_out:]
        f_out, g_t, gp_t, g_l, gp_l = outs[:5]
        fpad, acc_t, acc_l, sem_t, sem_out = scratch
        my_dp, my_t = me_ref[0], me_ref[1]
        for k in range(nb):
            for m in range(2):
                for y in range(2):
                    src = piece_refs[y].at[k] if m == 0 else piece_refs[2 + k].at[y]
                    for z in range(p.far):
                        row = pl.multiple_of(((z * 2 + y) ^ my_dp) * p.ra, 16)
                        pltpu.make_async_copy(
                            src.at[z], fpad.at[k, m, pl.ds(row, p.ra)], sem_t.at[k]
                        ).start()
        if first:
            acc_t[...] = jnp.zeros_like(acc_t)
            acc_l[...] = jnp.zeros_like(acc_l)
        else:
            acc_t_in, acc_l_in, n1t_, n1l_, c0, c1, c2, c3, vt, vl = rest_refs
            acc_t[...] = acc_t_in[...]
            acc_l[...] = acc_l_in[...]

        def gelu(u, g_ref, gp_ref, k):
            cdf = 0.5 + 0.5 * lax.erf(u * root)
            low = (u * cdf).astype(BF16)
            g_ref[k] = low
            dens = jnp.exp(u * u * -0.5) * (1.0 / math.sqrt(2.0 * math.pi))
            gp_ref[k] = (cdf + u * dens).astype(gp_ref.dtype)
            return low

        def block(k, carry):
            wait_for(fpad.at[k], sem_t.at[k])
            if not exact_t:
                for m in range(2):
                    fpad[k, m, pl.ds(0, p.wt)] = dot(spt[...], fpad[k, m]).astype(BF16)
            out_copy = pltpu.make_async_copy(
                fpad.at[k, :, pl.ds(0, p.wt)], f_out.at[k], sem_out
            )
            out_copy.start()
            own_t = (2 * k + core) ^ my_t
            g = gelu(dot(ht[...], fpad[k, 0, pl.ds(0, p.wt)]) + bt[own_t], g_t, gp_t, k)
            acc_t[...] += dot(g, fpad[k, 1, pl.ds(0, p.wt)], 1, 1)
            w = wl[k]
            up = w[:, 4 * p.cl : 4 * p.cl + p.hl]
            down = w[:, 4 * p.cl + p.hl : p.lay_cols]
            g = gelu(dot(hl[...], up) + bl[own_t], g_l, gp_l, k)
            acc_l[...] += dot(g, down, 1, 1)
            out_copy.wait()
            return carry

        lax.fori_loop(0, nb, block, 0)
        if first:
            outs[5][...] = acc_t[...]
            outs[6][...] = acc_l[...]
        else:
            out_tl, dr_t, dr_l, df_t, df_l, gv_t, gv_l, _ = outs[5:]
            cot = jnp.concatenate([ref[...] for ref in (c0, c1, c2, c3)], axis=0).astype(F32)
            for n1, acc, vec, begin, dr_ref, df_ref, gv in (
                (n1t_, acc_t, vt, 0, dr_t, df_t, gv_t),
                (n1l_, acc_l, vl, p.wt, dr_l, df_l, gv_l),
            ):
                width = n1.shape[1]
                ct = cot[:, begin : begin + width]
                h1 = n1[...] * vec[3:4] + vec[4:5]
                n2, inv2 = norm_parts(h1 + acc[...] + vec[5:6])
                out_tl[:, pl.ds(begin, width)] = (n2 * vec[6:7] + vec[7:8]).astype(BF16)
                dr = norm_back(ct, n2, inv2, vec[6:7])
                dr_ref[...] = dr
                df_ref[...] = dr.astype(BF16)
                gv[...] = jnp.zeros_like(gv)
                gv[5:6] = col_sum(dr)
                gv[6:7] = col_sum(ct * n2)
                gv[7:8] = col_sum(ct)
            outs[12][...] = jnp.zeros_like(outs[12])

    outs = [
        shape((nb, 2, p.wt, p.ht), BF16),
        shape((nb, rows, p.ht), BF16),
        shape((nb, rows, p.ht), BF16),
        shape((nb, rows, p.hl), BF16),
        shape((nb, rows, p.hl), BF16),
    ]
    if first:
        outs += [shape((rows, p.wt), F32), shape((rows, p.wl), F32)]
    else:
        outs += [
            shape((rows, p.wt + p.wl), BF16),
            shape((rows, p.wt), F32),
            shape((rows, p.wl), F32),
            shape((rows, p.wt), BF16),
            shape((rows, p.wl), BF16),
            shape((8, p.wt), F32),
            shape((8, p.wl), F32),
            shape((8, 128), F32),
        ]
    scratch = [
        pltpu.VMEM((nb, 2, padded_t, p.ht), BF16),
        pltpu.VMEM((rows, p.wt), F32),
        pltpu.VMEM((rows, p.wl), F32),
        pltpu.SemaphoreType.DMA((nb,)),
        pltpu.SemaphoreType.DMA,
    ]
    args = (me2, w_lay, h_t, h_l, bin_t, bin_l, spread_t, *rest_in, *pieces)
    return kernel_call(
        body,
        outs,
        [SM] + [VM] * (6 + n_rest) + [ANY] * 4,
        [ANY] + [VM] * (len(outs) - 1),
        scratch,
        args,
    )


def store_slots(p, staged, slot_of, my_dp, sem, slices):
    for z in range(p.far):
        for y in range(2):
            at = (z * 2 + y) ^ my_dp
            for dst, per, begin, count, off in slices:
                pltpu.make_async_copy(
                    staged.at[pl.ds(pl.multiple_of(at * per + begin, 16), count)],
                    slot_of(dst, y, z).at[pl.ds(off, count)],
                    sem,
                ).start()


def feed_backward(p, me2, f_all, w_lay, h_t, h_l, df_t, df_l, g_t, gp_t, g_l, gp_l, spread_t, prev, last):
    n_t, rows = p.n_t, p.rows
    padded_t = p.n_dp * p.ra
    exact_t = p.ra == p.d_own
    blocks = [t for t in range(n_t) if t % 2 == (0 if last else 1)]

    def body(*refs):
        (me_ref, f_any, wl, ht, hl, dft, dfl, gt, gpt, gl, gpl, spt), refs = refs[:12], refs[12:]
        if last:
            (pt, pl_, drt, drl, n1t, i1t, n1l, i1l, vt, vl), refs = refs[:10], refs[10:]
            n_out = 11
        else:
            n_out = 7
        outs, scratch = refs[:n_out], refs[n_out:]
        low, high, gfl, dbt, dbl = outs[:5]
        f_in, staged, acc_t, acc_l, sem_in, sem_out = scratch
        my_dp, my_t = me_ref[0], me_ref[1]
        for k, t in enumerate(blocks):
            pltpu.make_async_copy(f_any.at[k], f_in.at[k], sem_in.at[k]).start()
        dfT, hT = dft[...].T, ht[...].T
        dfTl, hTl = dfl[...].T, hl[...].T
        if last:
            acc_t[...] = pt[...]
            acc_l[...] = pl_[...]
        else:
            acc_t[...] = jnp.zeros_like(acc_t)
            acc_l[...] = jnp.zeros_like(acc_l)
        for k, t in enumerate(blocks):
            wait_for(f_in.at[k], sem_in.at[k])
            du = dot(dft[...], f_in[k, 1]) * gpt[k].astype(F32)
            dbt[k] = col_sum(du)
            du_low = du.astype(BF16)
            grads = (dot(hT, du_low).astype(BF16), dot(dfT, gt[k]).astype(BF16))
            for m in range(2):
                value = grads[m]
                if not exact_t:
                    value = dot(spt[...], value, 0, 0).astype(BF16)
                staged[k, m] = value
                x = t // 2
                if m == 0:
                    store_slots(p, staged.at[k, m], lambda d, y, z: low.at[x, y, z], my_dp, sem_out, [(0, p.ra, 0, p.ra, 0)])
                else:
                    store_slots(p, staged.at[k, m], lambda d, y, z: high.at[y, x, z], my_dp, sem_out, [(0, p.ra, 0, p.ra, 0)])
            acc_t[...] += dot(du_low, f_in[k, 0], 1, 1)
            w = wl[k]
            up = w[:, 4 * p.cl : 4 * p.cl + p.hl]
            down = w[:, 4 * p.cl + p.hl : p.lay_cols]
            du = dot(dfl[...], down) * gpl[k].astype(F32)
            dbl[k] = col_sum(du)
            du_low = du.astype(BF16)
            gfl[k, :, pl.ds(0, p.hl)] = dot(hTl, du_low).astype(BF16)
            gfl[k, :, pl.ds(p.hl, p.hl)] = dot(dfTl, gl[k]).astype(BF16)
            acc_l[...] += dot(du_low, up, 1, 1)
        if last:
            dr1t, dr1l, dat, dal, gvt, gvl = outs[5:]
            for dr, acc, n1, i1, vec, o, low_o, gv in (
                (drt, acc_t, n1t, i1t, vt, dr1t, dat, gvt),
                (drl, acc_l, n1l, i1l, vl, dr1l, dal, gvl),
            ):
                dh = dr[...] + acc[...]
                n = n1[...]
                dr1 = norm_back(dh, n, i1[...], vec[3:4])
                o[...] = dr1
                low_o[...] = dr1.astype(BF16)
                gv[...] = jnp.zeros_like(gv)
                gv[2:3] = col_sum(dr1)
                gv[3:4] = col_sum(dh * n)
                gv[4:5] = col_sum(dh)
        else:
            outs[5][...] = acc_t[...]
            outs[6][...] = acc_l[...]
        wait_for(staged, sem_out)

    nb = len(blocks)
    outs = [
        shape((2, 2, p.far, p.ra, p.ht), BF16),
        shape((2, 2, p.far, p.ra, p.ht), BF16),
        shape((nb, p.wl, 2 * p.hl), BF16),
        shape((nb, 1, p.ht), F32),
        shape((nb, 1, p.hl), F32),
    ]
    args = [me2, f_all, w_lay, h_t, h_l, df_t, df_l, g_t, gp_t, g_l, gp_l, spread_t]
    if last:
        args += list(prev)
        outs += [
            shape((rows, p.wt), F32),
            shape((rows, p.wl), F32),
            shape((rows, p.wt), BF16),
            shape((rows, p.wl), BF16),
            shape((8, p.wt), F32),
            shape((8, p.wl), F32),
        ]
    else:
        outs += [shape((rows, p.wt), F32), shape((rows, p.wl), F32)]
    scratch = [
        pltpu.VMEM((nb, 2, p.wt, p.ht), BF16),
        pltpu.VMEM((nb, 2, padded_t, p.ht), BF16),
        pltpu.VMEM((rows, p.wt), F32),
        pltpu.VMEM((rows, p.wl), F32),
        pltpu.SemaphoreType.DMA((nb,)),
        pltpu.SemaphoreType.DMA,
    ]
    specs = [SM, ANY] + [VM] * (len(args) - 2)
    return kernel_call(
        body, outs, specs, [ANY, ANY] + [VM] * (len(outs) - 2), scratch, args
    )


def attend_backward(p, me2, xs, w_all, w_lay, qkv, ctx, lse, x_low, lay_low, ints, ints_t, da_t, da_l, gfl, spread_t, spread_l, prev, last):
    n_t, rows, hw, nh = p.n_t, p.rows, p.hw, p.heads
    padded_t, padded_l = p.n_dp * p.ra, p.n_dp * p.rl
    exact_t = p.ra == p.d_own
    nb = len(xs)
    n_prev = len(prev)

    def body(*refs):
        (me_ref, w_any, wl_ref, qkv_r, ctx_r, lse_r, xl, ll, ir, itr, dat, dal, gfl_r, spt, spl), refs = refs[:15], refs[15:]
        prev_refs, refs = refs[:n_prev], refs[n_prev:]
        outs, scratch = refs[:6], refs[6:]
        low, high, gb_t, gb_l, out_a, out_b = outs
        (w_in, staged, staged_l, acc_t, acc_l, dctx, ctx_s, ctx_l, dp_t, dp_l, bin_rows, sem_in,
         sem_out, sem_bin) = scratch
        my_dp, my_t = me_ref[0], me_ref[1]
        for k, x in enumerate(xs):
            pltpu.make_async_copy(w_any.at[x], w_in.at[k], sem_in.at[k]).start()
        xT, lT = xl[...].T, ll[...].T
        daT, dalT = dat[...].T, dal[...].T
        seg_col, seg_row = ir[:, 0:1], itr[0:1, :]
        if prev:
            acc_t[...] = prev_refs[0][...]
            acc_l[...] = prev_refs[1][...]
        else:
            acc_t[...] = jnp.zeros_like(acc_t)
            acc_l[...] = jnp.zeros_like(acc_l)
        ones = jnp.ones((16, rows), BF16)
        for k, x in enumerate(xs):
            wait_for(w_in.at[k], sem_in.at[k])
            w = w_in[k]
            wl = wl_ref[x]
            d_t = dot(dat[...], w[:, 3 * p.ct :]).T
            d_l = dot(dal[...], wl[:, 3 * p.cl : 4 * p.cl]).T
            for h in range(nh):
                dctx[h, pl.ds(0, HD)] = d_t[h * HD : (h + 1) * HD].astype(BF16)
                dctx[h, pl.ds(HD, LHD)] = d_l[h * LHD : (h + 1) * LHD].astype(BF16)
                ctx_s[pl.ds(h * HD, HD)] = ctx_r[x, h, pl.ds(0, HD)]
                ctx_l[pl.ds(h * LHD, LHD)] = ctx_r[x, h, pl.ds(HD, LHD)]

            for h in range(nh):
                q, key, val = qkv_r[x, h], qkv_r[x, nh + h], qkv_r[x, 2 * nh + h]
                dc = dctx[h]
                scores = dot(key, q, 0, 0)
                probs = jnp.exp(
                    jnp.where(seg_col == seg_row, scores, NEG_FILL) - lse_r[x, pl.ds(h, 1), :]
                )
                low_p = probs.astype(BF16)
                prod = dc.astype(F32) * ctx_r[x, h].astype(F32)
                sum_lay = jnp.sum(prod[HD:], axis=0, keepdims=True)
                sum_all = jnp.sum(prod[:HD], axis=0, keepdims=True) + sum_lay
                dz_all = probs * (dot(val, dc, 0, 0) - sum_all)
                dz_lay = probs * (dot(val[HD:], dc[HD:], 0, 0) - sum_lay)
                ds_t, ds_l = dz_all.astype(BF16), dz_lay.astype(BF16)
                dv = dot(dc, low_p, 1, 1)
                dq_t = dot(key[:HD], ds_t) * (1.0 / math.sqrt(HD))
                dq_l = dot(key[HD:], ds_l) * (1.0 / math.sqrt(LHD))
                dk_t = dot(q[:HD], ds_t, 1, 1)
                dk_l = dot(q[HD:], ds_l, 1, 1)
                for c, (top, bot) in enumerate(((dq_t, dq_l), (dk_t, dk_l), (dv[:HD], dv[HD:]))):
                    dp_t[pl.ds(c * p.ct + h * HD, HD)] = top.astype(BF16)
                    dp_l[pl.ds(c * p.cl + h * LHD, LHD)] = bot.astype(BF16)
            gb_t[k] = dot(ones, dp_t[...], 1, 1)[:8]
            gb_l[k] = dot(ones, dp_l[...], 1, 1)[:8]
            acc_t[...] += dot(w[:, : 3 * p.ct], dp_t[...])
            acc_l[...] += dot(wl[:, : 3 * p.cl], dp_l[...])
            grad = jnp.concatenate(
                [dot(xT, dp_t[...], 1, 1), dot(daT, ctx_s[...], 1, 1)], axis=1
            ).astype(BF16)
            if not exact_t:
                grad = dot(spt[...], grad, 0, 0).astype(BF16)
            staged[k] = grad
            fill = p.cols - p.lay_cols
            grad_l = jnp.concatenate(
                [
                    dot(lT, dp_l[...], 1, 1),
                    dot(dalT, ctx_l[...], 1, 1),
                    gfl_r[x].astype(F32),
                    jnp.zeros((p.wl, fill), F32),
                ],
                axis=1,
            ).astype(BF16)
            staged_l[k] = dot(spl[...], grad_l, 0, 0).astype(BF16)
            rest = p.ra - p.half_a
            slot = lambda d, y, z: (high if d else low).at[k, y, z]
            slices = [(0, p.ra, 0, p.half_a, 0)]
            if rest:
                slices.append((1, p.ra, p.half_a, rest, 0))
            store_slots(p, staged.at[k], slot, my_dp, sem_out.at[0], slices)
            store_slots(p, staged_l.at[k], slot, my_dp, sem_out.at[1], [(1, p.rl, 0, p.rl, rest)])
        if last:
            gt = prev_refs[2][...] + acc_t[...].T
            gl = prev_refs[3][...] + acc_l[...].T
            out_a[:, pl.ds(0, p.wt)] = gt.astype(BF16)
            out_a[:, pl.ds(p.wt, p.wl)] = gl.astype(BF16)
            half = p.wl // 2
            bins = bin_rows.shape[0]
            levels = lax.broadcasted_iota(jnp.int32, (bins, 1), 0).astype(F32)
            for m in range(2):
                row = itr[1 + 2 * m : 2 + 2 * m, :] * 128.0 + itr[2 + 2 * m : 3 + 2 * m, :]
                hot = (levels == row).astype(F32).astype(BF16)
                part = gl[:, m * half : (m + 1) * half]
                top = part.astype(BF16)
                rest_part = (part - top.astype(F32)).astype(BF16)
                both = dot(hot, jnp.concatenate([top, rest_part], axis=1))
                bin_rows[:, pl.ds(m * half, half)] = (both[:, :half] + both[:, half:]).astype(BF16)
            if p.per % 16:
                pltpu.make_async_copy(bin_rows, out_b, sem_bin).start()
            else:
                for r in range(p.total):
                    z, y, x, c = r // 8, (r // 4) % 2, (r // 2) % 2, r % 2
                    at = ((r // n_t) ^ my_dp) * n_t + ((r % n_t) ^ my_t)
                    pltpu.make_async_copy(
                        bin_rows.at[pl.ds(pl.multiple_of(at * p.per, 16), p.per)],
                        out_b.at[c, x, y, z],
                        sem_bin,
                    ).start()
            wait_for(bin_rows, sem_bin)
        else:
            out_a[...] = acc_t[...]
            out_b[...] = acc_l[...]
        wait_for(staged, sem_out.at[0])
        wait_for(staged_l, sem_out.at[1])

    half_b = p.ra + p.rl - p.half_a
    outs = [
        shape((nb, 2, p.far, p.half_a, p.cols), BF16),
        shape((nb, 2, p.far, half_b, p.cols), BF16),
        shape((nb, 8, 3 * p.ct), F32),
        shape((nb, 8, 3 * p.cl), F32),
    ]
    args = [me2, w_all, w_lay, qkv, ctx, lse, x_low, lay_low, ints, ints_t, da_t, da_l, gfl, spread_t, spread_l]
    args += list(prev)
    if last:
        bins = p.per * p.total
        slots = (bins,) if p.per % 16 else (2, 2, 2, p.far, p.per)
        outs += [shape((rows, p.wt + p.wl), BF16), shape((*slots, p.wl), BF16)]
    else:
        outs += [shape((p.wt, rows), F32), shape((p.wl, rows), F32)]
    scratch = [
        pltpu.VMEM((nb, p.wt, p.cols), BF16),
        pltpu.VMEM((nb, padded_t, p.cols), BF16),
        pltpu.VMEM((nb, padded_l, p.cols), BF16),
        pltpu.VMEM((p.wt, rows), F32),
        pltpu.VMEM((p.wl, rows), F32),
        pltpu.VMEM((nh, hw, rows), BF16),
        pltpu.VMEM((p.ct, rows), BF16),
        pltpu.VMEM((p.cl, rows), BF16),
        pltpu.VMEM((3 * p.ct, rows), BF16),
        pltpu.VMEM((3 * p.cl, rows), BF16),
        pltpu.VMEM((p.per * p.total, p.wl), BF16),
        pltpu.SemaphoreType.DMA((nb,)),
        pltpu.SemaphoreType.DMA((2,)),
        pltpu.SemaphoreType.DMA,
    ]
    specs = [SM, ANY] + [VM] * (len(args) - 2)
    out_specs = [ANY, ANY] + [VM] * (len(outs) - 3) + [ANY if last else VM]
    return kernel_call(body, outs, specs, out_specs, scratch, args)


def tie(*groups):
    leaves, tree = jax.tree.flatten(groups)
    return jax.tree.unflatten(tree, lax.optimization_barrier(leaves))


def after(values, *others):
    return tie(values, *others)[0]


def line_of(shard, total):
    return [shard] + [xor_send(shard, total, 8 * r) for r in range(1, total // 8)]


def line_doubled(shard, total, others):
    line = [shard]
    while 8 * len(line) < total:
        held = jnp.stack(line)
        if len(line) > 1:
            held = after(held, others)
        theirs = xor_send(held, total, 8 * len(line))
        line = line + [theirs[z] for z in range(len(line))]
    return line


def halves_of(line, half):
    low = jnp.stack([member[:half] for member in line])
    high = jnp.stack([member[half:] for member in line])
    return low, high


def add_low(mine, theirs):
    return to_low(mine.astype(F32) + theirs.astype(F32))


def reduce_second(mine, got):
    send = [add_low(mine[k][1], got[k][1]) for k in range(2)]
    keep = [add_low(mine[k][0], got[k][0]) for k in range(2)]
    return send, keep


def reduce_line_parts(keep, got):
    return [
        jnp.concatenate([add_low(keep[k][z], got[k][z]) for k in range(2)], axis=0)
        for z in range(keep[0].shape[0])
    ]


def send_line(line, total):
    return line[:1] + [xor_send(line[z], total, 8 * z) for z in range(1, len(line))]


def add_line(line):
    out = line[0].astype(F32)
    for member in line[1:]:
        out = out + member.astype(F32)
    return out


def update_all(factor, matrices, flat, grads):
    states = [member for group in (*matrices, *flat) for member in group]

    def body(*refs):
        factor_ref, grads = refs[0], refs[1:7]
        ins, outs = refs[7:25], refs[25:]
        scale = factor_ref[0, 0]
        for k in range(6):
            w, m, v = (ins[3 * k + j][...] for j in range(3))
            results = adamw_step(
                w, m, v, grads[k][...] * scale, WEIGHT_DECAY if k < 4 else 0.0, LEARN_RATES[k]
            )
            for j in range(3):
                outs[3 * k + j][...] = results[j]

    return list(
        kernel_call(
            body,
            [shape(v.shape, F32) for v in states],
            [SM] + [VM] * 24,
            [VM] * 18,
            [],
            (factor.reshape(1, 1), *grads, *states),
        )
    )


def relative(blocks, me):
    total = blocks.shape[0]
    step = 1
    while step < total:
        pairs = blocks.reshape(total // (2 * step), 2, step, *blocks.shape[1:])
        swapped = jnp.stack([pairs[:, 1], pairs[:, 0]], axis=1)
        blocks = jnp.where((me // step) % 2 == 0, pairs, swapped).reshape(blocks.shape)
        step = step * 2
    return blocks


def on_device(
    text_in,
    layout_in,
    segment_ids,
    box_bins,
    text_cot,
    layout_cot,
    attend_text,
    attend_text_mean,
    attend_text_square,
    feed_text,
    feed_text_mean,
    feed_text_square,
    attend_layout,
    attend_layout_mean,
    attend_layout_square,
    feed_layout,
    feed_layout_mean,
    feed_layout_square,
    vectors,
    vectors_mean,
    vectors_square,
    tables,
    tables_mean,
    tables_square,
):
    n_dp, n_t = lax.axis_size("dp"), lax.axis_size("tensor")
    total = n_dp * n_t
    t_pos = lax.axis_index("tensor")
    pages, quarter, wt = text_in.shape
    wl = layout_in.shape[1] // quarter
    d_own, dl_own = attend_text.shape[0], attend_layout.shape[0]
    ct, cl = attend_text.shape[2], attend_layout.shape[2]
    ht, hl = feed_text.shape[2], feed_layout.shape[2]


    p = Plan(n_dp, n_t, quarter, wt, wl, ct, cl, ht, hl, tables.shape[0] // wl)
    me = lax.axis_index("dp") * n_t + t_pos
    me2 = jnp.stack([lax.axis_index("dp"), t_pos]).astype(jnp.int32)
    lay_cols = p.lay_cols

    def pad_rows(values, count):
        return jnp.pad(values, ((0, count - values.shape[0]), (0, 0)))

    lay_pack = jnp.concatenate(
        [
            to_low(attend_layout).reshape(dl_own, 4 * cl),
            to_low(feed_layout).reshape(dl_own, 2 * hl),
        ],
        axis=1,
    )
    lay_pack = jnp.pad(lay_pack, ((0, p.rl - dl_own), (0, p.cols - lay_cols)))
    attend_pack = jnp.concatenate(
        [pad_rows(to_low(attend_text).reshape(d_own, p.cols), p.ra), lay_pack]
    )
    low_feed = to_low(feed_text)
    feed_pack = jnp.concatenate(
        [pad_rows(low_feed[:, 0], p.ra), pad_rows(low_feed[:, 1], p.ra)]
    )
    bins = box_bins.reshape(pages, quarter, 2)
    digits = jnp.stack(
        [segment_ids, bins[..., 0] // 128, bins[..., 0] % 128, bins[..., 1] // 128, bins[..., 1] % 128],
        axis=-1,
    )
    packed_in = jnp.concatenate(
        [
            text_in,
            layout_in.reshape(pages, quarter, wl),
            jnp.pad(to_low(digits), ((0, 0), (0, 0), (0, 59))),
        ],
        axis=2,
    )
    packed_cot = jnp.concatenate([text_cot, layout_cot.reshape(pages, quarter, wl)], axis=2)

    def page_of(values):
        take = lambda r: lax.dynamic_index_in_dim(values, t_pos ^ r, 0, keepdims=False)
        return [take(0)] + [xor_send(take(r), total, r) for r in range(1, n_t)]

    def send_rows(page):
        blocks = page.reshape(n_t, quarter, page.shape[-1])
        return [blocks[0]] + [xor_send(blocks[r], total, r) for r in range(1, n_t)]

    def pages_of(blocks):
        out = jnp.zeros((n_t,) + blocks[0].shape, blocks[0].dtype)
        for r in range(n_t):
            out = lax.dynamic_update_slice(out, blocks[r][None], (t_pos ^ r, 0, 0))
        return out

    send = lambda values, distance: xor_send(values, total, distance)

    line_a = line_of(attend_pack, total)
    xin = page_of(packed_in)
    low, high = halves_of(line_a, p.half_a)
    low, high = after((low, high), xin)
    line_f = line_doubled(feed_pack, total, line_a)
    low0, high0 = jnp.stack([low, send(low, 2)]), jnp.stack([high, send(high, 4)])
    low4, high2 = send(low0, 4), send(high0, 2)
    low1, high1 = send(low0, 1), send(high0, 1)
    late_vectors, late_tables = after((vectors, tables), low0, high0)
    parts = split_vectors(late_vectors, [wt, wl], [n_t * ht, n_t * hl])
    biases, vecs, bins_in = [], [], []
    for s, width in ((0, ct), (1, cl)):
        vec, hidden = parts[s]
        biases.append(
            jnp.concatenate(
                [
                    vec[0].reshape(n_t, 1, width),
                    jnp.zeros((n_t, 1, width), F32),
                    vec[1].reshape(n_t, 1, width),
                ],
                axis=2,
            )
        )
        vecs.append(jnp.stack(vec))
        bins_in.append(hidden.reshape(n_t, 1, -1))
    table_rows = to_low(late_tables.reshape(-1, wl))
    spread_t = p.spread(d_own, p.ra) if p.ra != d_own else jnp.zeros((16, 128), BF16)
    spread_l = p.spread(dl_own, p.rl)

    flow, fhigh = halves_of(after(line_f, low0, high0), p.ra)
    flow, fhigh = after((flow, fhigh), low4, high2)
    att_fix = (biases[0], biases[1], vecs[0], vecs[1], spread_t, spread_l)
    low5, high3 = send(low4, 1), send(high2, 1)
    flow_x, fhigh_y = send(flow, 2), send(fhigh, 4)
    (w_all0, w_lay0, qkv0, ctx0, lse0, *row_state) = attend_forward(
        p, me2, 0, (*xin, table_rows), *att_fix, [low0, low4, high0, high2]
    )
    row_state, qkv0, low5, high3, low1, high1, flow_x, fhigh_y = tie(
        row_state, qkv0, low5, high3, low1, high1, flow_x, fhigh_y
    )
    flow0, fhigh0 = jnp.stack([flow, flow_x]), jnp.stack([fhigh, fhigh_y])
    row_state = after(row_state, flow0, fhigh0)
    flow4, fhigh2 = send(flow0, 4), send(fhigh0, 2)
    flow1, fhigh1 = send(flow0, 1), send(fhigh0, 1)
    (w_all1, w_lay1, qkv1, ctx1, lse1, n1t, i1t, h_t, n1l, i1l, h_l) = attend_forward(
        p, me2, 1, row_state, *att_fix, [low1, low5, high1, high3]
    )
    x_low, lay_low, _, ints, ints_t = row_state[:5]
    n1t, n1l, h_t, h_l, w_lay1, flow4, fhigh2, packed_cot = tie(
        n1t, n1l, h_t, h_l, w_lay1, flow4, fhigh2, packed_cot
    )
    flow5, fhigh3 = send(flow4, 1), send(fhigh2, 1)
    cots = page_of(packed_cot)
    (f_all0, g_t0, gp_t0, g_l0, gp_l0, acc_t, acc_l) = feed_forward(
        p, me2, 0, [flow0, flow4, fhigh0, fhigh2], w_lay0, h_t, h_l, bins_in[0], bins_in[1], spread_t, ()
    )
    acc_t, acc_l, f_all0, flow5, fhigh3, flow1, fhigh1, cots = tie(
        acc_t, acc_l, f_all0, flow5, fhigh3, flow1, fhigh1, cots
    )
    (f_all1, g_t1, gp_t1, g_l1, gp_l1, out_rows, dr_t, dr_l, df_t, df_l, gv2t, gv2l, _) = feed_forward(
        p, me2, 1, [flow1, flow5, fhigh1, fhigh3], w_lay1, h_t, h_l, bins_in[0], bins_in[1], spread_t,
        (acc_t, acc_l, n1t, n1l, *cots, vecs[0], vecs[1]),
    )
    rows_out = send_rows(out_rows)
    (gf_low1, gf_high1, gfl1, dbt1, dbl1, acc_t, acc_l) = feed_backward(
        p, me2, f_all1, w_lay1, h_t, h_l, df_t, df_l, g_t1, gp_t1, g_l1, gp_l1, spread_t, None, False
    )
    rows_out, gf_low1, gf_high1, gfl1, dbt1, dbl1, acc_t, acc_l = tie(
        rows_out, gf_low1, gf_high1, gfl1, dbt1, dbl1, acc_t, acc_l
    )
    got = [send(gf_low1, 1), send(gf_high1, 1)]
    (gf_low0, gf_high0, gfl0, dbt0, dbl0, dr1t, dr1l, da_t, da_l, gv1t, gv1l) = feed_backward(
        p, me2, f_all0, w_lay0, h_t, h_l, df_t, df_l, g_t0, gp_t0, g_l0, gp_l0, spread_t,
        (acc_t, acc_l, dr_t, dr_l, n1t, i1t, n1l, i1l, vecs[0], vecs[1]), True
    )
    got, gf_low0, gf_high0, gfl0, dbt0, dbl0, dr1t, dr1l, da_t, da_l, gv1t, gv1l = tie(
        got, gf_low0, gf_high0, gfl0, dbt0, dbl0, dr1t, dr1l, da_t, da_l, gv1t, gv1l
    )
    next_f, keep_f = reduce_second((gf_low0, gf_high0), got)
    da_t = after(da_t, next_f, keep_f)
    got_f = [send(next_f[0], 2), send(next_f[1], 4)]
    att_args = (x_low, lay_low, ints, ints_t, da_t, da_l)
    (ga_low1, ga_high1, gb_t1, gb_l1, acc_t, acc_l) = attend_backward(
        p, me2, (0, 1), w_all1, w_lay1, qkv1, ctx1, lse1, *att_args, gfl1, spread_t, spread_l, (), False
    )
    got_f, ga_low1, ga_high1, gb_t1, gb_l1, acc_t, acc_l = tie(
        got_f, ga_low1, ga_high1, gb_t1, gb_l1, acc_t, acc_l
    )
    next_f, keep_f = reduce_second(keep_f, got_f)
    acc_t = after(acc_t, next_f, keep_f)
    got = [send(ga_low1, 1), send(ga_high1, 1)]
    got_f = [send(next_f[0], 4), send(next_f[1], 2)]
    core_args = (w_all0, w_lay0, qkv0, ctx0, lse0, *att_args, gfl0, spread_t, spread_l)
    (low_x1, high_x1, gb_t02, gb_l02, acc_t, acc_l) = attend_backward(
        p, me2, (1,), *core_args, (acc_t, acc_l), False
    )
    got, got_f, low_x1, high_x1, gb_t02, gb_l02, acc_t, acc_l = tie(
        got, got_f, low_x1, high_x1, gb_t02, gb_l02, acc_t, acc_l
    )
    low_x1 = add_low(low_x1[0], got[0][1])
    high_x1 = add_low(high_x1[0], got[1][1])
    line_f = reduce_line_parts(keep_f, got_f)
    acc_t = after(acc_t, low_x1, high_x1, line_f)
    got_low = send(low_x1, 2)
    got_high1 = send(high_x1[1], 4)
    early = (p.far + 2) // 2
    line_f, late_f = send_line(line_f[:early], total), line_f[early:]
    (low_x0, high_x0, gb_t00, gb_l00, grad_rows, table_grad) = attend_backward(
        p, me2, (0,), *core_args, (acc_t, acc_l, dr1t, dr1l), True
    )
    low_x0, high_x0, gb_t00, gb_l00, grad_rows, table_grad = after(
        (low_x0, high_x0, gb_t00, gb_l00, grad_rows, table_grad), got_high1, got_low, line_f
    )
    line_f = line_f + [send(late_f[z], 8 * (early + z)) for z in range(len(late_f))]
    if p.per % 16:
        table_grad = relative(table_grad.reshape(total, p.per, wl), me)
        table_grad = table_grad.reshape(p.far, 2, 2, 2, p.per, wl).transpose(3, 2, 1, 0, 4, 5)
    table_got = send(table_grad[1], 1)
    table_sum = add_low(table_grad[0], table_got)
    rest = p.ra - p.half_a
    spare = high_x0.shape[-2] - rest - p.per

    def placed(part):
        edges = ((0, 0),) * (part.ndim - 2) + ((rest, spare), (lay_cols, p.cols - lay_cols - wl))
        return jnp.pad(part, edges).astype(F32)

    high_x0 = to_low(high_x0[0].astype(F32) + got[1][0].astype(F32) + placed(table_sum[0]))
    got_high0 = send(high_x0[1], 4)
    got_table = send(table_sum[1, 1], 4)
    low_x0, got_low = after((low_x0, got_low), high_x0)
    low = to_low(low_x0[0].astype(F32) + got[0][0].astype(F32) + got_low.astype(F32))
    got_low = send(low[1], 4)
    table_x1 = add_low(table_sum[1, 0], got_table)
    high_1 = to_low(high_x1[0].astype(F32) + got_high1.astype(F32) + placed(table_x1))
    got_high = send(high_1, 2)
    pieces = (gb_t1, gb_l1, gb_t02, gb_l02, gb_t00, gb_l00, dbt0, dbt1, dbl0, dbl1, gv1t, gv1l, gv2t, gv2l)
    (gb_t1, gb_l1, gb_t02, gb_l02, gb_t00, gb_l00, dbt0, dbt1, dbl0, dbl1, gv1t, gv1l, gv2t, gv2l) = after(
        pieces, high_1, low
    )
    gb_t0 = jnp.concatenate([gb_t00, gb_t02])
    gb_l0 = jnp.concatenate([gb_l00, gb_l02])
    feed_sum = add_line(after(line_f, high_1, low))
    high_0 = add_low(high_x0[0], got_high0)
    line_a = send_line(reduce_line_parts((low[0], high_0), (got_low, got_high)), total)
    got_a = (got_low, got_high)
    feed_sum = after(feed_sum, got_a)
    attend_sum = add_line(line_a)
    rows_grad = send_rows(after(grad_rows, got_a))
    rows_out = after(rows_out, got_a)

    def by_block(odd, even):
        both = jnp.stack([even[0], odd[0], even[1], odd[1]]).reshape(n_t, -1)
        order = jnp.arange(n_t) ^ t_pos
        hot = order[:, None] == jnp.arange(n_t)[None, :]
        return jnp.sum(jnp.where(hot[:, :, None], both[None], 0.0), axis=1).reshape(-1)

    gv_t, gv_l = gv2t + gv1t, gv2l + gv1l
    vector_grad = jnp.concatenate(
        [
            by_block(gb_t1[:, 0, : ct], gb_t0[:, 0, : ct]),
            by_block(gb_t1[:, 0, 2 * ct :], gb_t0[:, 0, 2 * ct :]),
            gv_t[2:].reshape(-1),
            by_block(dbt1, dbt0),
            by_block(gb_l1[:, 0, : cl], gb_l0[:, 0, : cl]),
            by_block(gb_l1[:, 0, 2 * cl :], gb_l0[:, 0, 2 * cl :]),
            gv_l[2:].reshape(-1),
            by_block(dbl1, dbl0),
        ]
    )
    own_sq = jnp.sum(feed_sum * feed_sum) + jnp.sum(attend_sum * attend_sum)
    n_vec = vector_grad.shape[0]
    summed = jnp.pad(vector_grad, (0, round_up(n_vec + 1, 1024) - n_vec)).reshape(-1, 128)
    spot = (lax.broadcasted_iota(jnp.int32, summed.shape, 0) == n_vec // 128) & (
        lax.broadcasted_iota(jnp.int32, summed.shape, 1) == n_vec % 128
    )
    summed = jnp.where(spot, own_sq, summed)
    spread_table = to_low(attend_sum[p.ra : p.ra + p.per, lay_cols : lay_cols + wl])
    distance = total // 2
    while distance:
        other = send(summed, distance)
        theirs = send(after(spread_table, summed), distance)
        summed = summed + other
        bit = (me // distance) % 2
        spread_table = jnp.where(
            bit == 0, jnp.stack([spread_table, theirs]), jnp.stack([theirs, spread_table])
        )
        distance = distance // 2
    deep = spread_table.ndim - 2
    order = tuple(range(deep - 1, -1, -1)) + (deep, deep + 1)
    table_grad = spread_table.transpose(order).reshape(-1, 128).astype(F32)
    vector_grad = summed
    all_sq = jnp.sum(jnp.where(spot, 0.0, summed * summed))
    shared_sq = all_sq + summed[n_vec // 128, n_vec % 128]
    clip_norm = jnp.sqrt(shared_sq)
    factor = jnp.minimum(1.0, CLIP_NORM / (clip_norm + 1e-06))
    flat = [
        [v.reshape(-1, 128) for v in group]
        for group in ((vectors, vectors_mean, vectors_square), (tables, tables_mean, tables_square))
    ]
    lay_sum = attend_sum[p.ra : p.ra + dl_own]
    grads = (
        attend_sum[:d_own].reshape(d_own, 4, ct),
        jnp.stack([feed_sum[:d_own], feed_sum[p.ra : p.ra + d_own]], axis=1),
        lay_sum[:, : 4 * cl].reshape(dl_own, 4, cl),
        lay_sum[:, 4 * cl : lay_cols].reshape(dl_own, 2, hl),
        vector_grad[: n_vec // 128],
        table_grad,
    )
    matrices = (
        (attend_text, attend_text_mean, attend_text_square),
        (feed_text, feed_text_mean, feed_text_square),
        (attend_layout, attend_layout_mean, attend_layout_square),
        (feed_layout, feed_layout_mean, feed_layout_square),
    )
    updated = update_all(factor, matrices, flat, grads)
    updated[12:] = [v.reshape(-1) for v in updated[12:]]
    rows_out, rows_grad = pages_of(rows_out), pages_of(rows_grad)
    return (
        rows_out[:, :, :wt],
        rows_out[:, :, wt:].reshape(pages, quarter * wl),
        rows_grad[:, :, :wt].astype(F32),
        rows_grad[:, :, wt:].astype(F32).reshape(pages, quarter * wl),
        *updated,
        clip_norm,
    )


def solution(mesh):
    rows3, rows2, cols3 = P("dp", "tensor", None), P("dp", "tensor"), P("dp", None, "tensor")
    in_specs = (rows3, rows2, rows2, rows2, rows3, rows2) + (cols3,) * 12 + (P(),) * 6
    out_specs = (rows3, rows2, rows3, rows2) + (cols3,) * 12 + (P(),) * 7
    return jax.shard_map(
        on_device, mesh=mesh, in_specs=in_specs, out_specs=out_specs, check_vma=False
    )
```

```python
import functools
import math

import jax
import jax.numpy as jnp
from jax import lax
from jax.experimental import pallas as pl
from jax.experimental.pallas import tpu as pltpu
from jax.sharding import PartitionSpec as P

HD = 64
LHD = 16
STEP = 10

NORM_EPS = 1e-05
NEG_FILL = -1000000000.0
CLIP_NORM = 1.0
LEARN_RATES = (0.3, 0.05, 0.3, 0.05, 0.3, 0.3)
BETA_ONE = 0.9
BETA_TWO = 0.999
ADAM_EPS = 1e-08
WEIGHT_DECAY = 0.01
AXES = ("dp", "tensor")
LAY_ROWS = 32
F32 = jnp.float32
BF16 = jnp.bfloat16


def to_low(values):
    return values.astype(BF16)


def xor_send(values, total, distance):
    return lax.ppermute(values, AXES, [(i, i ^ distance) for i in range(total)])


def split_vectors(packed, widths, hidden):
    result = []
    offset = 0
    for stream in range(2):
        width_now = widths[stream]
        pieces = [packed[offset + k * width_now : offset + (k + 1) * width_now] for k in range(8)]
        offset = offset + 8 * width_now
        result.append((pieces, packed[offset : offset + hidden[stream]]))
        offset = offset + hidden[stream]
    return result


def adamw_step(weight, moment, square, gradient, decay_rate, rate_now):
    new_moment = BETA_ONE * moment + (1.0 - BETA_ONE) * gradient
    new_square = BETA_TWO * square + (1.0 - BETA_TWO) * gradient * gradient
    moment_hat = new_moment / (1.0 - BETA_ONE**STEP)
    square_hat = new_square / (1.0 - BETA_TWO**STEP)
    new_weight = weight - rate_now * (
        moment_hat / (jnp.sqrt(square_hat) + ADAM_EPS) + decay_rate * weight
    )
    return (new_weight, new_moment, new_square)


def lane_mean(values):
    return jnp.sum(values, axis=-1, keepdims=True) * (1.0 / values.shape[-1])


def norm_parts(residual):
    centered = residual - lane_mean(residual)
    inv_std = lax.rsqrt(lane_mean(centered * centered) + NORM_EPS)
    return centered * inv_std, inv_std


def norm_back(gradient, normed, inv_std, gain_vec):
    scaled = gradient * gain_vec
    d_resid = inv_std * (
        scaled - lane_mean(scaled) - normed * lane_mean(scaled * normed)
    )
    return d_resid


def col_sum(values):
    return jnp.sum(values, axis=0, keepdims=True)


def dot(a, b, da=1, db=0):
    return lax.dot_general(a, b, (((da,), (db,)), ((), ())), preferred_element_type=F32)


def round_up(count, step):
    return -(-count // step) * step


class Plan:
    def __init__(self, n_dp, n_t, quarter, wt, wl, ct, cl, ht, hl, bins):
        self.n_dp, self.n_t, self.total = n_dp, n_t, n_dp * n_t
        self.far = self.total // 8
        self.quarter, self.rows = quarter, quarter * n_t
        self.wt, self.wl, self.ct, self.cl, self.ht, self.hl = wt, wl, ct, cl, ht, hl
        self.d_own, self.dl_own = wt // n_dp, wl // n_dp
        self.ra, self.rl = round_up(self.d_own, 16), round_up(self.dl_own, 16)
        self.cols = 4 * ct
        self.half_a = (self.ra + self.rl) // 2
        self.heads = ct // HD
        self.hw = HD + LHD
        self.lay_cols = 4 * cl + 2 * hl
        self.per = bins // self.total

    def spread(self, own, padded):
        out = jnp.arange(own * self.n_dp, dtype=jnp.int32)
        place = (out // own) * padded + out % own
        return (place[:, None] == jnp.arange(padded * self.n_dp, dtype=jnp.int32)[None]).astype(BF16)


VMEM_LIMIT = 60 * 2**20
COST = 10 * 10**9
ANY = pl.BlockSpec(memory_space=pl.ANY)
VM = pl.BlockSpec(memory_space=pltpu.VMEM)
SM = pl.BlockSpec(memory_space=pltpu.SMEM)


def kernel_call(body, outs, in_specs, out_specs, scratch, args):
    return pl.pallas_call(
        body,
        out_shape=outs,
        in_specs=in_specs,
        out_specs=out_specs,
        scratch_shapes=scratch,
        compiler_params=pltpu.CompilerParams(vmem_limit_bytes=VMEM_LIMIT),
        cost_estimate=pl.CostEstimate(flops=COST, bytes_accessed=2**20, transcendentals=0),
    )(*args)


def shape(dims, kind):
    return jax.ShapeDtypeStruct(tuple(dims), kind)


def wait_for(ref, sem):
    pltpu.make_async_copy(ref, ref, sem).wait()


def attend_forward(p, me2, core, rows_in, bias_t, bias_l, vec_t, vec_l, spread_t, spread_l, pieces):
    rows, hw, nh = p.rows, p.hw, p.heads
    padded_t, padded_l = p.n_dp * p.ra, p.n_dp * p.rl
    exact_t = p.ra == p.d_own
    first = core == 0
    nb = p.n_t // 2
    n_in = len(rows_in)

    def body(*refs):
        (me_ref, bt, bl, vt, vl, spt, spl), refs = refs[:7], refs[7:]
        in_refs, refs = refs[:n_in], refs[n_in:]
        piece_refs, refs = refs[:4], refs[4:]
        n_out = 12 if first else 11
        outs, scratch = refs[:n_out], refs[n_out:]
        wt_out, wl_out, qkv, ctx, lse_ref = outs[:5]
        wpad, lpad, acc_t, acc_l, ctx_rows, ctx_lay, sem_t, sem_l, sem_out = scratch
        my_dp, my_t = me_ref[0], me_ref[1]
        for k in range(nb):
            for y in range(2):
                low, high = piece_refs[y].at[k], piece_refs[2 + k].at[y]
                for z in range(p.far):
                    at = (z * 2 + y) ^ my_dp
                    row = pl.multiple_of(at * p.ra, 16)
                    lrow = pl.multiple_of(at * p.rl, 16)
                    pltpu.make_async_copy(
                        low.at[z], wpad.at[k, pl.ds(row, p.half_a)], sem_t.at[k]
                    ).start()
                    rest = p.ra - p.half_a
                    if rest:
                        pltpu.make_async_copy(
                            high.at[z, pl.ds(0, rest)],
                            wpad.at[k, pl.ds(pl.multiple_of(row + p.half_a, 16), rest)],
                            sem_t.at[k],
                        ).start()
                    pltpu.make_async_copy(
                        high.at[z, pl.ds(rest, p.rl)], lpad.at[k, pl.ds(lrow, p.rl)], sem_l
                    ).start()
        if first:
            x0, x1, x2, x3, tab = in_refs
            xt_ref, lay_low, lay_ref, ints_ref, intst_ref, acc_t_out, acc_l_out = outs[5:]
            for k, ref in enumerate((x0, x1, x2, x3)):
                xt_ref[pl.ds(k * p.quarter, p.quarter), :] = ref[:, : p.wt]
            x = xt_ref[...]
            side = jnp.concatenate([ref[:, p.wt :] for ref in (x0, x1, x2, x3)], axis=0).astype(F32)
            digits = side[:, p.wl : p.wl + 8]
            ints_ref[...] = digits
            intst_ref[...] = digits.T
            half = p.wl // 2
            levels = lax.broadcasted_iota(jnp.int32, (1, tab.shape[0]), 1).astype(F32)
            hot_x = (digits[:, 1:2] * 128.0 + digits[:, 2:3] == levels).astype(F32).astype(BF16)
            hot_y = (digits[:, 3:4] * 128.0 + digits[:, 4:5] == levels).astype(F32).astype(BF16)
            emb = jnp.concatenate([dot(hot_x, tab[:, :half]), dot(hot_y, tab[:, half:])], axis=1)
            lay = side[:, : p.wl] + emb
            low_rows = lay.astype(BF16)
            lay_low[...] = low_rows
            lay_ref[...] = lay
            acc_t[...] = jnp.zeros_like(acc_t)
            acc_l[...] = jnp.zeros_like(acc_l)
        else:
            xt_ref, lay_low, lay_ref, ints_ref, intst_ref, acc_t_in, acc_l_in = in_refs
            n1t, i1t, ht, n1l, i1l, hl = outs[5:]
            x, low_rows = xt_ref[...], lay_low[...]
            acc_t[...] = acc_t_in[...]
            acc_l[...] = acc_l_in[...]
        seg_col = ints_ref[:, 0:1]
        seg_row = intst_ref[0:1, :]
        wait_for(lpad, sem_l)
        for k in range(nb):
            wl_out[k] = dot(spl[...], lpad[k]).astype(BF16)

        def block(k, carry):
            wait_for(wpad.at[k], sem_t.at[k])
            if not exact_t:
                wpad[k, pl.ds(0, p.wt)] = dot(spt[...], wpad[k]).astype(BF16)
            out_copy = pltpu.make_async_copy(wpad.at[k, pl.ds(0, p.wt)], wt_out.at[k], sem_out)
            out_copy.start()
            own_t = (2 * k + core) ^ my_t
            w = wpad[k, pl.ds(0, p.wt)]
            wl = wl_out[k]
            raw = (dot(x, w[:, : 3 * p.ct]) + bt[own_t]).T
            raw_l = (dot(low_rows, wl[:, : 3 * p.cl]) + bl[own_t]).T
            for c in range(3):
                for h in range(nh):
                    top = raw[c * p.ct + h * HD : c * p.ct + (h + 1) * HD]
                    bot = raw_l[c * p.cl + h * LHD : c * p.cl + (h + 1) * LHD]
                    top, bot = top.astype(BF16), bot.astype(BF16)
                    if c == 0:
                        top = top * jnp.asarray(1.0 / math.sqrt(HD), BF16)
                        bot = bot * jnp.asarray(1.0 / math.sqrt(LHD), BF16)
                    qkv[k, c * nh + h, pl.ds(0, HD)] = top
                    qkv[k, c * nh + h, pl.ds(HD, LHD)] = bot
            for h in range(nh):
                scores = dot(qkv[k, nh + h], qkv[k, h], 0, 0)
                scores = jnp.where(seg_col == seg_row, scores, NEG_FILL)
                top_score = jnp.max(scores, axis=0, keepdims=True)
                expo = jnp.exp(scores - top_score)
                row_total = jnp.sum(expo, axis=0, keepdims=True)
                probs = (expo * (1.0 / row_total)).astype(BF16)
                mixed = dot(qkv[k, 2 * nh + h], probs).astype(BF16)
                ctx[k, h] = mixed
                ctx_rows[pl.ds(h * HD, HD)] = mixed[:HD]
                ctx_lay[pl.ds(h * LHD, LHD)] = mixed[HD:]
                lse_ref[k, pl.ds(h, 1), :] = top_score + jnp.log(row_total)
            acc_t[...] += dot(w[:, 3 * p.ct :], ctx_rows[...])
            acc_l[...] += dot(wl[:, 3 * p.cl : 4 * p.cl], ctx_lay[...])
            out_copy.wait()
            return carry

        lax.fori_loop(0, nb, block, 0)
        if first:
            acc_t_out[...] = acc_t[...]
            acc_l_out[...] = acc_l[...]
        else:
            for residual, acc, vec, n_ref, i_ref, h_ref in (
                (x.astype(F32), acc_t, vt, n1t, i1t, ht),
                (lay_ref[...], acc_l, vl, n1l, i1l, hl),
            ):
                normed, inv = norm_parts(residual + acc[...].T + vec[2:3])
                n_ref[...] = normed
                i_ref[...] = inv
                h_ref[...] = (normed * vec[3:4] + vec[4:5]).astype(BF16)

    outs = [
        shape((nb, p.wt, p.cols), BF16),
        shape((nb, p.wl, p.cols), BF16),
        shape((nb, 3 * nh, hw, rows), BF16),
        shape((nb, nh, hw, rows), BF16),
        shape((nb, 8, rows), F32),
    ]
    if first:
        outs += [
            shape((rows, p.wt), BF16),
            shape((rows, p.wl), BF16),
            shape((rows, p.wl), F32),
            shape((rows, 8), F32),
            shape((8, rows), F32),
            shape((p.wt, rows), F32),
            shape((p.wl, rows), F32),
        ]
    else:
        outs += [
            shape((rows, p.wt), F32),
            shape((rows, 1), F32),
            shape((rows, p.wt), BF16),
            shape((rows, p.wl), F32),
            shape((rows, 1), F32),
            shape((rows, p.wl), BF16),
        ]
    scratch = [
        pltpu.VMEM((nb, padded_t, p.cols), BF16),
        pltpu.VMEM((nb, padded_l, p.cols), BF16),
        pltpu.VMEM((p.wt, rows), F32),
        pltpu.VMEM((p.wl, rows), F32),
        pltpu.VMEM((p.ct, rows), BF16),
        pltpu.VMEM((p.cl, rows), BF16),
        pltpu.SemaphoreType.DMA((nb,)),
        pltpu.SemaphoreType.DMA,
        pltpu.SemaphoreType.DMA,
    ]
    args = (me2, bias_t, bias_l, vec_t, vec_l, spread_t, spread_l, *rows_in, *pieces)
    return kernel_call(
        body,
        outs,
        [SM] + [VM] * (6 + n_in) + [ANY] * 4,
        [ANY] + [VM] * (len(outs) - 1),
        scratch,
        args,
    )


def feed_forward(p, me2, pieces, w_lay, h_t, h_l, bin_t, bin_l, spread_t):
    rows = p.rows
    padded_t = p.n_dp * p.ra
    exact_t = p.ra == p.d_own
    root = 1.0 / math.sqrt(2.0)
    nb = p.n_t // 2

    def body(*refs):
        (me_ref, wl, ht, hl, bt, bl, spt), refs = refs[:7], refs[7:]
        piece_refs, refs = refs[:4], refs[4:]
        outs, scratch = refs[:7], refs[7:]
        f_out, g_t, gp_t, g_l, gp_l = outs[:5]
        fpad, acc_t, acc_l, sem_t, sem_out = scratch
        my_dp, my_t = me_ref[0], me_ref[1]
        for k in range(nb):
            for m in range(2):
                for y in range(2):
                    src = piece_refs[y].at[k] if m == 0 else piece_refs[2 + k].at[y]
                    for z in range(p.far):
                        row = pl.multiple_of(((z * 2 + y) ^ my_dp) * p.ra, 16)
                        pltpu.make_async_copy(
                            src.at[z], fpad.at[k, m, pl.ds(row, p.ra)], sem_t.at[k]
                        ).start()
        acc_t[...] = jnp.zeros_like(acc_t)
        acc_l[...] = jnp.zeros_like(acc_l)

        def gelu(u, g_ref, gp_ref, k):
            cdf = 0.5 + 0.5 * lax.erf(u * root)
            low = (u * cdf).astype(BF16)
            g_ref[k] = low
            dens = jnp.exp(u * u * -0.5) * (1.0 / math.sqrt(2.0 * math.pi))
            gp_ref[k] = (cdf + u * dens).astype(gp_ref.dtype)
            return low

        def block(k, carry):
            wait_for(fpad.at[k], sem_t.at[k])
            if not exact_t:
                for m in range(2):
                    fpad[k, m, pl.ds(0, p.wt)] = dot(spt[...], fpad[k, m]).astype(BF16)
            out_copy = pltpu.make_async_copy(
                fpad.at[k, :, pl.ds(0, p.wt)], f_out.at[k], sem_out
            )
            out_copy.start()
            own_t = (2 * k) ^ my_t
            g = gelu(dot(ht[...], fpad[k, 0, pl.ds(0, p.wt)]) + bt[own_t], g_t, gp_t, k)
            acc_t[...] += dot(g, fpad[k, 1, pl.ds(0, p.wt)], 1, 1)
            w = wl[k]
            up = w[:, 4 * p.cl : 4 * p.cl + p.hl]
            down = w[:, 4 * p.cl + p.hl : p.lay_cols]
            g = gelu(dot(hl[...], up) + bl[own_t], g_l, gp_l, k)
            acc_l[...] += dot(g, down, 1, 1)
            out_copy.wait()
            return carry

        lax.fori_loop(0, nb, block, 0)
        outs[5][...] = acc_t[...]
        outs[6][...] = acc_l[...]

    outs = [
        shape((nb, 2, p.wt, p.ht), BF16),
        shape((nb, rows, p.ht), BF16),
        shape((nb, rows, p.ht), BF16),
        shape((nb, rows, p.hl), BF16),
        shape((nb, rows, p.hl), BF16),
    ]
    outs += [shape((rows, p.wt), F32), shape((rows, p.wl), F32)]
    scratch = [
        pltpu.VMEM((nb, 2, padded_t, p.ht), BF16),
        pltpu.VMEM((rows, p.wt), F32),
        pltpu.VMEM((rows, p.wl), F32),
        pltpu.SemaphoreType.DMA((nb,)),
        pltpu.SemaphoreType.DMA,
    ]
    args = (me2, w_lay, h_t, h_l, bin_t, bin_l, spread_t, *pieces)
    return kernel_call(
        body,
        outs,
        [SM] + [VM] * 6 + [ANY] * 4,
        [ANY] + [VM] * (len(outs) - 1),
        scratch,
        args,
    )


def feed_middle(p, me2, pieces, w_lay, h_t, h_l, bin_t, bin_l, spread_t, rest_in):
    rows = p.rows
    padded_t = p.n_dp * p.ra
    exact_t = p.ra == p.d_own
    root = 1.0 / math.sqrt(2.0)
    nb = p.n_t // 2

    def body(*refs):
        (me_ref, wl, ht, hl, bt, bl, spt), refs = refs[:7], refs[7:]
        (acc_t_in, acc_l_in, n1t_, n1l_, c0, c1, c2, c3, vt, vl), refs = refs[:10], refs[10:]
        piece_refs, refs = refs[:4], refs[4:]
        outs, scratch = refs[:14], refs[14:]
        (low, high, gfl, dbt, dbl, out_tl, dr_t, dr_l, df_t, df_l, gv_t, gv_l, dh_t, dh_l) = outs
        fpad, staged, acc_t, acc_l, g_t, gp_t, g_l, gp_l, sem_t, sem_out = scratch
        my_dp, my_t = me_ref[0], me_ref[1]
        for k in range(nb):
            for m in range(2):
                for y in range(2):
                    src = piece_refs[y].at[k] if m == 0 else piece_refs[2 + k].at[y]
                    for z in range(p.far):
                        row = pl.multiple_of(((z * 2 + y) ^ my_dp) * p.ra, 16)
                        pltpu.make_async_copy(
                            src.at[z], fpad.at[k, m, pl.ds(row, p.ra)], sem_t.at[k]
                        ).start()
        acc_t[...] = acc_t_in[...]
        acc_l[...] = acc_l_in[...]

        def gelu(u, g_ref, gp_ref, k):
            cdf = 0.5 + 0.5 * lax.erf(u * root)
            value = (u * cdf).astype(BF16)
            g_ref[k] = value
            dens = jnp.exp(u * u * -0.5) * (1.0 / math.sqrt(2.0 * math.pi))
            gp_ref[k] = cdf + u * dens
            return value

        for k in range(nb):
            wait_for(fpad.at[k], sem_t.at[k])
            if not exact_t:
                for m in range(2):
                    fpad[k, m, pl.ds(0, p.wt)] = dot(spt[...], fpad[k, m]).astype(BF16)
            own_t = (2 * k + 1) ^ my_t
            g = gelu(dot(ht[...], fpad[k, 0, pl.ds(0, p.wt)]) + bt[own_t], g_t, gp_t, k)
            acc_t[...] += dot(g, fpad[k, 1, pl.ds(0, p.wt)], 1, 1)
            w = wl[k]
            up = w[:, 4 * p.cl : 4 * p.cl + p.hl]
            down = w[:, 4 * p.cl + p.hl : p.lay_cols]
            g = gelu(dot(hl[...], up) + bl[own_t], g_l, gp_l, k)
            acc_l[...] += dot(g, down, 1, 1)
        for n1, acc, vec, begin, dr_ref, df_ref, gv in (
            (n1t_, acc_t, vt, 0, dr_t, df_t, gv_t),
            (n1l_, acc_l, vl, p.wt, dr_l, df_l, gv_l),
        ):
            width = n1.shape[1]
            per = p.quarter
            h1 = n1[...] * vec[3:4] + vec[4:5]
            n2, inv2 = norm_parts(h1 + acc[...] + vec[5:6])
            out_tl[:, pl.ds(begin, width)] = (n2 * vec[6:7] + vec[7:8]).astype(BF16)
            ct = jnp.concatenate([ref[:, begin : begin + width] for ref in (c0, c1, c2, c3)], axis=0).astype(F32)
            dr = norm_back(ct, n2, inv2, vec[6:7])
            dr_ref[...] = dr
            df_ref[...] = dr.astype(BF16)
            gv[...] = jnp.zeros_like(gv)
            gv[5:6] = col_sum(dr)
            gv[6:7] = col_sum(ct * n2)
            gv[7:8] = col_sum(ct)
        df, dfl = df_t[...], df_l[...]
        dfT, hT, dfTl, hTl = df.T, ht[...].T, dfl.T, hl[...].T
        for k in range(nb):
            du = dot(df, fpad[k, 1, pl.ds(0, p.wt)]) * gp_t[k]
            dbt[k] = col_sum(du)
            du_low = du.astype(BF16)
            grads = (dot(hT, du_low).astype(BF16), dot(dfT, g_t[k]).astype(BF16))
            for m in range(2):
                value = grads[m]
                if not exact_t:
                    value = dot(spt[...], value, 0, 0).astype(BF16)
                staged[k, m] = value
                slot = (lambda d, y, z: low.at[k, y, z]) if m == 0 else (lambda d, y, z: high.at[y, k, z])
                store_slots(p, staged.at[k, m], slot, my_dp, sem_out, [(0, p.ra, 0, p.ra, 0)])
            more = dot(du_low, fpad[k, 0, pl.ds(0, p.wt)], 1, 1)
            if k == 0:
                dh_t[...] = more
            else:
                dh_t[...] += more
            w = wl[k]
            up = w[:, 4 * p.cl : 4 * p.cl + p.hl]
            down = w[:, 4 * p.cl + p.hl : p.lay_cols]
            du = dot(dfl, down) * gp_l[k]
            dbl[k] = col_sum(du)
            du_low = du.astype(BF16)
            gfl[k, :, pl.ds(0, p.hl)] = dot(hTl, du_low).astype(BF16)
            gfl[k, :, pl.ds(p.hl, p.hl)] = dot(dfTl, g_l[k]).astype(BF16)
            more = dot(du_low, up, 1, 1)
            if k == 0:
                dh_l[...] = more
            else:
                dh_l[...] += more
        wait_for(staged, sem_out)

    outs = [
        shape((2, 2, p.far, p.ra, p.ht), BF16),
        shape((2, 2, p.far, p.ra, p.ht), BF16),
        shape((nb, p.wl, 2 * p.hl), BF16),
        shape((nb, 1, p.ht), F32),
        shape((nb, 1, p.hl), F32),
        shape((rows, p.wt + p.wl), BF16),
        shape((rows, p.wt), F32),
        shape((rows, p.wl), F32),
        shape((rows, p.wt), BF16),
        shape((rows, p.wl), BF16),
        shape((8, p.wt), F32),
        shape((8, p.wl), F32),
        shape((rows, p.wt), F32),
        shape((rows, p.wl), F32),
    ]
    scratch = [
        pltpu.VMEM((nb, 2, padded_t, p.ht), BF16),
        pltpu.VMEM((nb, 2, padded_t, p.ht), BF16),
        pltpu.VMEM((rows, p.wt), F32),
        pltpu.VMEM((rows, p.wl), F32),
        pltpu.VMEM((nb, rows, p.ht), BF16),
        pltpu.VMEM((nb, rows, p.ht), F32),
        pltpu.VMEM((nb, rows, p.hl), BF16),
        pltpu.VMEM((nb, rows, p.hl), F32),
        pltpu.SemaphoreType.DMA((nb,)),
        pltpu.SemaphoreType.DMA,
    ]
    args = (me2, w_lay, h_t, h_l, bin_t, bin_l, spread_t, *rest_in, *pieces)
    return kernel_call(
        body, outs, [SM] + [VM] * 16 + [ANY] * 4, [ANY, ANY] + [VM] * 12, scratch, args
    )


def store_slots(p, staged, slot_of, my_dp, sem, slices):
    for z in range(p.far):
        for y in range(2):
            at = (z * 2 + y) ^ my_dp
            for dst, per, begin, count, off in slices:
                pltpu.make_async_copy(
                    staged.at[pl.ds(pl.multiple_of(at * per + begin, 16), count)],
                    slot_of(dst, y, z).at[pl.ds(off, count)],
                    sem,
                ).start()


def feed_backward(p, me2, f_all, w_lay, h_t, h_l, df_t, df_l, g_t, gp_t, g_l, gp_l, spread_t, prev):
    n_t, rows = p.n_t, p.rows
    padded_t = p.n_dp * p.ra
    exact_t = p.ra == p.d_own
    nb = n_t // 2

    def body(*refs):
        (me_ref, f_any, wl, ht, hl, dft, dfl, gt, gpt, gl, gpl, spt), refs = refs[:12], refs[12:]
        (pt, pl_, drt, drl, n1t, i1t, n1l, i1l, vt, vl), refs = refs[:10], refs[10:]
        outs, scratch = refs[:11], refs[11:]
        low, high, gfl, dbt, dbl = outs[:5]
        f_in, staged, acc_t, acc_l, sem_in, sem_out = scratch
        my_dp, my_t = me_ref[0], me_ref[1]
        for k in range(nb):
            pltpu.make_async_copy(f_any.at[k], f_in.at[k], sem_in.at[k]).start()
        dfT, hT = dft[...].T, ht[...].T
        dfTl, hTl = dfl[...].T, hl[...].T
        acc_t[...] = pt[...]
        acc_l[...] = pl_[...]
        for k in range(nb):
            wait_for(f_in.at[k], sem_in.at[k])
            du = dot(dft[...], f_in[k, 1]) * gpt[k].astype(F32)
            dbt[k] = col_sum(du)
            du_low = du.astype(BF16)
            grads = (dot(hT, du_low).astype(BF16), dot(dfT, gt[k]).astype(BF16))
            for m in range(2):
                value = grads[m]
                if not exact_t:
                    value = dot(spt[...], value, 0, 0).astype(BF16)
                staged[k, m] = value
                if m == 0:
                    store_slots(p, staged.at[k, m], lambda d, y, z: low.at[k, y, z], my_dp, sem_out, [(0, p.ra, 0, p.ra, 0)])
                else:
                    store_slots(p, staged.at[k, m], lambda d, y, z: high.at[y, k, z], my_dp, sem_out, [(0, p.ra, 0, p.ra, 0)])
            acc_t[...] += dot(du_low, f_in[k, 0], 1, 1)
            w = wl[k]
            up = w[:, 4 * p.cl : 4 * p.cl + p.hl]
            down = w[:, 4 * p.cl + p.hl : p.lay_cols]
            du = dot(dfl[...], down) * gpl[k].astype(F32)
            dbl[k] = col_sum(du)
            du_low = du.astype(BF16)
            gfl[k, :, pl.ds(0, p.hl)] = dot(hTl, du_low).astype(BF16)
            gfl[k, :, pl.ds(p.hl, p.hl)] = dot(dfTl, gl[k]).astype(BF16)
            acc_l[...] += dot(du_low, up, 1, 1)
        dr1t, dr1l, dat, dal, gvt, gvl = outs[5:]
        for dr, acc, n1, i1, vec, o, low_o, gv in (
            (drt, acc_t, n1t, i1t, vt, dr1t, dat, gvt),
            (drl, acc_l, n1l, i1l, vl, dr1l, dal, gvl),
        ):
            dh = dr[...] + acc[...]
            n = n1[...]
            dr1 = norm_back(dh, n, i1[...], vec[3:4])
            o[...] = dr1
            low_o[...] = dr1.astype(BF16)
            gv[...] = jnp.zeros_like(gv)
            gv[2:3] = col_sum(dr1)
            gv[3:4] = col_sum(dh * n)
            gv[4:5] = col_sum(dh)
        wait_for(staged, sem_out)

    outs = [
        shape((2, 2, p.far, p.ra, p.ht), BF16),
        shape((2, 2, p.far, p.ra, p.ht), BF16),
        shape((nb, p.wl, 2 * p.hl), BF16),
        shape((nb, 1, p.ht), F32),
        shape((nb, 1, p.hl), F32),
    ]
    args = [me2, f_all, w_lay, h_t, h_l, df_t, df_l, g_t, gp_t, g_l, gp_l, spread_t]
    args += list(prev)
    outs += [
        shape((rows, p.wt), F32),
        shape((rows, p.wl), F32),
        shape((rows, p.wt), BF16),
        shape((rows, p.wl), BF16),
        shape((8, p.wt), F32),
        shape((8, p.wl), F32),
    ]
    scratch = [
        pltpu.VMEM((nb, 2, p.wt, p.ht), BF16),
        pltpu.VMEM((nb, 2, padded_t, p.ht), BF16),
        pltpu.VMEM((rows, p.wt), F32),
        pltpu.VMEM((rows, p.wl), F32),
        pltpu.SemaphoreType.DMA((nb,)),
        pltpu.SemaphoreType.DMA,
    ]
    specs = [SM, ANY] + [VM] * (len(args) - 2)
    return kernel_call(
        body, outs, specs, [ANY, ANY] + [VM] * (len(outs) - 2), scratch, args
    )


def attend_backward(p, me2, xs, cores, x_low, lay_low, ints, ints_t, da_t, da_l, spread_t, spread_l, prev, last):
    n_t, rows, hw, nh = p.n_t, p.rows, p.hw, p.heads
    padded_t, padded_l = p.n_dp * p.ra, p.n_dp * p.rl
    exact_t = p.ra == p.d_own
    nb = len(xs)
    n_prev, n_core = len(prev), len(cores)

    def body(*refs):
        (me_ref, xl, ll, ir, itr, dat, dal, spt, spl), refs = refs[:9], refs[9:]
        core_refs = [refs[6 * c : 6 * c + 6] for c in range(n_core)]
        refs = refs[6 * n_core :]
        prev_refs, refs = refs[:n_prev], refs[n_prev:]
        n_out = 2 * n_core + 4
        outs, scratch = refs[:n_out], refs[n_out:]
        slot_refs = [outs[2 * c : 2 * c + 2] for c in range(n_core)]
        gb_t, gb_l, out_a, out_b = outs[2 * n_core :]
        (w_in, staged, staged_l, acc_t, acc_l, dctx, ctx_s, ctx_l, dp_t, dp_l, bin_rows, sem_in,
         sem_out, sem_bin) = scratch
        my_dp, my_t = me_ref[0], me_ref[1]
        for k, (c, x) in enumerate(xs):
            pltpu.make_async_copy(core_refs[c][0].at[x], w_in.at[k], sem_in.at[k]).start()
        xT, lT = xl[...].T, ll[...].T
        daT, dalT = dat[...].T, dal[...].T
        seg_col, seg_row = ir[:, 0:1], itr[0:1, :]
        if prev:
            acc_t[...] = prev_refs[0][...]
            acc_l[...] = prev_refs[1][...]
        else:
            acc_t[...] = jnp.zeros_like(acc_t)
            acc_l[...] = jnp.zeros_like(acc_l)
        ones = jnp.ones((16, rows), BF16)
        for k, (c, x) in enumerate(xs):
            _, wl_ref, qkv_r, ctx_r, lse_r, gfl_r = core_refs[c]
            low, high = slot_refs[c]
            at_k = sum(1 for d, _ in xs[:k] if d == c)
            wait_for(w_in.at[k], sem_in.at[k])
            w = w_in[k]
            wl = wl_ref[x]
            d_t = dot(dat[...], w[:, 3 * p.ct :]).T
            d_l = dot(dal[...], wl[:, 3 * p.cl : 4 * p.cl]).T
            for h in range(nh):
                dctx[h, pl.ds(0, HD)] = d_t[h * HD : (h + 1) * HD].astype(BF16)
                dctx[h, pl.ds(HD, LHD)] = d_l[h * LHD : (h + 1) * LHD].astype(BF16)
                ctx_s[pl.ds(h * HD, HD)] = ctx_r[x, h, pl.ds(0, HD)]
                ctx_l[pl.ds(h * LHD, LHD)] = ctx_r[x, h, pl.ds(HD, LHD)]

            for h in range(nh):
                q, key, val = qkv_r[x, h], qkv_r[x, nh + h], qkv_r[x, 2 * nh + h]
                dc = dctx[h]
                scores = dot(key, q, 0, 0)
                probs = jnp.exp(
                    jnp.where(seg_col == seg_row, scores, NEG_FILL) - lse_r[x, pl.ds(h, 1), :]
                )
                low_p = probs.astype(BF16)
                prod = dc.astype(F32) * ctx_r[x, h].astype(F32)
                sum_lay = jnp.sum(prod[HD:], axis=0, keepdims=True)
                sum_all = jnp.sum(prod[:HD], axis=0, keepdims=True) + sum_lay
                dz_all = probs * (dot(val, dc, 0, 0) - sum_all)
                dz_lay = probs * (dot(val[HD:], dc[HD:], 0, 0) - sum_lay)
                ds_t, ds_l = dz_all.astype(BF16), dz_lay.astype(BF16)
                dv = dot(dc, low_p, 1, 1)
                dq_t = dot(key[:HD], ds_t) * (1.0 / math.sqrt(HD))
                dq_l = dot(key[HD:], ds_l) * (1.0 / math.sqrt(LHD))
                dk_t = dot(q[:HD], ds_t, 1, 1)
                dk_l = dot(q[HD:], ds_l, 1, 1)
                for m, (top, bot) in enumerate(((dq_t, dq_l), (dk_t, dk_l), (dv[:HD], dv[HD:]))):
                    dp_t[pl.ds(m * p.ct + h * HD, HD)] = top.astype(BF16)
                    dp_l[pl.ds(m * p.cl + h * LHD, LHD)] = bot.astype(BF16)
            gb_t[k] = dot(ones, dp_t[...], 1, 1)[:8]
            gb_l[k] = dot(ones, dp_l[...], 1, 1)[:8]
            acc_t[...] += dot(w[:, : 3 * p.ct], dp_t[...])
            acc_l[...] += dot(wl[:, : 3 * p.cl], dp_l[...])
            grad = jnp.concatenate(
                [dot(xT, dp_t[...], 1, 1), dot(daT, ctx_s[...], 1, 1)], axis=1
            ).astype(BF16)
            if not exact_t:
                grad = dot(spt[...], grad, 0, 0).astype(BF16)
            staged[k] = grad
            fill = p.cols - p.lay_cols
            grad_l = jnp.concatenate(
                [
                    dot(lT, dp_l[...], 1, 1),
                    dot(dalT, ctx_l[...], 1, 1),
                    gfl_r[x].astype(F32),
                    jnp.zeros((p.wl, fill), F32),
                ],
                axis=1,
            ).astype(BF16)
            staged_l[k] = dot(spl[...], grad_l, 0, 0).astype(BF16)
            rest = p.ra - p.half_a
            slot = lambda d, y, z: high.at[y, at_k, z] if d else low.at[at_k, y, z]
            slices = [(0, p.ra, 0, p.half_a, 0)]
            if rest:
                slices.append((1, p.ra, p.half_a, rest, 0))
            store_slots(p, staged.at[k], slot, my_dp, sem_out.at[0], slices)
            store_slots(p, staged_l.at[k], slot, my_dp, sem_out.at[1], [(1, p.rl, 0, p.rl, rest)])
        if last:
            gt = prev_refs[2][...] + acc_t[...].T
            gl = prev_refs[3][...] + acc_l[...].T
            out_a[:, pl.ds(0, p.wt)] = gt.astype(BF16)
            out_a[:, pl.ds(p.wt, p.wl)] = gl.astype(BF16)
            half = p.wl // 2
            bins = bin_rows.shape[0]
            levels = lax.broadcasted_iota(jnp.int32, (bins, 1), 0).astype(F32)
            for m in range(2):
                row = itr[1 + 2 * m : 2 + 2 * m, :] * 128.0 + itr[2 + 2 * m : 3 + 2 * m, :]
                hot = (levels == row).astype(F32).astype(BF16)
                part = gl[:, m * half : (m + 1) * half]
                top = part.astype(BF16)
                rest_part = (part - top.astype(F32)).astype(BF16)
                both = dot(hot, jnp.concatenate([top, rest_part], axis=1))
                bin_rows[:, pl.ds(m * half, half)] = (both[:, :half] + both[:, half:]).astype(BF16)
            if p.per % 16:
                pltpu.make_async_copy(bin_rows, out_b, sem_bin).start()
            else:
                for r in range(p.total):
                    z, y, x, c = r // 8, (r // 4) % 2, (r // 2) % 2, r % 2
                    at = ((r // n_t) ^ my_dp) * n_t + ((r % n_t) ^ my_t)
                    pltpu.make_async_copy(
                        bin_rows.at[pl.ds(pl.multiple_of(at * p.per, 16), p.per)],
                        out_b.at[c, y, x, z],
                        sem_bin,
                    ).start()
            wait_for(bin_rows, sem_bin)
        else:
            out_a[...] = acc_t[...]
            out_b[...] = acc_l[...]
        wait_for(staged, sem_out.at[0])
        wait_for(staged_l, sem_out.at[1])

    half_b = p.ra + p.rl - p.half_a
    slots_out = []
    for c in range(n_core):
        held = sum(1 for d, _ in xs if d == c)
        slots_out += [
            shape((held, 2, p.far, p.half_a, p.cols), BF16),
            shape((2, held, p.far, half_b, p.cols), BF16),
        ]
    outs = slots_out + [
        shape((nb, 8, 3 * p.ct), F32),
        shape((nb, 8, 3 * p.cl), F32),
    ]
    args = [me2, x_low, lay_low, ints, ints_t, da_t, da_l, spread_t, spread_l]
    specs = [SM] + [VM] * 8 + ([ANY] + [VM] * 5) * n_core + [VM] * n_prev
    args += [member for core in cores for member in core] + list(prev)
    if last:
        bins = p.per * p.total
        slots = (bins,) if p.per % 16 else (2, 2, 2, p.far, p.per)
        outs += [shape((rows, p.wt + p.wl), BF16), shape((*slots, p.wl), BF16)]
    else:
        outs += [shape((p.wt, rows), F32), shape((p.wl, rows), F32)]
    scratch = [
        pltpu.VMEM((nb, p.wt, p.cols), BF16),
        pltpu.VMEM((nb, padded_t, p.cols), BF16),
        pltpu.VMEM((nb, padded_l, p.cols), BF16),
        pltpu.VMEM((p.wt, rows), F32),
        pltpu.VMEM((p.wl, rows), F32),
        pltpu.VMEM((nh, hw, rows), BF16),
        pltpu.VMEM((p.ct, rows), BF16),
        pltpu.VMEM((p.cl, rows), BF16),
        pltpu.VMEM((3 * p.ct, rows), BF16),
        pltpu.VMEM((3 * p.cl, rows), BF16),
        pltpu.VMEM((p.per * p.total, p.wl), BF16),
        pltpu.SemaphoreType.DMA((nb,)),
        pltpu.SemaphoreType.DMA((2,)),
        pltpu.SemaphoreType.DMA,
    ]
    out_specs = [ANY] * (2 * n_core) + [VM] * 3 + [ANY if last else VM]
    return kernel_call(body, outs, specs, out_specs, scratch, args)


def tie(*groups):
    leaves, tree = jax.tree.flatten(groups)
    return jax.tree.unflatten(tree, lax.optimization_barrier(leaves))


def after(values, *others):
    return tie(values, *others)[0]


def line_of(shard, total):
    return [shard] + [xor_send(shard, total, 8 * r) for r in range(1, total // 8)]


def line_doubled(shard, total, others):
    line = [shard]
    while 8 * len(line) < total:
        held = jnp.stack(line)
        if len(line) > 1:
            held = after(held, others)
        theirs = xor_send(held, total, 8 * len(line))
        line = line + [theirs[z] for z in range(len(line))]
    return line


def halves_of(line, half):
    low = jnp.stack([member[:half] for member in line])
    high = jnp.stack([member[half:] for member in line])
    return low, high


def add_low(mine, theirs):
    return to_low(mine.astype(F32) + theirs.astype(F32))


def reduce_second(mine, got):
    send = [add_low(mine[k][1], got[k][1]) for k in range(2)]
    keep = [add_low(mine[k][0], got[k][0]) for k in range(2)]
    return send, keep


def reduce_line_parts(keep, got):
    return [
        jnp.concatenate([add_low(keep[k][z], got[k][z]) for k in range(2)], axis=0)
        for z in range(keep[0].shape[0])
    ]


def send_line(line, total):
    return line[:1] + [xor_send(line[z], total, 8 * z) for z in range(1, len(line))]


def add_line(line):
    out = line[0].astype(F32)
    for member in line[1:]:
        out = out + member.astype(F32)
    return out


def update_all(factor, matrices, flat, grads):
    states = [member for group in (*matrices, *flat) for member in group]

    def body(*refs):
        factor_ref, grads = refs[0], refs[1:7]
        ins, outs = refs[7:25], refs[25:]
        scale = factor_ref[0, 0]
        for k in range(6):
            w, m, v = (ins[3 * k + j][...] for j in range(3))
            results = adamw_step(
                w, m, v, grads[k][...] * scale, WEIGHT_DECAY if k < 4 else 0.0, LEARN_RATES[k]
            )
            for j in range(3):
                outs[3 * k + j][...] = results[j]

    return list(
        kernel_call(
            body,
            [shape(v.shape, F32) for v in states],
            [SM] + [VM] * 24,
            [VM] * 18,
            [],
            (factor.reshape(1, 1), *grads, *states),
        )
    )


def relative(blocks, me):
    total = blocks.shape[0]
    step = 1
    while step < total:
        pairs = blocks.reshape(total // (2 * step), 2, step, *blocks.shape[1:])
        swapped = jnp.stack([pairs[:, 1], pairs[:, 0]], axis=1)
        blocks = jnp.where((me // step) % 2 == 0, pairs, swapped).reshape(blocks.shape)
        step = step * 2
    return blocks


def on_device(
    text_in,
    layout_in,
    segment_ids,
    box_bins,
    text_cot,
    layout_cot,
    attend_text,
    attend_text_mean,
    attend_text_square,
    feed_text,
    feed_text_mean,
    feed_text_square,
    attend_layout,
    attend_layout_mean,
    attend_layout_square,
    feed_layout,
    feed_layout_mean,
    feed_layout_square,
    vectors,
    vectors_mean,
    vectors_square,
    tables,
    tables_mean,
    tables_square,
):
    n_dp, n_t = lax.axis_size("dp"), lax.axis_size("tensor")
    total = n_dp * n_t
    t_pos = lax.axis_index("tensor")
    pages, quarter, wt = text_in.shape
    wl = layout_in.shape[1] // quarter
    d_own, dl_own = attend_text.shape[0], attend_layout.shape[0]
    ct, cl = attend_text.shape[2], attend_layout.shape[2]
    ht, hl = feed_text.shape[2], feed_layout.shape[2]


    p = Plan(n_dp, n_t, quarter, wt, wl, ct, cl, ht, hl, tables.shape[0] // wl)
    me = lax.axis_index("dp") * n_t + t_pos
    me2 = jnp.stack([lax.axis_index("dp"), t_pos]).astype(jnp.int32)
    lay_cols = p.lay_cols

    def pad_rows(values, count):
        return jnp.pad(values, ((0, count - values.shape[0]), (0, 0)))

    lay_pack = jnp.concatenate(
        [
            to_low(attend_layout).reshape(dl_own, 4 * cl),
            to_low(feed_layout).reshape(dl_own, 2 * hl),
        ],
        axis=1,
    )
    lay_pack = jnp.pad(lay_pack, ((0, p.rl - dl_own), (0, p.cols - lay_cols)))
    attend_pack = jnp.concatenate(
        [pad_rows(to_low(attend_text).reshape(d_own, p.cols), p.ra), lay_pack]
    )
    low_feed = to_low(feed_text)
    feed_pack = jnp.concatenate(
        [pad_rows(low_feed[:, 0], p.ra), pad_rows(low_feed[:, 1], p.ra)]
    )
    bins = box_bins.reshape(pages, quarter, 2)
    digits = jnp.stack(
        [segment_ids, bins[..., 0] // 128, bins[..., 0] % 128, bins[..., 1] // 128, bins[..., 1] % 128],
        axis=-1,
    )
    packed_in = jnp.concatenate(
        [
            text_in,
            layout_in.reshape(pages, quarter, wl),
            jnp.pad(to_low(digits), ((0, 0), (0, 0), (0, 59))),
        ],
        axis=2,
    )
    packed_cot = jnp.concatenate([text_cot, layout_cot.reshape(pages, quarter, wl)], axis=2)

    def page_of(values):
        take = lambda r: lax.dynamic_index_in_dim(values, t_pos ^ r, 0, keepdims=False)
        return [take(0)] + [xor_send(take(r), total, r) for r in range(1, n_t)]

    def send_rows(page):
        blocks = page.reshape(n_t, quarter, page.shape[-1])
        return [blocks[0]] + [xor_send(blocks[r], total, r) for r in range(1, n_t)]

    def pages_of(blocks):
        out = jnp.zeros((n_t,) + blocks[0].shape, blocks[0].dtype)
        for r in range(n_t):
            out = lax.dynamic_update_slice(out, blocks[r][None], (t_pos ^ r, 0, 0))
        return out

    send = lambda values, distance: xor_send(values, total, distance)

    line_a = line_of(attend_pack, total)
    xin = page_of(packed_in)
    low, high = halves_of(line_a, p.half_a)
    low, high = after((low, high), xin)
    line_f = line_doubled(feed_pack, total, line_a)
    low0, high0 = jnp.stack([low, send(low, 2)]), jnp.stack([high, send(high, 4)])
    low4, high2 = send(low0, 4), send(high0, 2)
    low1, high1 = send(low0, 1), send(high0, 1)
    late_vectors, late_tables = after((vectors, tables), low0, high0)
    parts = split_vectors(late_vectors, [wt, wl], [n_t * ht, n_t * hl])
    biases, vecs, bins_in = [], [], []
    for s, width in ((0, ct), (1, cl)):
        vec, hidden = parts[s]
        biases.append(
            jnp.concatenate(
                [
                    vec[0].reshape(n_t, 1, width),
                    jnp.zeros((n_t, 1, width), F32),
                    vec[1].reshape(n_t, 1, width),
                ],
                axis=2,
            )
        )
        vecs.append(jnp.stack(vec))
        bins_in.append(hidden.reshape(n_t, 1, -1))
    table_rows = to_low(late_tables.reshape(-1, wl))
    spread_t = p.spread(d_own, p.ra) if p.ra != d_own else jnp.zeros((16, 128), BF16)
    spread_l = p.spread(dl_own, p.rl)

    flow, fhigh = halves_of(after(line_f, low0, high0), p.ra)
    flow, fhigh = after((flow, fhigh), low4, high2)
    att_fix = (biases[0], biases[1], vecs[0], vecs[1], spread_t, spread_l)
    low5, high3 = send(low4, 1), send(high2, 1)
    flow_x, fhigh_y = send(flow, 2), send(fhigh, 4)
    (w_all0, w_lay0, qkv0, ctx0, lse0, *row_state) = attend_forward(
        p, me2, 0, (*xin, table_rows), *att_fix, [low0, low4, high0, high2]
    )
    row_state, qkv0, low5, high3, low1, high1, flow_x, fhigh_y = tie(
        row_state, qkv0, low5, high3, low1, high1, flow_x, fhigh_y
    )
    flow0, fhigh0 = jnp.stack([flow, flow_x]), jnp.stack([fhigh, fhigh_y])
    row_state = after(row_state, flow0, fhigh0)
    flow4, fhigh2 = send(flow0, 4), send(fhigh0, 2)
    flow1, fhigh1 = send(flow0, 1), send(fhigh0, 1)
    (w_all1, w_lay1, qkv1, ctx1, lse1, n1t, i1t, h_t, n1l, i1l, h_l) = attend_forward(
        p, me2, 1, row_state, *att_fix, [low1, low5, high1, high3]
    )
    x_low, lay_low, _, ints, ints_t = row_state[:5]
    n1t, n1l, h_t, h_l, w_lay1, flow4, fhigh2, packed_cot = tie(
        n1t, n1l, h_t, h_l, w_lay1, flow4, fhigh2, packed_cot
    )
    flow5, fhigh3 = send(flow4, 1), send(fhigh2, 1)
    cots = page_of(packed_cot)
    (f_all0, g_t0, gp_t0, g_l0, gp_l0, acc_t, acc_l) = feed_forward(
        p, me2, [flow0, flow4, fhigh0, fhigh2], w_lay0, h_t, h_l, bins_in[0], bins_in[1], spread_t
    )
    acc_t, acc_l, f_all0, flow5, fhigh3, flow1, fhigh1, cots = tie(
        acc_t, acc_l, f_all0, flow5, fhigh3, flow1, fhigh1, cots
    )
    (gf_low1, gf_high1, gfl1, dbt1, dbl1, out_rows, dr_t, dr_l, df_t, df_l, gv2t, gv2l, acc_t, acc_l) = feed_middle(
        p, me2, [flow1, flow5, fhigh1, fhigh3], w_lay1, h_t, h_l, bins_in[0], bins_in[1], spread_t,
        (acc_t, acc_l, n1t, n1l, *cots, vecs[0], vecs[1]),
    )
    rows_out = send_rows(out_rows)
    got = [send(gf_low1, 1), send(gf_high1, 1)]
    (gf_low0, gf_high0, gfl0, dbt0, dbl0, dr1t, dr1l, da_t, da_l, gv1t, gv1l) = feed_backward(
        p, me2, f_all0, w_lay0, h_t, h_l, df_t, df_l, g_t0, gp_t0, g_l0, gp_l0, spread_t,
        (acc_t, acc_l, dr_t, dr_l, n1t, i1t, n1l, i1l, vecs[0], vecs[1])
    )
    got, rows_out, gf_low0, gf_high0, gfl0, dbt0, dbl0, dr1t, dr1l, da_t, da_l, gv1t, gv1l = tie(
        got, rows_out, gf_low0, gf_high0, gfl0, dbt0, dbl0, dr1t, dr1l, da_t, da_l, gv1t, gv1l
    )
    next_f, keep_f = reduce_second((gf_low0, gf_high0), got)
    da_t = after(da_t, next_f)
    got_f = [send(next_f[0], 2), send(next_f[1], 4)]
    att_args = (x_low, lay_low, ints, ints_t, da_t, da_l, spread_t, spread_l)
    cores = ((w_all0, w_lay0, qkv0, ctx0, lse0, gfl0), (w_all1, w_lay1, qkv1, ctx1, lse1, gfl1))
    (low_x1, high_x1, ga_low1, ga_high1, gb_t1, gb_l1, acc_t, acc_l) = attend_backward(
        p, me2, ((1, 0), (1, 1), (0, 1)), cores, *att_args, (), False
    )
    got_f, low_x1, high_x1, ga_low1, ga_high1, gb_t1, gb_l1, acc_t, acc_l = tie(
        got_f, low_x1, high_x1, ga_low1, ga_high1, gb_t1, gb_l1, acc_t, acc_l
    )
    next_f, keep_f = reduce_second(keep_f, got_f)
    acc_t = after(acc_t, next_f)
    got = [send(ga_low1, 1), send(ga_high1, 1)]
    got_f = [send(next_f[0], 4), send(next_f[1], 2)]
    (low_x0, high_x0, gb_t00, gb_l00, grad_rows, table_grad) = attend_backward(
        p, me2, ((0, 0),), cores[:1], *att_args, (acc_t, acc_l, dr1t, dr1l), True
    )
    got, got_f, low_x0, high_x0, gb_t00, gb_l00, grad_rows, table_grad = tie(
        got, got_f, low_x0, high_x0, gb_t00, gb_l00, grad_rows, table_grad
    )
    if p.per % 16:
        table_grad = relative(table_grad.reshape(total, p.per, wl), me)
        table_grad = table_grad.reshape(p.far, 2, 2, 2, p.per, wl).transpose(3, 1, 2, 0, 4, 5)
    table_got = send(table_grad[1], 1)
    low_x1 = add_low(low_x1[0], got[0][1])
    got_low = send(low_x1, 2)
    rest = p.ra - p.half_a
    spare = high_x0.shape[-2] - rest - p.per
    edges = ((0, 0), (0, 0), (0, 0), (rest, spare), (lay_cols, p.cols - lay_cols - wl))
    table_sum = jnp.pad(add_low(table_grad[0], after(table_got, low_x1)), edges)
    both = [jnp.concatenate([high_x0[y], high_x1[y]]) for y in range(2)]
    next_high = to_low(both[1].astype(F32) + got[1][1].astype(F32) + table_sum[1].astype(F32))
    got_high = send(next_high, 4)
    line_f = send_line(reduce_line_parts(keep_f, after(got_f, next_high)), total)
    low = to_low(low_x0[0].astype(F32) + got[0][0].astype(F32) + got_low.astype(F32))
    got_low = send(low[1], 4)
    high = to_low(
        both[0].astype(F32)
        + got[1][0].astype(F32)
        + table_sum[0].astype(F32)
        + got_high.astype(F32)
    )
    got_high = send(high[1], 2)
    pieces = (gb_t1, gb_l1, gb_t00, gb_l00, dbt0, dbt1, dbl0, dbl1, gv1t, gv1l, gv2t, gv2l)
    (gb_t1, gb_l1, gb_t00, gb_l00, dbt0, dbt1, dbl0, dbl1, gv1t, gv1l, gv2t, gv2l) = after(
        pieces, next_high
    )
    gb_t0 = jnp.concatenate([gb_t00, gb_t1[2:]])
    gb_l0 = jnp.concatenate([gb_l00, gb_l1[2:]])
    feed_sum = add_line(after(line_f, low, high))
    line_a = reduce_line_parts((low[0], high[0]), (got_low, got_high))
    rows_out, grad_rows = after((rows_out, grad_rows), line_a)
    line_a = send_line(line_a, total)
    rows_grad = send_rows(grad_rows)
    feed_sum = after(feed_sum, line_a[1])
    rows_out, rows_grad = pages_of(rows_out), pages_of(rows_grad)
    row_outputs = (
        rows_out[:, :, :wt],
        rows_out[:, :, wt:].reshape(pages, quarter * wl),
        rows_grad[:, :, :wt].astype(F32),
        rows_grad[:, :, wt:].astype(F32).reshape(pages, quarter * wl),
    )
    attend_sum = add_line(after(line_a, row_outputs[:2]))

    def by_block(odd, even):
        both = jnp.stack([even[0], odd[0], even[1], odd[1]]).reshape(n_t, -1)
        order = jnp.arange(n_t) ^ t_pos
        hot = order[:, None] == jnp.arange(n_t)[None, :]
        return jnp.sum(jnp.where(hot[:, :, None], both[None], 0.0), axis=1).reshape(-1)

    gv_t, gv_l = gv2t + gv1t, gv2l + gv1l
    vector_grad = jnp.concatenate(
        [
            by_block(gb_t1[:, 0, : ct], gb_t0[:, 0, : ct]),
            by_block(gb_t1[:, 0, 2 * ct :], gb_t0[:, 0, 2 * ct :]),
            gv_t[2:].reshape(-1),
            by_block(dbt1, dbt0),
            by_block(gb_l1[:, 0, : cl], gb_l0[:, 0, : cl]),
            by_block(gb_l1[:, 0, 2 * cl :], gb_l0[:, 0, 2 * cl :]),
            gv_l[2:].reshape(-1),
            by_block(dbl1, dbl0),
        ]
    )
    own_sq = jnp.sum(feed_sum * feed_sum) + jnp.sum(attend_sum * attend_sum)
    n_vec = vector_grad.shape[0]
    summed = jnp.pad(vector_grad, (0, round_up(n_vec + 1, 1024) - n_vec)).reshape(-1, 128)
    spot = (lax.broadcasted_iota(jnp.int32, summed.shape, 0) == n_vec // 128) & (
        lax.broadcasted_iota(jnp.int32, summed.shape, 1) == n_vec % 128
    )
    summed = jnp.where(spot, own_sq, summed)
    spread_table = to_low(attend_sum[p.ra : p.ra + p.per, lay_cols : lay_cols + wl])
    distance = total // 2
    while distance:
        other = send(summed, distance)
        theirs = send(after(spread_table, summed), distance)
        summed = summed + other
        bit = (me // distance) % 2
        spread_table = jnp.where(
            bit == 0, jnp.stack([spread_table, theirs]), jnp.stack([theirs, spread_table])
        )
        distance = distance // 2
    deep = spread_table.ndim - 2
    order = tuple(range(deep - 1, -1, -1)) + (deep, deep + 1)
    table_grad = spread_table.transpose(order).reshape(-1, 128).astype(F32)
    vector_grad = summed
    all_sq = jnp.sum(jnp.where(spot, 0.0, summed * summed))
    shared_sq = all_sq + summed[n_vec // 128, n_vec % 128]
    clip_norm = jnp.sqrt(shared_sq)
    factor = jnp.minimum(1.0, CLIP_NORM / (clip_norm + 1e-06))
    flat = [
        [v.reshape(-1, 128) for v in group]
        for group in ((vectors, vectors_mean, vectors_square), (tables, tables_mean, tables_square))
    ]
    lay_sum = attend_sum[p.ra : p.ra + dl_own]
    grads = (
        attend_sum[:d_own].reshape(d_own, 4, ct),
        jnp.stack([feed_sum[:d_own], feed_sum[p.ra : p.ra + d_own]], axis=1),
        lay_sum[:, : 4 * cl].reshape(dl_own, 4, cl),
        lay_sum[:, 4 * cl : lay_cols].reshape(dl_own, 2, hl),
        vector_grad[: n_vec // 128],
        table_grad,
    )
    matrices = (
        (attend_text, attend_text_mean, attend_text_square),
        (feed_text, feed_text_mean, feed_text_square),
        (attend_layout, attend_layout_mean, attend_layout_square),
        (feed_layout, feed_layout_mean, feed_layout_square),
    )
    updated = update_all(factor, matrices, flat, grads)
    updated[12:] = [v.reshape(-1) for v in updated[12:]]
    return (
        *row_outputs,
        *updated,
        clip_norm,
    )


def solution(mesh):
    rows3, rows2, cols3 = P("dp", "tensor", None), P("dp", "tensor"), P("dp", None, "tensor")
    in_specs = (rows3, rows2, rows2, rows2, rows3, rows2) + (cols3,) * 12 + (P(),) * 6
    out_specs = (rows3, rows2, rows3, rows2) + (cols3,) * 12 + (P(),) * 7
    return jax.shard_map(
        on_device, mesh=mesh, in_specs=in_specs, out_specs=out_specs, check_vma=False
    )
```

```python
import functools
import math

import jax
import jax.numpy as jnp
from jax import lax
from jax.experimental import pallas as pl
from jax.experimental.pallas import tpu as pltpu
from jax.sharding import PartitionSpec as P

HD = 64
LHD = 16
STEP = 10

NORM_EPS = 1e-05
NEG_FILL = -1000000000.0
CLIP_NORM = 1.0
LEARN_RATES = (0.3, 0.05, 0.3, 0.05, 0.3, 0.3)
BETA_ONE = 0.9
BETA_TWO = 0.999
ADAM_EPS = 1e-08
WEIGHT_DECAY = 0.01
AXES = ("dp", "tensor")
LAY_ROWS = 32
F32 = jnp.float32
BF16 = jnp.bfloat16


def to_low(values):
    return values.astype(BF16)


def xor_send(values, total, distance):
    return lax.ppermute(values, AXES, [(i, i ^ distance) for i in range(total)])


def split_vectors(packed, widths, hidden):
    result = []
    offset = 0
    for stream in range(2):
        width_now = widths[stream]
        pieces = [packed[offset + k * width_now : offset + (k + 1) * width_now] for k in range(8)]
        offset = offset + 8 * width_now
        result.append((pieces, packed[offset : offset + hidden[stream]]))
        offset = offset + hidden[stream]
    return result


def adamw_step(weight, moment, square, gradient, decay_rate, rate_now):
    new_moment = BETA_ONE * moment + (1.0 - BETA_ONE) * gradient
    new_square = BETA_TWO * square + (1.0 - BETA_TWO) * gradient * gradient
    moment_hat = new_moment / (1.0 - BETA_ONE**STEP)
    square_hat = new_square / (1.0 - BETA_TWO**STEP)
    new_weight = weight - rate_now * (
        moment_hat / (jnp.sqrt(square_hat) + ADAM_EPS) + decay_rate * weight
    )
    return (new_weight, new_moment, new_square)


def lane_mean(values):
    return jnp.sum(values, axis=-1, keepdims=True) * (1.0 / values.shape[-1])


def norm_parts(residual):
    centered = residual - lane_mean(residual)
    inv_std = lax.rsqrt(lane_mean(centered * centered) + NORM_EPS)
    return centered * inv_std, inv_std


def norm_back(gradient, normed, inv_std, gain_vec):
    scaled = gradient * gain_vec
    d_resid = inv_std * (
        scaled - lane_mean(scaled) - normed * lane_mean(scaled * normed)
    )
    return d_resid


def col_sum(values):
    return jnp.sum(values, axis=0, keepdims=True)


def dot(a, b, da=1, db=0):
    return lax.dot_general(a, b, (((da,), (db,)), ((), ())), preferred_element_type=F32)


def round_up(count, step):
    return -(-count // step) * step


class Plan:
    def __init__(self, n_dp, n_t, quarter, wt, wl, ct, cl, ht, hl, bins):
        self.n_dp, self.n_t, self.total = n_dp, n_t, n_dp * n_t
        self.far = self.total // 8
        self.quarter, self.rows = quarter, quarter * n_t
        self.wt, self.wl, self.ct, self.cl, self.ht, self.hl = wt, wl, ct, cl, ht, hl
        self.d_own, self.dl_own = wt // n_dp, wl // n_dp
        self.ra, self.rl = round_up(self.d_own, 16), round_up(self.dl_own, 16)
        self.cols = 4 * ct
        self.half_a = (self.ra + self.rl) // 2
        self.heads = ct // HD
        self.hw = HD + LHD
        self.lay_cols = 4 * cl + 2 * hl
        self.per = bins // self.total

    def spread(self, own, padded):
        out = jnp.arange(own * self.n_dp, dtype=jnp.int32)
        place = (out // own) * padded + out % own
        return (place[:, None] == jnp.arange(padded * self.n_dp, dtype=jnp.int32)[None]).astype(BF16)


VMEM_LIMIT = 60 * 2**20
COST = 10 * 10**9
ANY = pl.BlockSpec(memory_space=pl.ANY)
VM = pl.BlockSpec(memory_space=pltpu.VMEM)
SM = pl.BlockSpec(memory_space=pltpu.SMEM)


def kernel_call(body, outs, in_specs, out_specs, scratch, args):
    return pl.pallas_call(
        body,
        out_shape=outs,
        in_specs=in_specs,
        out_specs=out_specs,
        scratch_shapes=scratch,
        compiler_params=pltpu.CompilerParams(vmem_limit_bytes=VMEM_LIMIT),
        cost_estimate=pl.CostEstimate(flops=COST, bytes_accessed=2**20, transcendentals=0),
    )(*args)


def shape(dims, kind):
    return jax.ShapeDtypeStruct(tuple(dims), kind)


def wait_for(ref, sem):
    pltpu.make_async_copy(ref, ref, sem).wait()


def attend_forward(p, me2, blocks, rows_in, bias_t, bias_l, vec_t, vec_l, spread_t, spread_l, pieces):
    rows, hw, nh = p.rows, p.hw, p.heads
    padded_t, padded_l = p.n_dp * p.ra, p.n_dp * p.rl
    exact_t = p.ra == p.d_own
    nb = len(blocks)
    first = nb == 1
    n_piece = len(pieces)
    n_in = len(rows_in)

    def body(*refs):
        (me_ref, bt, bl, vt, vl, spt, spl), refs = refs[:7], refs[7:]
        in_refs, refs = refs[:n_in], refs[n_in:]
        piece_refs, refs = refs[:n_piece], refs[n_piece:]
        n_out = 12 if first else 11
        outs, scratch = refs[:n_out], refs[n_out:]
        wt_out, wl_out, qkv, ctx, lse_ref = outs[:5]
        wpad, lpad, acc_t, acc_l, ctx_rows, ctx_lay, sem_t, sem_l, sem_out = scratch
        my_dp, my_t = me_ref[0], me_ref[1]
        for k, (core, x_at) in enumerate(blocks):
            for y in range(2):
                low, high = piece_refs[4 * core + y].at[x_at], piece_refs[4 * core + 2 + x_at].at[y]
                for z in range(p.far):
                    at = (z * 2 + y) ^ my_dp
                    row = pl.multiple_of(at * p.ra, 16)
                    lrow = pl.multiple_of(at * p.rl, 16)
                    pltpu.make_async_copy(
                        low.at[z], wpad.at[k, pl.ds(row, p.half_a)], sem_t.at[k]
                    ).start()
                    rest = p.ra - p.half_a
                    if rest:
                        pltpu.make_async_copy(
                            high.at[z, pl.ds(0, rest)],
                            wpad.at[k, pl.ds(pl.multiple_of(row + p.half_a, 16), rest)],
                            sem_t.at[k],
                        ).start()
                    pltpu.make_async_copy(
                        high.at[z, pl.ds(rest, p.rl)], lpad.at[k, pl.ds(lrow, p.rl)], sem_l
                    ).start()
        if first:
            x0, x1, x2, x3, tab = in_refs
            xt_ref, lay_low, lay_ref, ints_ref, intst_ref, acc_t_out, acc_l_out = outs[5:]
            for k, ref in enumerate((x0, x1, x2, x3)):
                xt_ref[pl.ds(k * p.quarter, p.quarter), :] = ref[:, : p.wt]
            x = xt_ref[...]
            side = jnp.concatenate([ref[:, p.wt :] for ref in (x0, x1, x2, x3)], axis=0).astype(F32)
            digits = side[:, p.wl : p.wl + 8]
            ints_ref[...] = digits
            intst_ref[...] = digits.T
            half = p.wl // 2
            levels = lax.broadcasted_iota(jnp.int32, (1, tab.shape[0]), 1).astype(F32)
            hot_x = (digits[:, 1:2] * 128.0 + digits[:, 2:3] == levels).astype(F32).astype(BF16)
            hot_y = (digits[:, 3:4] * 128.0 + digits[:, 4:5] == levels).astype(F32).astype(BF16)
            emb = jnp.concatenate([dot(hot_x, tab[:, :half]), dot(hot_y, tab[:, half:])], axis=1)
            lay = side[:, : p.wl] + emb
            low_rows = lay.astype(BF16)
            lay_low[...] = low_rows
            lay_ref[...] = lay
            acc_t[...] = jnp.zeros_like(acc_t)
            acc_l[...] = jnp.zeros_like(acc_l)
        else:
            xt_ref, lay_low, lay_ref, ints_ref, intst_ref, acc_t_in, acc_l_in = in_refs
            n1t, i1t, ht, n1l, i1l, hl = outs[5:]
            x, low_rows = xt_ref[...], lay_low[...]
            acc_t[...] = acc_t_in[...]
            acc_l[...] = acc_l_in[...]
        seg_col = ints_ref[:, 0:1]
        seg_row = intst_ref[0:1, :]
        wait_for(lpad, sem_l)
        for k in range(nb):
            wl_out[k] = dot(spl[...], lpad[k]).astype(BF16)

        def block(k, core, x_at):
            wait_for(wpad.at[k], sem_t.at[k])
            if not exact_t:
                wpad[k, pl.ds(0, p.wt)] = dot(spt[...], wpad[k]).astype(BF16)
            out_copy = pltpu.make_async_copy(wpad.at[k, pl.ds(0, p.wt)], wt_out.at[k], sem_out)
            out_copy.start()
            own_t = (2 * x_at + core) ^ my_t
            w = wpad[k, pl.ds(0, p.wt)]
            wl = wl_out[k]
            raw = (dot(x, w[:, : 3 * p.ct]) + bt[own_t]).T
            raw_l = (dot(low_rows, wl[:, : 3 * p.cl]) + bl[own_t]).T
            for c in range(3):
                for h in range(nh):
                    top = raw[c * p.ct + h * HD : c * p.ct + (h + 1) * HD]
                    bot = raw_l[c * p.cl + h * LHD : c * p.cl + (h + 1) * LHD]
                    top, bot = top.astype(BF16), bot.astype(BF16)
                    if c == 0:
                        top = top * jnp.asarray(1.0 / math.sqrt(HD), BF16)
                        bot = bot * jnp.asarray(1.0 / math.sqrt(LHD), BF16)
                    qkv[k, c * nh + h, pl.ds(0, HD)] = top
                    qkv[k, c * nh + h, pl.ds(HD, LHD)] = bot
            for h in range(nh):
                scores = dot(qkv[k, nh + h], qkv[k, h], 0, 0)
                scores = jnp.where(seg_col == seg_row, scores, NEG_FILL)
                top_score = jnp.max(scores, axis=0, keepdims=True)
                expo = jnp.exp(scores - top_score)
                row_total = jnp.sum(expo, axis=0, keepdims=True)
                probs = (expo * (1.0 / row_total)).astype(BF16)
                mixed = dot(qkv[k, 2 * nh + h], probs).astype(BF16)
                ctx[k, h] = mixed
                ctx_rows[pl.ds(h * HD, HD)] = mixed[:HD]
                ctx_lay[pl.ds(h * LHD, LHD)] = mixed[HD:]
                lse_ref[k, pl.ds(h, 1), :] = top_score + jnp.log(row_total)
            acc_t[...] += dot(w[:, 3 * p.ct :], ctx_rows[...])
            acc_l[...] += dot(wl[:, 3 * p.cl : 4 * p.cl], ctx_lay[...])
            out_copy.wait()

        for k, (core, x_at) in enumerate(blocks):
            block(k, core, x_at)
        if first:
            acc_t_out[...] = acc_t[...]
            acc_l_out[...] = acc_l[...]
        else:
            for residual, acc, vec, n_ref, i_ref, h_ref in (
                (x.astype(F32), acc_t, vt, n1t, i1t, ht),
                (lay_ref[...], acc_l, vl, n1l, i1l, hl),
            ):
                normed, inv = norm_parts(residual + acc[...].T + vec[2:3])
                n_ref[...] = normed
                i_ref[...] = inv
                h_ref[...] = (normed * vec[3:4] + vec[4:5]).astype(BF16)

    outs = [
        shape((nb, p.wt, p.cols), BF16),
        shape((nb, p.wl, p.cols), BF16),
        shape((nb, 3 * nh, hw, rows), BF16),
        shape((nb, nh, hw, rows), BF16),
        shape((nb, 8, rows), F32),
    ]
    if first:
        outs += [
            shape((rows, p.wt), BF16),
            shape((rows, p.wl), BF16),
            shape((rows, p.wl), F32),
            shape((rows, 8), F32),
            shape((8, rows), F32),
            shape((p.wt, rows), F32),
            shape((p.wl, rows), F32),
        ]
    else:
        outs += [
            shape((rows, p.wt), F32),
            shape((rows, 1), F32),
            shape((rows, p.wt), BF16),
            shape((rows, p.wl), F32),
            shape((rows, 1), F32),
            shape((rows, p.wl), BF16),
        ]
    scratch = [
        pltpu.VMEM((nb, padded_t, p.cols), BF16),
        pltpu.VMEM((nb, padded_l, p.cols), BF16),
        pltpu.VMEM((p.wt, rows), F32),
        pltpu.VMEM((p.wl, rows), F32),
        pltpu.VMEM((p.ct, rows), BF16),
        pltpu.VMEM((p.cl, rows), BF16),
        pltpu.SemaphoreType.DMA((nb,)),
        pltpu.SemaphoreType.DMA,
        pltpu.SemaphoreType.DMA,
    ]
    args = (me2, bias_t, bias_l, vec_t, vec_l, spread_t, spread_l, *rows_in, *pieces)
    return kernel_call(
        body,
        outs,
        [SM] + [VM] * (6 + n_in) + [ANY] * n_piece,
        [ANY] + [VM] * (len(outs) - 1),
        scratch,
        args,
    )


def feed_forward(p, me2, pieces, w_lays, h_t, h_l, bin_t, bin_l, spread_t):
    rows = p.rows
    padded_t = p.n_dp * p.ra
    exact_t = p.ra == p.d_own
    root = 1.0 / math.sqrt(2.0)
    nb = p.n_t // 2

    def body(*refs):
        (me_ref, wl_a, wl_b, ht, hl, bt, bl, spt), refs = refs[:8], refs[8:]
        piece_refs, refs = refs[:4], refs[4:]
        outs, scratch = refs[:6], refs[6:]
        g_t, gp_t, g_l, gp_l = outs[:4]
        fpad, acc_t, acc_l, sem_t = scratch
        my_dp, my_t = me_ref[0], me_ref[1]
        for k in range(nb):
            for m in range(2):
                for y in range(2):
                    src = piece_refs[y].at[k] if m == 0 else piece_refs[2 + k].at[y]
                    for z in range(p.far):
                        row = pl.multiple_of(((z * 2 + y) ^ my_dp) * p.ra, 16)
                        pltpu.make_async_copy(
                            src.at[z], fpad.at[k, m, pl.ds(row, p.ra)], sem_t.at[k]
                        ).start()
        acc_t[...] = jnp.zeros_like(acc_t)
        acc_l[...] = jnp.zeros_like(acc_l)

        def gelu(u, g_ref, gp_ref, k):
            cdf = 0.5 + 0.5 * lax.erf(u * root)
            low = (u * cdf).astype(BF16)
            g_ref[k] = low
            dens = jnp.exp(u * u * -0.5) * (1.0 / math.sqrt(2.0 * math.pi))
            gp_ref[k] = (cdf + u * dens).astype(gp_ref.dtype)
            return low

        def block(k):
            wait_for(fpad.at[k], sem_t.at[k])
            if not exact_t:
                for m in range(2):
                    fpad[k, m, pl.ds(0, p.wt)] = dot(spt[...], fpad[k, m]).astype(BF16)
            own_t = (2 * k) ^ my_t
            g = gelu(dot(ht[...], fpad[k, 0, pl.ds(0, p.wt)]) + bt[own_t], g_t, gp_t, k)
            acc_t[...] += dot(g, fpad[k, 1, pl.ds(0, p.wt)], 1, 1)
            w = wl_b[2] if k else wl_a[0]
            up = w[:, 4 * p.cl : 4 * p.cl + p.hl]
            down = w[:, 4 * p.cl + p.hl : p.lay_cols]
            g = gelu(dot(hl[...], up) + bl[own_t], g_l, gp_l, k)
            acc_l[...] += dot(g, down, 1, 1)

        for k in range(nb):
            block(k)
        outs[4][...] = acc_t[...]
        outs[5][...] = acc_l[...]

    outs = [
        shape((nb, rows, p.ht), BF16),
        shape((nb, rows, p.ht), BF16),
        shape((nb, rows, p.hl), BF16),
        shape((nb, rows, p.hl), BF16),
    ]
    outs += [shape((rows, p.wt), F32), shape((rows, p.wl), F32)]
    scratch = [
        pltpu.VMEM((nb, 2, padded_t, p.ht), BF16),
        pltpu.VMEM((rows, p.wt), F32),
        pltpu.VMEM((rows, p.wl), F32),
        pltpu.SemaphoreType.DMA((nb,)),
    ]
    args = (me2, *w_lays, h_t, h_l, bin_t, bin_l, spread_t, *pieces)
    return kernel_call(
        body,
        outs,
        [SM] + [VM] * 7 + [ANY] * 4,
        [VM] * len(outs),
        scratch,
        args,
    )


def feed_middle(p, me2, pieces, w_lay, h_t, h_l, bin_t, bin_l, spread_t, rest_in):
    rows = p.rows
    padded_t = p.n_dp * p.ra
    exact_t = p.ra == p.d_own
    root = 1.0 / math.sqrt(2.0)
    nb = p.n_t // 2

    def body(*refs):
        (me_ref, wl, ht, hl, bt, bl, spt), refs = refs[:7], refs[7:]
        (acc_t_in, acc_l_in, n1t_, n1l_, c0, c1, c2, c3, vt, vl), refs = refs[:10], refs[10:]
        piece_refs, refs = refs[:4], refs[4:]
        n_out = 11 + p.n_t
        outs, scratch = refs[:n_out], refs[n_out:]
        out_tl = outs[11:]
        (low, high, gfl, dbt, dbl, df_t, df_l, gv_t, gv_l, dh_t, dh_l) = outs[:11]
        fpad, staged, acc_t, acc_l, g_t, gp_t, g_l, gp_l, sem_t, sem_out = scratch
        my_dp, my_t = me_ref[0], me_ref[1]
        for k in range(nb):
            for m in range(2):
                for y in range(2):
                    src = piece_refs[y].at[k] if m == 0 else piece_refs[2 + k].at[y]
                    for z in range(p.far):
                        row = pl.multiple_of(((z * 2 + y) ^ my_dp) * p.ra, 16)
                        pltpu.make_async_copy(
                            src.at[z], fpad.at[k, m, pl.ds(row, p.ra)], sem_t.at[k]
                        ).start()
        acc_t[...] = acc_t_in[...]
        acc_l[...] = acc_l_in[...]

        def gelu(u, g_ref, gp_ref, k):
            cdf = 0.5 + 0.5 * lax.erf(u * root)
            value = (u * cdf).astype(BF16)
            g_ref[k] = value
            dens = jnp.exp(u * u * -0.5) * (1.0 / math.sqrt(2.0 * math.pi))
            gp_ref[k] = cdf + u * dens
            return value

        for k in range(nb):
            wait_for(fpad.at[k], sem_t.at[k])
            if not exact_t:
                for m in range(2):
                    fpad[k, m, pl.ds(0, p.wt)] = dot(spt[...], fpad[k, m]).astype(BF16)
            own_t = (2 * k + 1) ^ my_t
            g = gelu(dot(ht[...], fpad[k, 0, pl.ds(0, p.wt)]) + bt[own_t], g_t, gp_t, k)
            acc_t[...] += dot(g, fpad[k, 1, pl.ds(0, p.wt)], 1, 1)
            w = wl[k]
            up = w[:, 4 * p.cl : 4 * p.cl + p.hl]
            down = w[:, 4 * p.cl + p.hl : p.lay_cols]
            g = gelu(dot(hl[...], up) + bl[own_t], g_l, gp_l, k)
            acc_l[...] += dot(g, down, 1, 1)
        for n1, acc, vec, begin, dr_ref, df_ref, gv in (
            (n1t_, acc_t, vt, 0, dh_t, df_t, gv_t),
            (n1l_, acc_l, vl, p.wt, dh_l, df_l, gv_l),
        ):
            width = n1.shape[1]
            per = p.quarter
            h1 = n1[...] * vec[3:4] + vec[4:5]
            n2, inv2 = norm_parts(h1 + acc[...] + vec[5:6])
            value = (n2 * vec[6:7] + vec[7:8]).astype(BF16)
            for k in range(p.n_t):
                out_tl[k][:, pl.ds(begin, width)] = value[k * p.quarter : (k + 1) * p.quarter]
            ct = jnp.concatenate([ref[:, begin : begin + width] for ref in (c0, c1, c2, c3)], axis=0).astype(F32)
            dr = norm_back(ct, n2, inv2, vec[6:7])
            dr_ref[...] = dr
            df_ref[...] = dr.astype(BF16)
            gv[...] = jnp.zeros_like(gv)
            gv[5:6] = col_sum(dr)
            gv[6:7] = col_sum(ct * n2)
            gv[7:8] = col_sum(ct)
        df, dfl = df_t[...], df_l[...]
        dfT, hT, dfTl, hTl = df.T, ht[...].T, dfl.T, hl[...].T
        for k in range(nb):
            du = dot(df, fpad[k, 1, pl.ds(0, p.wt)]) * gp_t[k]
            dbt[k] = col_sum(du)
            du_low = du.astype(BF16)
            grads = (dot(hT, du_low).astype(BF16), dot(dfT, g_t[k]).astype(BF16))
            for m in range(2):
                value = grads[m]
                if not exact_t:
                    value = dot(spt[...], value, 0, 0).astype(BF16)
                staged[k, m] = value
                slot = (lambda d, y, z: low.at[k, y, z]) if m == 0 else (lambda d, y, z: high.at[y, k, z])
                store_slots(p, staged.at[k, m], slot, my_dp, sem_out, [(0, p.ra, 0, p.ra, 0)])
            dh_t[...] += dot(du_low, fpad[k, 0, pl.ds(0, p.wt)], 1, 1)
            w = wl[k]
            up = w[:, 4 * p.cl : 4 * p.cl + p.hl]
            down = w[:, 4 * p.cl + p.hl : p.lay_cols]
            du = dot(dfl, down) * gp_l[k]
            dbl[k] = col_sum(du)
            du_low = du.astype(BF16)
            gfl[k, :, pl.ds(0, p.hl)] = dot(hTl, du_low).astype(BF16)
            gfl[k, :, pl.ds(p.hl, p.hl)] = dot(dfTl, g_l[k]).astype(BF16)
            dh_l[...] += dot(du_low, up, 1, 1)
        wait_for(staged, sem_out)

    outs = [
        shape((2, 2, p.far, p.ra, p.ht), BF16),
        shape((2, 2, p.far, p.ra, p.ht), BF16),
        shape((nb, p.wl, 2 * p.hl), BF16),
        shape((nb, 1, p.ht), F32),
        shape((nb, 1, p.hl), F32),
        shape((rows, p.wt), BF16),
        shape((rows, p.wl), BF16),
        shape((8, p.wt), F32),
        shape((8, p.wl), F32),
        shape((rows, p.wt), F32),
        shape((rows, p.wl), F32),
    ]
    outs += [shape((p.quarter, p.wt + p.wl), BF16)] * p.n_t
    scratch = [
        pltpu.VMEM((nb, 2, padded_t, p.ht), BF16),
        pltpu.VMEM((nb, 2, padded_t, p.ht), BF16),
        pltpu.VMEM((rows, p.wt), F32),
        pltpu.VMEM((rows, p.wl), F32),
        pltpu.VMEM((nb, rows, p.ht), BF16),
        pltpu.VMEM((nb, rows, p.ht), F32),
        pltpu.VMEM((nb, rows, p.hl), BF16),
        pltpu.VMEM((nb, rows, p.hl), F32),
        pltpu.SemaphoreType.DMA((nb,)),
        pltpu.SemaphoreType.DMA,
    ]
    args = (me2, w_lay, h_t, h_l, bin_t, bin_l, spread_t, *rest_in, *pieces)
    return kernel_call(
        body, outs, [SM] + [VM] * 16 + [ANY] * 4, [ANY, ANY] + [VM] * (len(outs) - 2), scratch, args
    )


def store_slots(p, staged, slot_of, my_dp, sem, slices):
    for z in range(p.far):
        for y in range(2):
            at = (z * 2 + y) ^ my_dp
            for dst, per, begin, count, off in slices:
                pltpu.make_async_copy(
                    staged.at[pl.ds(pl.multiple_of(at * per + begin, 16), count)],
                    slot_of(dst, y, z).at[pl.ds(off, count)],
                    sem,
                ).start()


def feed_backward(p, me2, pieces, w_lays, h_t, h_l, df_t, df_l, g_t, gp_t, g_l, gp_l, spread_t, prev):
    n_t, rows = p.n_t, p.rows
    padded_t = p.n_dp * p.ra
    exact_t = p.ra == p.d_own
    nb = n_t // 2

    def body(*refs):
        (me_ref, wl_a, wl_b, ht, hl, dft, dfl, gt, gpt, gl, gpl, spt), refs = refs[:12], refs[12:]
        (pt, pl_, n1t, i1t, n1l, i1l, vt, vl), refs = refs[:8], refs[8:]
        piece_refs, refs = refs[:4], refs[4:]
        outs, scratch = refs[:11], refs[11:]
        low, high, gfl, dbt, dbl = outs[:5]
        f_in, staged, acc_t, acc_l, sem_in, sem_out = scratch
        my_dp, my_t = me_ref[0], me_ref[1]
        for k in range(nb):
            for m in range(2):
                for y in range(2):
                    src = piece_refs[y].at[k] if m == 0 else piece_refs[2 + k].at[y]
                    for z in range(p.far):
                        row = pl.multiple_of(((z * 2 + y) ^ my_dp) * p.ra, 16)
                        pltpu.make_async_copy(
                            src.at[z], f_in.at[k, m, pl.ds(row, p.ra)], sem_in.at[k]
                        ).start()
        dfT, hT = dft[...].T, ht[...].T
        dfTl, hTl = dfl[...].T, hl[...].T
        acc_t[...] = pt[...]
        acc_l[...] = pl_[...]
        for k in range(nb):
            wait_for(f_in.at[k], sem_in.at[k])
            if not exact_t:
                for m in range(2):
                    f_in[k, m, pl.ds(0, p.wt)] = dot(spt[...], f_in[k, m]).astype(BF16)
            du = dot(dft[...], f_in[k, 1, pl.ds(0, p.wt)]) * gpt[k].astype(F32)
            dbt[k] = col_sum(du)
            du_low = du.astype(BF16)
            grads = (dot(hT, du_low).astype(BF16), dot(dfT, gt[k]).astype(BF16))
            for m in range(2):
                value = grads[m]
                if not exact_t:
                    value = dot(spt[...], value, 0, 0).astype(BF16)
                staged[k, m] = value
                if m == 0:
                    store_slots(p, staged.at[k, m], lambda d, y, z: low.at[k, y, z], my_dp, sem_out, [(0, p.ra, 0, p.ra, 0)])
                else:
                    store_slots(p, staged.at[k, m], lambda d, y, z: high.at[y, k, z], my_dp, sem_out, [(0, p.ra, 0, p.ra, 0)])
            acc_t[...] += dot(du_low, f_in[k, 0, pl.ds(0, p.wt)], 1, 1)
            w = wl_b[2] if k else wl_a[0]
            up = w[:, 4 * p.cl : 4 * p.cl + p.hl]
            down = w[:, 4 * p.cl + p.hl : p.lay_cols]
            du = dot(dfl[...], down) * gpl[k].astype(F32)
            dbl[k] = col_sum(du)
            du_low = du.astype(BF16)
            gfl[k, :, pl.ds(0, p.hl)] = dot(hTl, du_low).astype(BF16)
            gfl[k, :, pl.ds(p.hl, p.hl)] = dot(dfTl, gl[k]).astype(BF16)
            acc_l[...] += dot(du_low, up, 1, 1)
        dr1t, dr1l, dat, dal, gvt, gvl = outs[5:]
        for acc, n1, i1, vec, o, low_o, gv in (
            (acc_t, n1t, i1t, vt, dr1t, dat, gvt),
            (acc_l, n1l, i1l, vl, dr1l, dal, gvl),
        ):
            dh = acc[...]
            n = n1[...]
            dr1 = norm_back(dh, n, i1[...], vec[3:4])
            o[...] = dr1
            low_o[...] = dr1.astype(BF16)
            gv[...] = jnp.zeros_like(gv)
            gv[2:3] = col_sum(dr1)
            gv[3:4] = col_sum(dh * n)
            gv[4:5] = col_sum(dh)
        wait_for(staged, sem_out)

    outs = [
        shape((2, 2, p.far, p.ra, p.ht), BF16),
        shape((2, 2, p.far, p.ra, p.ht), BF16),
        shape((nb, p.wl, 2 * p.hl), BF16),
        shape((nb, 1, p.ht), F32),
        shape((nb, 1, p.hl), F32),
    ]
    args = [me2, *w_lays, h_t, h_l, df_t, df_l, g_t, gp_t, g_l, gp_l, spread_t]
    args += list(prev) + list(pieces)
    outs += [
        shape((rows, p.wt), F32),
        shape((rows, p.wl), F32),
        shape((rows, p.wt), BF16),
        shape((rows, p.wl), BF16),
        shape((8, p.wt), F32),
        shape((8, p.wl), F32),
    ]
    scratch = [
        pltpu.VMEM((nb, 2, padded_t, p.ht), BF16),
        pltpu.VMEM((nb, 2, padded_t, p.ht), BF16),
        pltpu.VMEM((rows, p.wt), F32),
        pltpu.VMEM((rows, p.wl), F32),
        pltpu.SemaphoreType.DMA((nb,)),
        pltpu.SemaphoreType.DMA,
    ]
    specs = [SM] + [VM] * (len(args) - 5) + [ANY] * 4
    return kernel_call(
        body, outs, specs, [ANY, ANY] + [VM] * (len(outs) - 2), scratch, args
    )


def attend_backward(p, me2, xs, arrays, gfls, x_low, lay_low, ints, ints_t, da_t, da_l, spread_t, spread_l, prev, last):
    n_t, rows, hw, nh = p.n_t, p.rows, p.hw, p.heads
    padded_t, padded_l = p.n_dp * p.ra, p.n_dp * p.rl
    exact_t = p.ra == p.d_own
    nb = len(xs)
    n_prev, n_core = len(prev), len(gfls)

    def body(*refs):
        (me_ref, xl, ll, ir, itr, dat, dal, spt, spl), refs = refs[:9], refs[9:]
        (w_any, wl_ref, qkv_r, ctx_r, lse_r), refs = refs[:5], refs[5:]
        gfl_refs, refs = refs[:n_core], refs[n_core:]
        prev_refs, refs = refs[:n_prev], refs[n_prev:]
        n_out = 2 * n_core + 4
        outs, scratch = refs[:n_out], refs[n_out:]
        slot_refs = [outs[2 * c : 2 * c + 2] for c in range(n_core)]
        gb_t, gb_l, out_a, out_b = outs[2 * n_core :]
        (w_in, staged, staged_l, acc_t, acc_l, dctx, ctx_s, ctx_l, dp_t, dp_l, bin_rows, sem_in,
         sem_out, sem_bin) = scratch
        my_dp, my_t = me_ref[0], me_ref[1]
        for k, (_, x, _) in enumerate(xs):
            pltpu.make_async_copy(w_any.at[x], w_in.at[k], sem_in.at[k]).start()
        xT, lT = xl[...].T, ll[...].T
        daT, dalT = dat[...].T, dal[...].T
        seg_col, seg_row = ir[:, 0:1], itr[0:1, :]
        if prev:
            acc_t[...] = prev_refs[0][...]
            acc_l[...] = prev_refs[1][...]
        else:
            acc_t[...] = jnp.zeros_like(acc_t)
            acc_l[...] = jnp.zeros_like(acc_l)
        ones = jnp.ones((16, rows), BF16)
        for k, (c, x, g_at) in enumerate(xs):
            low, high = slot_refs[c]
            at_k = sum(1 for member in xs[:k] if member[0] == c)
            wait_for(w_in.at[k], sem_in.at[k])
            w = w_in[k]
            wl = wl_ref[x]
            d_t = dot(dat[...], w[:, 3 * p.ct :]).T
            d_l = dot(dal[...], wl[:, 3 * p.cl : 4 * p.cl]).T
            for h in range(nh):
                dctx[h, pl.ds(0, HD)] = d_t[h * HD : (h + 1) * HD].astype(BF16)
                dctx[h, pl.ds(HD, LHD)] = d_l[h * LHD : (h + 1) * LHD].astype(BF16)
                ctx_s[pl.ds(h * HD, HD)] = ctx_r[x, h, pl.ds(0, HD)]
                ctx_l[pl.ds(h * LHD, LHD)] = ctx_r[x, h, pl.ds(HD, LHD)]

            for h in range(nh):
                q, key, val = qkv_r[x, h], qkv_r[x, nh + h], qkv_r[x, 2 * nh + h]
                dc = dctx[h]
                scores = dot(key, q, 0, 0)
                probs = jnp.exp(
                    jnp.where(seg_col == seg_row, scores, NEG_FILL) - lse_r[x, pl.ds(h, 1), :]
                )
                low_p = probs.astype(BF16)
                prod = dc.astype(F32) * ctx_r[x, h].astype(F32)
                sum_lay = jnp.sum(prod[HD:], axis=0, keepdims=True)
                sum_all = jnp.sum(prod[:HD], axis=0, keepdims=True) + sum_lay
                dz_all = probs * (dot(val, dc, 0, 0) - sum_all)
                dz_lay = probs * (dot(val[HD:], dc[HD:], 0, 0) - sum_lay)
                ds_t, ds_l = dz_all.astype(BF16), dz_lay.astype(BF16)
                dv = dot(dc, low_p, 1, 1)
                dq_t = dot(key[:HD], ds_t) * (1.0 / math.sqrt(HD))
                dq_l = dot(key[HD:], ds_l) * (1.0 / math.sqrt(LHD))
                dk_t = dot(q[:HD], ds_t, 1, 1)
                dk_l = dot(q[HD:], ds_l, 1, 1)
                for m, (top, bot) in enumerate(((dq_t, dq_l), (dk_t, dk_l), (dv[:HD], dv[HD:]))):
                    dp_t[pl.ds(m * p.ct + h * HD, HD)] = top.astype(BF16)
                    dp_l[pl.ds(m * p.cl + h * LHD, LHD)] = bot.astype(BF16)
            gb_t[k] = dot(ones, dp_t[...], 1, 1)[:8]
            gb_l[k] = dot(ones, dp_l[...], 1, 1)[:8]
            acc_t[...] += dot(w[:, : 3 * p.ct], dp_t[...])
            acc_l[...] += dot(wl[:, : 3 * p.cl], dp_l[...])
            grad = jnp.concatenate(
                [dot(xT, dp_t[...], 1, 1), dot(daT, ctx_s[...], 1, 1)], axis=1
            ).astype(BF16)
            if not exact_t:
                grad = dot(spt[...], grad, 0, 0).astype(BF16)
            staged[k] = grad
            fill = p.cols - p.lay_cols
            grad_l = jnp.concatenate(
                [
                    dot(lT, dp_l[...], 1, 1),
                    dot(dalT, ctx_l[...], 1, 1),
                    gfl_refs[c][g_at].astype(F32),
                    jnp.zeros((p.wl, fill), F32),
                ],
                axis=1,
            ).astype(BF16)
            staged_l[k] = dot(spl[...], grad_l, 0, 0).astype(BF16)
            rest = p.ra - p.half_a
            slot = lambda d, y, z: high.at[y, at_k, z] if d else low.at[at_k, y, z]
            slices = [(0, p.ra, 0, p.half_a, 0)]
            if rest:
                slices.append((1, p.ra, p.half_a, rest, 0))
            store_slots(p, staged.at[k], slot, my_dp, sem_out.at[0], slices)
            store_slots(p, staged_l.at[k], slot, my_dp, sem_out.at[1], [(1, p.rl, 0, p.rl, rest)])
        if last:
            gt = prev_refs[2][...] + acc_t[...].T
            gl = prev_refs[3][...] + acc_l[...].T
            out_a[:, pl.ds(0, p.wt)] = gt.astype(BF16)
            out_a[:, pl.ds(p.wt, p.wl)] = gl.astype(BF16)
            half = p.wl // 2
            bins = bin_rows.shape[0]
            levels = lax.broadcasted_iota(jnp.int32, (bins, 1), 0).astype(F32)
            for m in range(2):
                row = itr[1 + 2 * m : 2 + 2 * m, :] * 128.0 + itr[2 + 2 * m : 3 + 2 * m, :]
                hot = (levels == row).astype(F32).astype(BF16)
                part = gl[:, m * half : (m + 1) * half]
                top = part.astype(BF16)
                rest_part = (part - top.astype(F32)).astype(BF16)
                both = dot(hot, jnp.concatenate([top, rest_part], axis=1))
                bin_rows[:, pl.ds(m * half, half)] = (both[:, :half] + both[:, half:]).astype(BF16)
            if p.per % 16:
                pltpu.make_async_copy(bin_rows, out_b, sem_bin).start()
            else:
                for r in range(p.total):
                    z, y, x, c = r // 8, (r // 4) % 2, (r // 2) % 2, r % 2
                    at = ((r // n_t) ^ my_dp) * n_t + ((r % n_t) ^ my_t)
                    pltpu.make_async_copy(
                        bin_rows.at[pl.ds(pl.multiple_of(at * p.per, 16), p.per)],
                        out_b.at[c, y, x, z],
                        sem_bin,
                    ).start()
            wait_for(bin_rows, sem_bin)
        else:
            out_a[...] = acc_t[...]
            out_b[...] = acc_l[...]
        wait_for(staged, sem_out.at[0])
        wait_for(staged_l, sem_out.at[1])

    half_b = p.ra + p.rl - p.half_a
    slots_out = []
    for c in range(n_core):
        held = sum(1 for member in xs if member[0] == c)
        slots_out += [
            shape((held, 2, p.far, p.half_a, p.cols), BF16),
            shape((2, held, p.far, half_b, p.cols), BF16),
        ]
    outs = slots_out + [
        shape((nb, 8, 3 * p.ct), F32),
        shape((nb, 8, 3 * p.cl), F32),
    ]
    args = [me2, x_low, lay_low, ints, ints_t, da_t, da_l, spread_t, spread_l]
    specs = [SM] + [VM] * 8 + [ANY] + [VM] * (4 + n_core + n_prev)
    args += [*arrays, *gfls, *prev]
    if last:
        bins = p.per * p.total
        slots = (bins,) if p.per % 16 else (2, 2, 2, p.far, p.per)
        outs += [shape((rows, p.wt + p.wl), BF16), shape((*slots, p.wl), BF16)]
    else:
        outs += [shape((p.wt, rows), F32), shape((p.wl, rows), F32)]
    scratch = [
        pltpu.VMEM((nb, p.wt, p.cols), BF16),
        pltpu.VMEM((nb, padded_t, p.cols), BF16),
        pltpu.VMEM((nb, padded_l, p.cols), BF16),
        pltpu.VMEM((p.wt, rows), F32),
        pltpu.VMEM((p.wl, rows), F32),
        pltpu.VMEM((nh, hw, rows), BF16),
        pltpu.VMEM((p.ct, rows), BF16),
        pltpu.VMEM((p.cl, rows), BF16),
        pltpu.VMEM((3 * p.ct, rows), BF16),
        pltpu.VMEM((3 * p.cl, rows), BF16),
        pltpu.VMEM((p.per * p.total, p.wl), BF16),
        pltpu.SemaphoreType.DMA((nb,)),
        pltpu.SemaphoreType.DMA((2,)),
        pltpu.SemaphoreType.DMA,
    ]
    out_specs = [ANY] * (2 * n_core) + [VM] * 3 + [ANY if last else VM]
    return kernel_call(body, outs, specs, out_specs, scratch, args)


def tie(*groups):
    leaves, tree = jax.tree.flatten(groups)
    return jax.tree.unflatten(tree, lax.optimization_barrier(leaves))


def after(values, *others):
    return tie(values, *others)[0]


def line_of(shard, total):
    return [shard] + [xor_send(shard, total, 8 * r) for r in range(1, total // 8)]


def line_doubled(shard, total, others):
    line = [shard]
    while 8 * len(line) < total:
        held = jnp.stack(line)
        if len(line) > 1:
            held = after(held, others)
        theirs = xor_send(held, total, 8 * len(line))
        line = line + [theirs[z] for z in range(len(line))]
    return line


def halves_of(line, half):
    low = jnp.stack([member[:half] for member in line])
    high = jnp.stack([member[half:] for member in line])
    return low, high


def add_low(mine, theirs):
    return to_low(mine.astype(F32) + theirs.astype(F32))


def reduce_second(mine, got):
    send = [add_low(mine[k][1], got[k][1]) for k in range(2)]
    keep = [add_low(mine[k][0], got[k][0]) for k in range(2)]
    return send, keep


def reduce_line_parts(keep, got):
    return [
        jnp.concatenate([add_low(keep[k][z], got[k][z]) for k in range(2)], axis=0)
        for z in range(keep[0].shape[0])
    ]


def send_line(line, total):
    return line[:1] + [xor_send(line[z], total, 8 * z) for z in range(1, len(line))]


def add_line(line):
    out = line[0].astype(F32)
    for member in line[1:]:
        out = out + member.astype(F32)
    return out


def update_all(factor, matrices, flat, grads):
    states = [member for group in (*matrices, *flat) for member in group]

    def body(*refs):
        factor_ref, grads = refs[0], refs[1:7]
        ins, outs = refs[7:25], refs[25:]
        scale = factor_ref[0, 0]
        for k in range(6):
            w, m, v = (ins[3 * k + j][...] for j in range(3))
            results = adamw_step(
                w, m, v, grads[k][...] * scale, WEIGHT_DECAY if k < 4 else 0.0, LEARN_RATES[k]
            )
            for j in range(3):
                outs[3 * k + j][...] = results[j]

    return list(
        kernel_call(
            body,
            [shape(v.shape, F32) for v in states],
            [SM] + [VM] * 24,
            [VM] * 18,
            [],
            (factor.reshape(1, 1), *grads, *states),
        )
    )


def relative(blocks, me):
    total = blocks.shape[0]
    step = 1
    while step < total:
        pairs = blocks.reshape(total // (2 * step), 2, step, *blocks.shape[1:])
        swapped = jnp.stack([pairs[:, 1], pairs[:, 0]], axis=1)
        blocks = jnp.where((me // step) % 2 == 0, pairs, swapped).reshape(blocks.shape)
        step = step * 2
    return blocks


def on_device(
    text_in,
    layout_in,
    segment_ids,
    box_bins,
    text_cot,
    layout_cot,
    attend_text,
    attend_text_mean,
    attend_text_square,
    feed_text,
    feed_text_mean,
    feed_text_square,
    attend_layout,
    attend_layout_mean,
    attend_layout_square,
    feed_layout,
    feed_layout_mean,
    feed_layout_square,
    vectors,
    vectors_mean,
    vectors_square,
    tables,
    tables_mean,
    tables_square,
):
    n_dp, n_t = lax.axis_size("dp"), lax.axis_size("tensor")
    total = n_dp * n_t
    t_pos = lax.axis_index("tensor")
    pages, quarter, wt = text_in.shape
    wl = layout_in.shape[1] // quarter
    d_own, dl_own = attend_text.shape[0], attend_layout.shape[0]
    ct, cl = attend_text.shape[2], attend_layout.shape[2]
    ht, hl = feed_text.shape[2], feed_layout.shape[2]


    p = Plan(n_dp, n_t, quarter, wt, wl, ct, cl, ht, hl, tables.shape[0] // wl)
    me = lax.axis_index("dp") * n_t + t_pos
    me2 = jnp.stack([lax.axis_index("dp"), t_pos]).astype(jnp.int32)
    lay_cols = p.lay_cols

    def pad_rows(values, count):
        return jnp.pad(values, ((0, count - values.shape[0]), (0, 0)))

    lay_pack = jnp.concatenate(
        [
            to_low(attend_layout).reshape(dl_own, 4 * cl),
            to_low(feed_layout).reshape(dl_own, 2 * hl),
        ],
        axis=1,
    )
    lay_pack = jnp.pad(lay_pack, ((0, p.rl - dl_own), (0, p.cols - lay_cols)))
    attend_pack = jnp.concatenate(
        [pad_rows(to_low(attend_text).reshape(d_own, p.cols), p.ra), lay_pack]
    )
    low_feed = to_low(feed_text)
    feed_pack = jnp.concatenate(
        [pad_rows(low_feed[:, 0], p.ra), pad_rows(low_feed[:, 1], p.ra)]
    )
    bins = box_bins.reshape(pages, quarter, 2)
    digits = jnp.stack(
        [segment_ids, bins[..., 0] // 128, bins[..., 0] % 128, bins[..., 1] // 128, bins[..., 1] % 128],
        axis=-1,
    )
    packed_in = jnp.concatenate(
        [
            text_in,
            layout_in.reshape(pages, quarter, wl),
            jnp.pad(to_low(digits), ((0, 0), (0, 0), (0, 59))),
        ],
        axis=2,
    )
    packed_cot = jnp.concatenate([text_cot, layout_cot.reshape(pages, quarter, wl)], axis=2)

    def blocks_of(values):
        return [lax.dynamic_index_in_dim(values, t_pos ^ r, 0, keepdims=False) for r in range(n_t)]

    def send_blocks(blocks):
        return [blocks[0]] + [xor_send(blocks[r], total, r) for r in range(1, n_t)]

    def page_of(values):
        return send_blocks(blocks_of(values))

    def send_rows(page):
        return send_blocks(page.reshape(n_t, quarter, page.shape[-1]))

    def pages_of(blocks):
        out = jnp.zeros((n_t,) + blocks[0].shape, blocks[0].dtype)
        for r in range(n_t):
            out = lax.dynamic_update_slice(out, blocks[r][None], (t_pos ^ r, 0, 0))
        return out

    send = lambda values, distance: xor_send(values, total, distance)
    packed_cot = blocks_of(packed_cot)

    line_a = line_of(attend_pack, total)
    xin = page_of(packed_in)
    low, high = halves_of(line_a, p.half_a)
    low, high = after((low, high), xin)
    line_f = line_doubled(feed_pack, total, line_a)
    low0, high0 = jnp.stack([low, send(low, 2)]), jnp.stack([high, send(high, 4)])
    low4, high2 = send(low0, 4), send(high0, 2)
    low1, high1 = send(low0, 1), send(high0, 1)
    late_vectors, late_tables = after((vectors, tables), low0, high0)
    parts = split_vectors(late_vectors, [wt, wl], [n_t * ht, n_t * hl])
    biases, vecs, bins_in = [], [], []
    for s, width in ((0, ct), (1, cl)):
        vec, hidden = parts[s]
        biases.append(
            jnp.concatenate(
                [
                    vec[0].reshape(n_t, 1, width),
                    jnp.zeros((n_t, 1, width), F32),
                    vec[1].reshape(n_t, 1, width),
                ],
                axis=2,
            )
        )
        vecs.append(jnp.stack(vec))
        bins_in.append(hidden.reshape(n_t, 1, -1))
    table_rows = to_low(late_tables.reshape(-1, wl))
    spread_t = p.spread(d_own, p.ra) if p.ra != d_own else jnp.zeros((16, 128), BF16)
    spread_l = p.spread(dl_own, p.rl)

    flow, fhigh = halves_of(after(line_f, low0, high0), p.ra)
    flow, fhigh = after((flow, fhigh), low4, high2)
    att_fix = (biases[0], biases[1], vecs[0], vecs[1], spread_t, spread_l)
    low5, high3 = send(low4, 1), send(high2, 1)
    flow_x, fhigh_y = send(flow, 2), send(fhigh, 4)
    (w_all0, w_lay0, qkv0, ctx0, lse0, *row_state) = attend_forward(
        p, me2, ((0, 0),), (*after(xin, bins_in, packed_cot), table_rows), *att_fix, [low0, low4, high0, high2]
    )
    row_state, qkv0, low5, high3, low1, high1, flow_x, fhigh_y = tie(
        row_state, qkv0, low5, high3, low1, high1, flow_x, fhigh_y
    )
    flow0, fhigh0 = jnp.stack([flow, flow_x]), jnp.stack([fhigh, fhigh_y])
    row_state = after(row_state, flow0, fhigh0)
    flow4, fhigh2 = send(flow0, 4), send(fhigh0, 2)
    flow1, fhigh1 = send(flow0, 1), send(fhigh0, 1)
    (w_all1, w_lay1, qkv1, ctx1, lse1, n1t, i1t, h_t, n1l, i1l, h_l) = attend_forward(
        p, me2, ((1, 0), (1, 1), (0, 1)), row_state, *att_fix,
        [low0, low4, high0, high2, low1, low5, high1, high3],
    )
    x_low, lay_low, _, ints, ints_t = row_state[:5]
    n1t, n1l, h_t, h_l, w_lay1, flow4, fhigh2, packed_cot = tie(
        n1t, n1l, h_t, h_l, w_lay1, flow4, fhigh2, packed_cot
    )
    flow5, fhigh3 = send(flow4, 1), send(fhigh2, 1)
    cots = send_blocks(packed_cot)
    (g_t0, gp_t0, g_l0, gp_l0, acc_t, acc_l) = feed_forward(
        p, me2, [flow0, flow4, fhigh0, fhigh2], (w_lay0, w_lay1), h_t, h_l, bins_in[0], bins_in[1], spread_t
    )
    acc_t, acc_l, flow5, fhigh3, flow1, fhigh1, cots = tie(
        acc_t, acc_l, flow5, fhigh3, flow1, fhigh1, cots
    )
    (gf_low1, gf_high1, gfl1, dbt1, dbl1, df_t, df_l, gv2t, gv2l, acc_t, acc_l, *out_rows) = feed_middle(
        p, me2, [flow1, flow5, fhigh1, fhigh3], w_lay1, h_t, h_l, bins_in[0], bins_in[1], spread_t,
        (acc_t, acc_l, n1t, n1l, *cots, vecs[0], vecs[1]),
    )
    rows_out = send_blocks(out_rows)
    got = [send(gf_low1, 1), send(gf_high1, 1)]
    (gf_low0, gf_high0, gfl0, dbt0, dbl0, dr1t, dr1l, da_t, da_l, gv1t, gv1l) = feed_backward(
        p, me2, [flow0, flow4, fhigh0, fhigh2], (w_lay0, w_lay1), h_t, h_l, df_t, df_l, g_t0, gp_t0, g_l0, gp_l0, spread_t,
        (acc_t, acc_l, n1t, i1t, n1l, i1l, vecs[0], vecs[1])
    )
    got, rows_out, gf_low0, gf_high0, gfl0, dbt0, dbl0, dr1t, dr1l, da_t, da_l, gv1t, gv1l = tie(
        got, rows_out, gf_low0, gf_high0, gfl0, dbt0, dbl0, dr1t, dr1l, da_t, da_l, gv1t, gv1l
    )
    next_f = [add_low(gf_low0[1], got[0][1]), add_low(gf_high0[1], got[1][1])]
    da_t, got_feed = after(da_t, next_f), got
    got_f = [send(next_f[0], 2), send(next_f[1], 4)]
    att_args = (x_low, lay_low, ints, ints_t, da_t, da_l, spread_t, spread_l)
    first_arrays, arrays = (w_all0, w_lay0, qkv0, ctx0, lse0), (w_all1, w_lay1, qkv1, ctx1, lse1)
    (low_x1, high_x1, ga_low1, ga_high1, gb_t1, gb_l1, acc_t, acc_l) = attend_backward(
        p, me2, ((1, 0, 0), (1, 1, 1), (0, 2, 1)), arrays, (gfl0, gfl1), *att_args, (), False
    )
    got_f, low_x1, high_x1, ga_low1, ga_high1, gb_t1, gb_l1, acc_t, acc_l = tie(
        got_f, low_x1, high_x1, ga_low1, ga_high1, gb_t1, gb_l1, acc_t, acc_l
    )
    stay = after((gf_low0, gf_high0, got_feed[0], got_feed[1]), got_f)
    keep_f = [add_low(stay[k][0], stay[2 + k][0]) for k in range(2)]
    next_f = [add_low(keep_f[k][1], got_f[k][1]) for k in range(2)]
    keep_f = [add_low(keep_f[k][0], got_f[k][0]) for k in range(2)]
    acc_t = after(acc_t, next_f)
    got = [send(ga_low1, 1), send(ga_high1, 1)]
    got_f = [send(next_f[0], 4), send(next_f[1], 2)]
    (low_x0, high_x0, gb_t00, gb_l00, grad_rows, table_grad) = attend_backward(
        p, me2, ((0, 0, 0),), first_arrays, (gfl0,), *att_args, (acc_t, acc_l, dr1t, dr1l), True
    )
    got, got_f, low_x0, high_x0, gb_t00, gb_l00, grad_rows, table_grad = tie(
        got, got_f, low_x0, high_x0, gb_t00, gb_l00, grad_rows, table_grad
    )
    if p.per % 16:
        table_grad = relative(table_grad.reshape(total, p.per, wl), me)
        table_grad = table_grad.reshape(p.far, 2, 2, 2, p.per, wl).transpose(3, 1, 2, 0, 4, 5)
    table_got = send(table_grad[1], 1)
    low_x1 = add_low(low_x1[0], got[0][1])
    got_low = send(low_x1, 2)
    rest = p.ra - p.half_a
    spare = high_x0.shape[-2] - rest - p.per
    edges = ((0, 0), (0, 0), (0, 0), (rest, spare), (lay_cols, p.cols - lay_cols - wl))
    table_sum = jnp.pad(add_low(table_grad[0], after(table_got, low_x1)), edges)
    both = [jnp.concatenate([high_x0[y], high_x1[y]]) for y in range(2)]
    next_high = to_low(both[1].astype(F32) + got[1][1].astype(F32) + table_sum[1].astype(F32))
    got_high = send(next_high, 4)
    line_f = send_line(reduce_line_parts(keep_f, after(got_f, next_high)), total)
    low = to_low(low_x0[0].astype(F32) + got[0][0].astype(F32) + got_low.astype(F32))
    got_low = send(low[1], 4)
    high = to_low(
        both[0].astype(F32)
        + got[1][0].astype(F32)
        + table_sum[0].astype(F32)
        + got_high.astype(F32)
    )
    got_high = send(high[1], 2)
    pieces = (gb_t1, gb_l1, gb_t00, gb_l00, dbt0, dbt1, dbl0, dbl1, gv1t, gv1l, gv2t, gv2l)
    (gb_t1, gb_l1, gb_t00, gb_l00, dbt0, dbt1, dbl0, dbl1, gv1t, gv1l, gv2t, gv2l) = after(
        pieces, next_high
    )
    gb_t0 = jnp.concatenate([gb_t00, gb_t1[2:]])
    gb_l0 = jnp.concatenate([gb_l00, gb_l1[2:]])
    feed_sum = add_line(after(line_f, low, high))
    line_a = reduce_line_parts((low[0], high[0]), (got_low, got_high))
    rows_out, grad_rows = after((rows_out, grad_rows), line_a)
    late_pos = after(t_pos, next_high)
    line_a = send_line(line_a, total)
    rows_grad = send_rows(grad_rows)
    feed_sum = after(feed_sum, line_a[1])
    rows_out, rows_grad = pages_of(rows_out), pages_of(rows_grad)
    row_outputs = (
        rows_out[:, :, :wt],
        rows_out[:, :, wt:].reshape(pages, quarter * wl),
        rows_grad[:, :, :wt].astype(F32),
        rows_grad[:, :, wt:].astype(F32).reshape(pages, quarter * wl),
    )
    attend_sum = add_line(after(line_a, row_outputs[:2]))

    def by_block(odd, even):
        both = jnp.stack([even[0], odd[0], even[1], odd[1]]).reshape(n_t, -1)
        order = jnp.arange(n_t) ^ late_pos
        hot = order[:, None] == jnp.arange(n_t)[None, :]
        return jnp.sum(jnp.where(hot[:, :, None], both[None], 0.0), axis=1).reshape(-1)

    gv_t, gv_l = gv2t + gv1t, gv2l + gv1l
    vector_grad = jnp.concatenate(
        [
            by_block(gb_t1[:, 0, : ct], gb_t0[:, 0, : ct]),
            by_block(gb_t1[:, 0, 2 * ct :], gb_t0[:, 0, 2 * ct :]),
            gv_t[2:].reshape(-1),
            by_block(dbt1, dbt0),
            by_block(gb_l1[:, 0, : cl], gb_l0[:, 0, : cl]),
            by_block(gb_l1[:, 0, 2 * cl :], gb_l0[:, 0, 2 * cl :]),
            gv_l[2:].reshape(-1),
            by_block(dbl1, dbl0),
        ]
    )
    own_sq = jnp.sum(feed_sum * feed_sum) + jnp.sum(attend_sum * attend_sum)
    n_vec = vector_grad.shape[0]
    summed = jnp.pad(vector_grad, (0, round_up(n_vec + 1, 1024) - n_vec)).reshape(-1, 128)
    spot = (lax.broadcasted_iota(jnp.int32, summed.shape, 0) == n_vec // 128) & (
        lax.broadcasted_iota(jnp.int32, summed.shape, 1) == n_vec % 128
    )
    summed = jnp.where(spot, own_sq, summed)
    spread_table = to_low(attend_sum[p.ra : p.ra + p.per, lay_cols : lay_cols + wl])
    distance = total // 2
    while distance:
        other = send(summed, distance)
        theirs = send(after(spread_table, summed), distance)
        summed = summed + other
        bit = (me // distance) % 2
        spread_table = jnp.where(
            bit == 0, jnp.stack([spread_table, theirs]), jnp.stack([theirs, spread_table])
        )
        distance = distance // 2
    deep = spread_table.ndim - 2
    order = tuple(range(deep - 1, -1, -1)) + (deep, deep + 1)
    table_grad = spread_table.transpose(order).reshape(-1, 128).astype(F32)
    vector_grad = summed
    all_sq = jnp.sum(jnp.where(spot, 0.0, summed * summed))
    shared_sq = all_sq + summed[n_vec // 128, n_vec % 128]
    clip_norm = jnp.sqrt(shared_sq)
    factor = jnp.minimum(1.0, CLIP_NORM / (clip_norm + 1e-06))
    flat = [
        [v.reshape(-1, 128) for v in group]
        for group in ((vectors, vectors_mean, vectors_square), (tables, tables_mean, tables_square))
    ]
    lay_sum = attend_sum[p.ra : p.ra + dl_own]
    grads = (
        attend_sum[:d_own].reshape(d_own, 4, ct),
        jnp.stack([feed_sum[:d_own], feed_sum[p.ra : p.ra + d_own]], axis=1),
        lay_sum[:, : 4 * cl].reshape(dl_own, 4, cl),
        lay_sum[:, 4 * cl : lay_cols].reshape(dl_own, 2, hl),
        vector_grad[: n_vec // 128],
        table_grad,
    )
    matrices = (
        (attend_text, attend_text_mean, attend_text_square),
        (feed_text, feed_text_mean, feed_text_square),
        (attend_layout, attend_layout_mean, attend_layout_square),
        (feed_layout, feed_layout_mean, feed_layout_square),
    )
    updated = update_all(factor, matrices, flat, grads)
    updated[12:] = [v.reshape(-1) for v in updated[12:]]
    return (
        *row_outputs,
        *updated,
        clip_norm,
    )


def solution(mesh):
    rows3, rows2, cols3 = P("dp", "tensor", None), P("dp", "tensor"), P("dp", None, "tensor")
    in_specs = (rows3, rows2, rows2, rows2, rows3, rows2) + (cols3,) * 12 + (P(),) * 6
    out_specs = (rows3, rows2, rows3, rows2) + (cols3,) * 12 + (P(),) * 7
    return jax.shard_map(
        on_device, mesh=mesh, in_specs=in_specs, out_specs=out_specs, check_vma=False
    )
```

```python
import functools
import math

import jax
import jax.numpy as jnp
from jax import lax
from jax.experimental import pallas as pl
from jax.experimental.pallas import tpu as pltpu
from jax.sharding import PartitionSpec as P

HD = 64
LHD = 16
STEP = 10

NORM_EPS = 1e-05
NEG_FILL = -1000000000.0
CLIP_NORM = 1.0
LEARN_RATES = (0.3, 0.05, 0.3, 0.05, 0.3, 0.3)
BETA_ONE = 0.9
BETA_TWO = 0.999
ADAM_EPS = 1e-08
WEIGHT_DECAY = 0.01
AXES = ("dp", "tensor")
LAY_ROWS = 32
F32 = jnp.float32
BF16 = jnp.bfloat16


def to_low(values):
    return values.astype(BF16)


def xor_send(values, total, distance):
    return lax.ppermute(values, AXES, [(i, i ^ distance) for i in range(total)])


def split_vectors(packed, widths, hidden):
    result = []
    offset = 0
    for stream in range(2):
        width_now = widths[stream]
        pieces = [packed[offset + k * width_now : offset + (k + 1) * width_now] for k in range(8)]
        offset = offset + 8 * width_now
        result.append((pieces, packed[offset : offset + hidden[stream]]))
        offset = offset + hidden[stream]
    return result


def adamw_step(weight, moment, square, gradient, decay_rate, rate_now):
    new_moment = BETA_ONE * moment + (1.0 - BETA_ONE) * gradient
    new_square = BETA_TWO * square + (1.0 - BETA_TWO) * gradient * gradient
    moment_hat = new_moment / (1.0 - BETA_ONE**STEP)
    square_hat = new_square / (1.0 - BETA_TWO**STEP)
    new_weight = weight - rate_now * (
        moment_hat / (jnp.sqrt(square_hat) + ADAM_EPS) + decay_rate * weight
    )
    return (new_weight, new_moment, new_square)


def lane_mean(values):
    return jnp.sum(values, axis=-1, keepdims=True) * (1.0 / values.shape[-1])


def norm_parts(residual):
    centered = residual - lane_mean(residual)
    inv_std = lax.rsqrt(lane_mean(centered * centered) + NORM_EPS)
    return centered * inv_std, inv_std


def norm_back(gradient, normed, inv_std, gain_vec):
    scaled = gradient * gain_vec
    d_resid = inv_std * (
        scaled - lane_mean(scaled) - normed * lane_mean(scaled * normed)
    )
    return d_resid


def col_sum(values):
    return jnp.sum(values, axis=0, keepdims=True)


def dot(a, b, da=1, db=0):
    return lax.dot_general(a, b, (((da,), (db,)), ((), ())), preferred_element_type=F32)


def round_up(count, step):
    return -(-count // step) * step


class Plan:
    def __init__(self, n_dp, n_t, quarter, wt, wl, ct, cl, ht, hl, bins):
        self.n_dp, self.n_t, self.total = n_dp, n_t, n_dp * n_t
        self.far = self.total // 8
        self.quarter, self.rows = quarter, quarter * n_t
        self.wt, self.wl, self.ct, self.cl, self.ht, self.hl = wt, wl, ct, cl, ht, hl
        self.d_own, self.dl_own = wt // n_dp, wl // n_dp
        self.ra, self.rl = round_up(self.d_own, 16), round_up(self.dl_own, 16)
        self.cols = 4 * ct
        self.half_a = (self.ra + self.rl) // 2
        self.heads = ct // HD
        self.hw = HD + LHD
        self.lay_cols = 4 * cl + 2 * hl
        self.per = bins // self.total

    def spread(self, own, padded):
        out = jnp.arange(own * self.n_dp, dtype=jnp.int32)
        place = (out // own) * padded + out % own
        return (place[:, None] == jnp.arange(padded * self.n_dp, dtype=jnp.int32)[None]).astype(BF16)


VMEM_LIMIT = 60 * 2**20
COST = 10 * 10**9
ANY = pl.BlockSpec(memory_space=pl.ANY)
VM = pl.BlockSpec(memory_space=pltpu.VMEM)
SM = pl.BlockSpec(memory_space=pltpu.SMEM)


def kernel_call(body, outs, in_specs, out_specs, scratch, args):
    return pl.pallas_call(
        body,
        out_shape=outs,
        in_specs=in_specs,
        out_specs=out_specs,
        scratch_shapes=scratch,
        compiler_params=pltpu.CompilerParams(vmem_limit_bytes=VMEM_LIMIT),
        cost_estimate=pl.CostEstimate(flops=COST, bytes_accessed=2**20, transcendentals=0),
    )(*args)


def shape(dims, kind):
    return jax.ShapeDtypeStruct(tuple(dims), kind)


def wait_for(ref, sem):
    pltpu.make_async_copy(ref, ref, sem).wait()


def attend_forward(p, me2, blocks, rows_in, bias_t, bias_l, vec_t, vec_l, spread_t, spread_l, pieces):
    rows, hw, nh = p.rows, p.hw, p.heads
    padded_t, padded_l = p.n_dp * p.ra, p.n_dp * p.rl
    exact_t = p.ra == p.d_own
    nb = len(blocks)
    first = nb == 1
    n_piece = len(pieces)
    n_in = len(rows_in)

    def body(*refs):
        (me_ref, bt, bl, vt, vl, spt, spl), refs = refs[:7], refs[7:]
        in_refs, refs = refs[:n_in], refs[n_in:]
        piece_refs, refs = refs[:n_piece], refs[n_piece:]
        n_out = 12 if first else 11
        outs, scratch = refs[:n_out], refs[n_out:]
        wt_out, wl_out, qkv, ctx, lse_ref = outs[:5]
        wpad, lpad, acc_t, acc_l, ctx_rows, ctx_lay, sem_t, sem_l, sem_out = scratch
        my_dp, my_t = me_ref[0], me_ref[1]
        for k, (core, x_at) in enumerate(blocks):
            for y in range(2):
                low, high = piece_refs[4 * core + y].at[x_at], piece_refs[4 * core + 2 + x_at].at[y]
                for z in range(p.far):
                    at = (z * 2 + y) ^ my_dp
                    row = pl.multiple_of(at * p.ra, 16)
                    lrow = pl.multiple_of(at * p.rl, 16)
                    pltpu.make_async_copy(
                        low.at[z], wpad.at[k, pl.ds(row, p.half_a)], sem_t.at[k]
                    ).start()
                    rest = p.ra - p.half_a
                    if rest:
                        pltpu.make_async_copy(
                            high.at[z, pl.ds(0, rest)],
                            wpad.at[k, pl.ds(pl.multiple_of(row + p.half_a, 16), rest)],
                            sem_t.at[k],
                        ).start()
                    pltpu.make_async_copy(
                        high.at[z, pl.ds(rest, p.rl)], lpad.at[k, pl.ds(lrow, p.rl)], sem_l
                    ).start()
        if first:
            x0, x1, x2, x3, tab = in_refs
            xt_ref, lay_low, lay_ref, ints_ref, intst_ref, acc_t_out, acc_l_out = outs[5:]
            for k, ref in enumerate((x0, x1, x2, x3)):
                xt_ref[pl.ds(k * p.quarter, p.quarter), :] = ref[:, : p.wt]
            x = xt_ref[...]
            side = jnp.concatenate([ref[:, p.wt :] for ref in (x0, x1, x2, x3)], axis=0).astype(F32)
            digits = side[:, p.wl : p.wl + 8]
            ints_ref[...] = digits
            intst_ref[...] = digits.T
            half = p.wl // 2
            levels = lax.broadcasted_iota(jnp.int32, (1, tab.shape[0]), 1).astype(F32)
            hot_x = (digits[:, 1:2] * 128.0 + digits[:, 2:3] == levels).astype(F32).astype(BF16)
            hot_y = (digits[:, 3:4] * 128.0 + digits[:, 4:5] == levels).astype(F32).astype(BF16)
            emb = jnp.concatenate([dot(hot_x, tab[:, :half]), dot(hot_y, tab[:, half:])], axis=1)
            lay = side[:, : p.wl] + emb
            low_rows = lay.astype(BF16)
            lay_low[...] = low_rows
            lay_ref[...] = lay
            acc_t[...] = jnp.zeros_like(acc_t)
            acc_l[...] = jnp.zeros_like(acc_l)
        else:
            xt_ref, lay_low, lay_ref, ints_ref, intst_ref, acc_t_in, acc_l_in = in_refs
            n1t, i1t, ht, n1l, i1l, hl = outs[5:]
            x, low_rows = xt_ref[...], lay_low[...]
            acc_t[...] = acc_t_in[...]
            acc_l[...] = acc_l_in[...]
        seg_col = ints_ref[:, 0:1]
        seg_row = intst_ref[0:1, :]
        wait_for(lpad, sem_l)
        for k in range(nb):
            wl_out[k] = dot(spl[...], lpad[k]).astype(BF16)

        def block(k, core, x_at):
            wait_for(wpad.at[k], sem_t.at[k])
            if not exact_t:
                wpad[k, pl.ds(0, p.wt)] = dot(spt[...], wpad[k]).astype(BF16)
            out_copy = pltpu.make_async_copy(wpad.at[k, pl.ds(0, p.wt)], wt_out.at[k], sem_out)
            out_copy.start()
            own_t = (2 * x_at + core) ^ my_t
            w = wpad[k, pl.ds(0, p.wt)]
            wl = wl_out[k]
            raw = (dot(x, w[:, : 3 * p.ct]) + bt[own_t]).T
            raw_l = (dot(low_rows, wl[:, : 3 * p.cl]) + bl[own_t]).T
            for c in range(3):
                for h in range(nh):
                    top = raw[c * p.ct + h * HD : c * p.ct + (h + 1) * HD]
                    bot = raw_l[c * p.cl + h * LHD : c * p.cl + (h + 1) * LHD]
                    top, bot = top.astype(BF16), bot.astype(BF16)
                    if c == 0:
                        top = top * jnp.asarray(1.0 / math.sqrt(HD), BF16)
                        bot = bot * jnp.asarray(1.0 / math.sqrt(LHD), BF16)
                    qkv[k, c * nh + h, pl.ds(0, HD)] = top
                    qkv[k, c * nh + h, pl.ds(HD, LHD)] = bot
            for h in range(nh):
                scores = dot(qkv[k, nh + h], qkv[k, h], 0, 0)
                scores = jnp.where(seg_col == seg_row, scores, NEG_FILL)
                top_score = jnp.max(scores, axis=0, keepdims=True)
                expo = jnp.exp(scores - top_score)
                row_total = jnp.sum(expo, axis=0, keepdims=True)
                probs = (expo * (1.0 / row_total)).astype(BF16)
                mixed = dot(qkv[k, 2 * nh + h], probs).astype(BF16)
                ctx[k, h] = mixed
                ctx_rows[pl.ds(h * HD, HD)] = mixed[:HD]
                ctx_lay[pl.ds(h * LHD, LHD)] = mixed[HD:]
                lse_ref[k, pl.ds(h, 1), :] = top_score + jnp.log(row_total)
            acc_t[...] += dot(w[:, 3 * p.ct :], ctx_rows[...])
            acc_l[...] += dot(wl[:, 3 * p.cl : 4 * p.cl], ctx_lay[...])
            out_copy.wait()

        for k, (core, x_at) in enumerate(blocks):
            block(k, core, x_at)
        if first:
            acc_t_out[...] = acc_t[...]
            acc_l_out[...] = acc_l[...]
        else:
            for residual, acc, vec, n_ref, i_ref, h_ref in (
                (x.astype(F32), acc_t, vt, n1t, i1t, ht),
                (lay_ref[...], acc_l, vl, n1l, i1l, hl),
            ):
                normed, inv = norm_parts(residual + acc[...].T + vec[2:3])
                n_ref[...] = normed
                i_ref[...] = inv
                h_ref[...] = (normed * vec[3:4] + vec[4:5]).astype(BF16)

    outs = [
        shape((nb, p.wt, p.cols), BF16),
        shape((nb, p.wl, p.cols), BF16),
        shape((nb, 3 * nh, hw, rows), BF16),
        shape((nb, nh, hw, rows), BF16),
        shape((nb, 8, rows), F32),
    ]
    if first:
        outs += [
            shape((rows, p.wt), BF16),
            shape((rows, p.wl), BF16),
            shape((rows, p.wl), F32),
            shape((rows, 8), F32),
            shape((8, rows), F32),
            shape((p.wt, rows), F32),
            shape((p.wl, rows), F32),
        ]
    else:
        outs += [
            shape((rows, p.wt), F32),
            shape((rows, 1), F32),
            shape((rows, p.wt), BF16),
            shape((rows, p.wl), F32),
            shape((rows, 1), F32),
            shape((rows, p.wl), BF16),
        ]
    scratch = [
        pltpu.VMEM((nb, padded_t, p.cols), BF16),
        pltpu.VMEM((nb, padded_l, p.cols), BF16),
        pltpu.VMEM((p.wt, rows), F32),
        pltpu.VMEM((p.wl, rows), F32),
        pltpu.VMEM((p.ct, rows), BF16),
        pltpu.VMEM((p.cl, rows), BF16),
        pltpu.SemaphoreType.DMA((nb,)),
        pltpu.SemaphoreType.DMA,
        pltpu.SemaphoreType.DMA,
    ]
    args = (me2, bias_t, bias_l, vec_t, vec_l, spread_t, spread_l, *rows_in, *pieces)
    return kernel_call(
        body,
        outs,
        [SM] + [VM] * (6 + n_in) + [ANY] * n_piece,
        [ANY] + [VM] * (len(outs) - 1),
        scratch,
        args,
    )


def feed_forward(p, me2, pieces, w_lays, h_t, h_l, bin_t, bin_l, spread_t):
    rows = p.rows
    padded_t = p.n_dp * p.ra
    exact_t = p.ra == p.d_own
    root = 1.0 / math.sqrt(2.0)
    nb = p.n_t // 2

    def body(*refs):
        (me_ref, wl_a, wl_b, ht, hl, bt, bl, spt), refs = refs[:8], refs[8:]
        piece_refs, refs = refs[:4], refs[4:]
        outs, scratch = refs[:6], refs[6:]
        g_t, gp_t, g_l, gp_l = outs[:4]
        fpad, acc_t, acc_l, sem_t = scratch
        my_dp, my_t = me_ref[0], me_ref[1]
        for k in range(nb):
            for m in range(2):
                for y in range(2):
                    src = piece_refs[y].at[k] if m == 0 else piece_refs[2 + k].at[y]
                    for z in range(p.far):
                        row = pl.multiple_of(((z * 2 + y) ^ my_dp) * p.ra, 16)
                        pltpu.make_async_copy(
                            src.at[z], fpad.at[k, m, pl.ds(row, p.ra)], sem_t.at[k]
                        ).start()
        acc_t[...] = jnp.zeros_like(acc_t)
        acc_l[...] = jnp.zeros_like(acc_l)

        def gelu(u, g_ref, gp_ref, k):
            cdf = 0.5 + 0.5 * lax.erf(u * root)
            low = (u * cdf).astype(BF16)
            g_ref[k] = low
            dens = jnp.exp(u * u * -0.5) * (1.0 / math.sqrt(2.0 * math.pi))
            gp_ref[k] = (cdf + u * dens).astype(gp_ref.dtype)
            return low

        def block(k):
            wait_for(fpad.at[k], sem_t.at[k])
            if not exact_t:
                for m in range(2):
                    fpad[k, m, pl.ds(0, p.wt)] = dot(spt[...], fpad[k, m]).astype(BF16)
            own_t = (2 * k) ^ my_t
            g = gelu(dot(ht[...], fpad[k, 0, pl.ds(0, p.wt)]) + bt[own_t], g_t, gp_t, k)
            acc_t[...] += dot(g, fpad[k, 1, pl.ds(0, p.wt)], 1, 1)
            w = wl_b[2] if k else wl_a[0]
            up = w[:, 4 * p.cl : 4 * p.cl + p.hl]
            down = w[:, 4 * p.cl + p.hl : p.lay_cols]
            g = gelu(dot(hl[...], up) + bl[own_t], g_l, gp_l, k)
            acc_l[...] += dot(g, down, 1, 1)

        for k in range(nb):
            block(k)
        outs[4][...] = acc_t[...]
        outs[5][...] = acc_l[...]

    outs = [
        shape((nb, rows, p.ht), BF16),
        shape((nb, rows, p.ht), BF16),
        shape((nb, rows, p.hl), BF16),
        shape((nb, rows, p.hl), BF16),
    ]
    outs += [shape((rows, p.wt), F32), shape((rows, p.wl), F32)]
    scratch = [
        pltpu.VMEM((nb, 2, padded_t, p.ht), BF16),
        pltpu.VMEM((rows, p.wt), F32),
        pltpu.VMEM((rows, p.wl), F32),
        pltpu.SemaphoreType.DMA((nb,)),
    ]
    args = (me2, *w_lays, h_t, h_l, bin_t, bin_l, spread_t, *pieces)
    return kernel_call(
        body,
        outs,
        [SM] + [VM] * 7 + [ANY] * 4,
        [VM] * len(outs),
        scratch,
        args,
    )


def feed_middle(p, me2, pieces, w_lay, h_t, h_l, bin_t, bin_l, spread_t, rest_in):
    rows = p.rows
    padded_t = p.n_dp * p.ra
    exact_t = p.ra == p.d_own
    root = 1.0 / math.sqrt(2.0)
    nb = p.n_t // 2

    def body(*refs):
        (me_ref, wl, ht, hl, bt, bl, spt), refs = refs[:7], refs[7:]
        (acc_t_in, acc_l_in, n1t_, n1l_, c0, c1, c2, c3, vt, vl), refs = refs[:10], refs[10:]
        piece_refs, refs = refs[:4], refs[4:]
        n_out = 11 + p.n_t
        outs, scratch = refs[:n_out], refs[n_out:]
        out_tl = outs[11:]
        (low, high, gfl, dbt, dbl, df_t, df_l, gv_t, gv_l, dh_t, dh_l) = outs[:11]
        fpad, staged, acc_t, acc_l, g_t, gp_t, g_l, gp_l, sem_t, sem_out = scratch
        my_dp, my_t = me_ref[0], me_ref[1]
        for k in range(nb):
            for m in range(2):
                for y in range(2):
                    src = piece_refs[y].at[k] if m == 0 else piece_refs[2 + k].at[y]
                    for z in range(p.far):
                        row = pl.multiple_of(((z * 2 + y) ^ my_dp) * p.ra, 16)
                        pltpu.make_async_copy(
                            src.at[z], fpad.at[k, m, pl.ds(row, p.ra)], sem_t.at[k]
                        ).start()
        acc_t[...] = acc_t_in[...]
        acc_l[...] = acc_l_in[...]

        def gelu(u, g_ref, gp_ref, k):
            cdf = 0.5 + 0.5 * lax.erf(u * root)
            value = (u * cdf).astype(BF16)
            g_ref[k] = value
            dens = jnp.exp(u * u * -0.5) * (1.0 / math.sqrt(2.0 * math.pi))
            gp_ref[k] = cdf + u * dens
            return value

        for k in range(nb):
            wait_for(fpad.at[k], sem_t.at[k])
            if not exact_t:
                for m in range(2):
                    fpad[k, m, pl.ds(0, p.wt)] = dot(spt[...], fpad[k, m]).astype(BF16)
            own_t = (2 * k + 1) ^ my_t
            g = gelu(dot(ht[...], fpad[k, 0, pl.ds(0, p.wt)]) + bt[own_t], g_t, gp_t, k)
            acc_t[...] += dot(g, fpad[k, 1, pl.ds(0, p.wt)], 1, 1)
            w = wl[k]
            up = w[:, 4 * p.cl : 4 * p.cl + p.hl]
            down = w[:, 4 * p.cl + p.hl : p.lay_cols]
            g = gelu(dot(hl[...], up) + bl[own_t], g_l, gp_l, k)
            acc_l[...] += dot(g, down, 1, 1)
        for n1, acc, vec, begin, dr_ref, df_ref, gv in (
            (n1t_, acc_t, vt, 0, dh_t, df_t, gv_t),
            (n1l_, acc_l, vl, p.wt, dh_l, df_l, gv_l),
        ):
            width = n1.shape[1]
            per = p.quarter
            h1 = n1[...] * vec[3:4] + vec[4:5]
            n2, inv2 = norm_parts(h1 + acc[...] + vec[5:6])
            value = (n2 * vec[6:7] + vec[7:8]).astype(BF16)
            for k in range(p.n_t):
                out_tl[k][:, pl.ds(begin, width)] = value[k * p.quarter : (k + 1) * p.quarter]
            ct = jnp.concatenate([ref[:, begin : begin + width] for ref in (c0, c1, c2, c3)], axis=0).astype(F32)
            dr = norm_back(ct, n2, inv2, vec[6:7])
            dr_ref[...] = dr
            df_ref[...] = dr.astype(BF16)
            gv[...] = jnp.zeros_like(gv)
            gv[5:6] = col_sum(dr)
            gv[6:7] = col_sum(ct * n2)
            gv[7:8] = col_sum(ct)
        df, dfl = df_t[...], df_l[...]
        dfT, hT, dfTl, hTl = df.T, ht[...].T, dfl.T, hl[...].T
        for k in range(nb):
            du = dot(df, fpad[k, 1, pl.ds(0, p.wt)]) * gp_t[k]
            dbt[k] = col_sum(du)
            du_low = du.astype(BF16)
            grads = (dot(hT, du_low).astype(BF16), dot(dfT, g_t[k]).astype(BF16))
            for m in range(2):
                value = grads[m]
                if not exact_t:
                    value = dot(spt[...], value, 0, 0).astype(BF16)
                staged[k, m] = value
                slot = (lambda d, y, z: low.at[k, y, z]) if m == 0 else (lambda d, y, z: high.at[y, k, z])
                store_slots(p, staged.at[k, m], slot, my_dp, sem_out, [(0, p.ra, 0, p.ra, 0)])
            dh_t[...] += dot(du_low, fpad[k, 0, pl.ds(0, p.wt)], 1, 1)
            w = wl[k]
            up = w[:, 4 * p.cl : 4 * p.cl + p.hl]
            down = w[:, 4 * p.cl + p.hl : p.lay_cols]
            du = dot(dfl, down) * gp_l[k]
            dbl[k] = col_sum(du)
            du_low = du.astype(BF16)
            gfl[k, :, pl.ds(0, p.hl)] = dot(hTl, du_low).astype(BF16)
            gfl[k, :, pl.ds(p.hl, p.hl)] = dot(dfTl, g_l[k]).astype(BF16)
            dh_l[...] += dot(du_low, up, 1, 1)
        wait_for(staged, sem_out)

    outs = [
        shape((2, 2, p.far, p.ra, p.ht), BF16),
        shape((2, 2, p.far, p.ra, p.ht), BF16),
        shape((nb, p.wl, 2 * p.hl), BF16),
        shape((nb, 1, p.ht), F32),
        shape((nb, 1, p.hl), F32),
        shape((rows, p.wt), BF16),
        shape((rows, p.wl), BF16),
        shape((8, p.wt), F32),
        shape((8, p.wl), F32),
        shape((rows, p.wt), F32),
        shape((rows, p.wl), F32),
    ]
    outs += [shape((p.quarter, p.wt + p.wl), BF16)] * p.n_t
    scratch = [
        pltpu.VMEM((nb, 2, padded_t, p.ht), BF16),
        pltpu.VMEM((nb, 2, padded_t, p.ht), BF16),
        pltpu.VMEM((rows, p.wt), F32),
        pltpu.VMEM((rows, p.wl), F32),
        pltpu.VMEM((nb, rows, p.ht), BF16),
        pltpu.VMEM((nb, rows, p.ht), F32),
        pltpu.VMEM((nb, rows, p.hl), BF16),
        pltpu.VMEM((nb, rows, p.hl), F32),
        pltpu.SemaphoreType.DMA((nb,)),
        pltpu.SemaphoreType.DMA,
    ]
    args = (me2, w_lay, h_t, h_l, bin_t, bin_l, spread_t, *rest_in, *pieces)
    return kernel_call(
        body, outs, [SM] + [VM] * 16 + [ANY] * 4, [ANY, ANY] + [VM] * (len(outs) - 2), scratch, args
    )


def store_slots(p, staged, slot_of, my_dp, sem, slices):
    for z in range(p.far):
        for y in range(2):
            at = (z * 2 + y) ^ my_dp
            for dst, per, begin, count, off in slices:
                pltpu.make_async_copy(
                    staged.at[pl.ds(pl.multiple_of(at * per + begin, 16), count)],
                    slot_of(dst, y, z).at[pl.ds(off, count)],
                    sem,
                ).start()


def feed_backward(p, me2, pieces, w_lays, h_t, h_l, df_t, df_l, g_t, gp_t, g_l, gp_l, spread_t, prev):
    n_t, rows = p.n_t, p.rows
    padded_t = p.n_dp * p.ra
    exact_t = p.ra == p.d_own
    nb = n_t // 2

    def body(*refs):
        (me_ref, wl_a, wl_b, ht, hl, dft, dfl, gt, gpt, gl, gpl, spt), refs = refs[:12], refs[12:]
        (pt, pl_, n1t, i1t, n1l, i1l, vt, vl), refs = refs[:8], refs[8:]
        piece_refs, refs = refs[:4], refs[4:]
        outs, scratch = refs[:11], refs[11:]
        low, high, gfl, dbt, dbl = outs[:5]
        f_in, staged, acc_t, acc_l, sem_in, sem_out = scratch
        my_dp, my_t = me_ref[0], me_ref[1]
        for k in range(nb):
            for m in range(2):
                for y in range(2):
                    src = piece_refs[y].at[k] if m == 0 else piece_refs[2 + k].at[y]
                    for z in range(p.far):
                        row = pl.multiple_of(((z * 2 + y) ^ my_dp) * p.ra, 16)
                        pltpu.make_async_copy(
                            src.at[z], f_in.at[k, m, pl.ds(row, p.ra)], sem_in.at[k]
                        ).start()
        dfT, hT = dft[...].T, ht[...].T
        dfTl, hTl = dfl[...].T, hl[...].T
        acc_t[...] = pt[...]
        acc_l[...] = pl_[...]
        for k in range(nb):
            wait_for(f_in.at[k], sem_in.at[k])
            if not exact_t:
                for m in range(2):
                    f_in[k, m, pl.ds(0, p.wt)] = dot(spt[...], f_in[k, m]).astype(BF16)
            du = dot(dft[...], f_in[k, 1, pl.ds(0, p.wt)]) * gpt[k].astype(F32)
            dbt[k] = col_sum(du)
            du_low = du.astype(BF16)
            grads = (dot(hT, du_low).astype(BF16), dot(dfT, gt[k]).astype(BF16))
            for m in range(2):
                value = grads[m]
                if not exact_t:
                    value = dot(spt[...], value, 0, 0).astype(BF16)
                staged[k, m] = value
                if m == 0:
                    store_slots(p, staged.at[k, m], lambda d, y, z: low.at[k, y, z], my_dp, sem_out, [(0, p.ra, 0, p.ra, 0)])
                else:
                    store_slots(p, staged.at[k, m], lambda d, y, z: high.at[y, k, z], my_dp, sem_out, [(0, p.ra, 0, p.ra, 0)])
            acc_t[...] += dot(du_low, f_in[k, 0, pl.ds(0, p.wt)], 1, 1)
            w = wl_b[2] if k else wl_a[0]
            up = w[:, 4 * p.cl : 4 * p.cl + p.hl]
            down = w[:, 4 * p.cl + p.hl : p.lay_cols]
            du = dot(dfl[...], down) * gpl[k].astype(F32)
            dbl[k] = col_sum(du)
            du_low = du.astype(BF16)
            gfl[k, :, pl.ds(0, p.hl)] = dot(hTl, du_low).astype(BF16)
            gfl[k, :, pl.ds(p.hl, p.hl)] = dot(dfTl, gl[k]).astype(BF16)
            acc_l[...] += dot(du_low, up, 1, 1)
        dr1t, dr1l, dat, dal, gvt, gvl = outs[5:]
        for acc, n1, i1, vec, o, low_o, gv in (
            (acc_t, n1t, i1t, vt, dr1t, dat, gvt),
            (acc_l, n1l, i1l, vl, dr1l, dal, gvl),
        ):
            dh = acc[...]
            n = n1[...]
            dr1 = norm_back(dh, n, i1[...], vec[3:4])
            o[...] = dr1
            low_o[...] = dr1.astype(BF16)
            gv[...] = jnp.zeros_like(gv)
            gv[2:3] = col_sum(dr1)
            gv[3:4] = col_sum(dh * n)
            gv[4:5] = col_sum(dh)
        wait_for(staged, sem_out)

    outs = [
        shape((2, 2, p.far, p.ra, p.ht), BF16),
        shape((2, 2, p.far, p.ra, p.ht), BF16),
        shape((nb, p.wl, 2 * p.hl), BF16),
        shape((nb, 1, p.ht), F32),
        shape((nb, 1, p.hl), F32),
    ]
    args = [me2, *w_lays, h_t, h_l, df_t, df_l, g_t, gp_t, g_l, gp_l, spread_t]
    args += list(prev) + list(pieces)
    outs += [
        shape((rows, p.wt), F32),
        shape((rows, p.wl), F32),
        shape((rows, p.wt), BF16),
        shape((rows, p.wl), BF16),
        shape((8, p.wt), F32),
        shape((8, p.wl), F32),
    ]
    scratch = [
        pltpu.VMEM((nb, 2, padded_t, p.ht), BF16),
        pltpu.VMEM((nb, 2, padded_t, p.ht), BF16),
        pltpu.VMEM((rows, p.wt), F32),
        pltpu.VMEM((rows, p.wl), F32),
        pltpu.SemaphoreType.DMA((nb,)),
        pltpu.SemaphoreType.DMA,
    ]
    specs = [SM] + [VM] * (len(args) - 5) + [ANY] * 4
    return kernel_call(
        body, outs, specs, [ANY, ANY] + [VM] * (len(outs) - 2), scratch, args
    )


def attend_backward(p, me2, xs, arrays, gfls, x_low, lay_low, ints, ints_t, da_t, da_l, spread_t, spread_l, prev, last):
    n_t, rows, hw, nh = p.n_t, p.rows, p.hw, p.heads
    padded_t, padded_l = p.n_dp * p.ra, p.n_dp * p.rl
    exact_t = p.ra == p.d_own
    nb = len(xs)
    n_prev, n_core = len(prev), len(gfls)

    def body(*refs):
        (me_ref, xl, ll, ir, itr, dat, dal, spt, spl), refs = refs[:9], refs[9:]
        (w_any, wl_ref, qkv_r, ctx_r, lse_r), refs = refs[:5], refs[5:]
        gfl_refs, refs = refs[:n_core], refs[n_core:]
        prev_refs, refs = refs[:n_prev], refs[n_prev:]
        n_out = 2 * n_core + 4
        outs, scratch = refs[:n_out], refs[n_out:]
        slot_refs = [outs[2 * c : 2 * c + 2] for c in range(n_core)]
        gb_t, gb_l, out_a, out_b = outs[2 * n_core :]
        (w_in, staged, staged_l, acc_t, acc_l, dctx, ctx_s, ctx_l, dp_t, dp_l, bin_rows, sem_in,
         sem_out, sem_bin) = scratch
        my_dp, my_t = me_ref[0], me_ref[1]
        for k, (_, x, _) in enumerate(xs):
            pltpu.make_async_copy(w_any.at[x], w_in.at[k], sem_in.at[k]).start()
        xT, lT = xl[...].T, ll[...].T
        daT, dalT = dat[...].T, dal[...].T
        seg_col, seg_row = ir[:, 0:1], itr[0:1, :]
        if prev:
            acc_t[...] = prev_refs[0][...]
            acc_l[...] = prev_refs[1][...]
        else:
            acc_t[...] = jnp.zeros_like(acc_t)
            acc_l[...] = jnp.zeros_like(acc_l)
        ones = jnp.ones((16, rows), BF16)
        for k, (c, x, g_at) in enumerate(xs):
            low, high = slot_refs[c]
            at_k = sum(1 for member in xs[:k] if member[0] == c)
            wait_for(w_in.at[k], sem_in.at[k])
            w = w_in[k]
            wl = wl_ref[x]
            d_t = dot(dat[...], w[:, 3 * p.ct :]).T
            d_l = dot(dal[...], wl[:, 3 * p.cl : 4 * p.cl]).T
            for h in range(nh):
                dctx[h, pl.ds(0, HD)] = d_t[h * HD : (h + 1) * HD].astype(BF16)
                dctx[h, pl.ds(HD, LHD)] = d_l[h * LHD : (h + 1) * LHD].astype(BF16)
                ctx_s[pl.ds(h * HD, HD)] = ctx_r[x, h, pl.ds(0, HD)]
                ctx_l[pl.ds(h * LHD, LHD)] = ctx_r[x, h, pl.ds(HD, LHD)]

            for h in range(nh):
                q, key, val = qkv_r[x, h], qkv_r[x, nh + h], qkv_r[x, 2 * nh + h]
                dc = dctx[h]
                scores = dot(key, q, 0, 0)
                probs = jnp.exp(
                    jnp.where(seg_col == seg_row, scores, NEG_FILL) - lse_r[x, pl.ds(h, 1), :]
                )
                low_p = probs.astype(BF16)
                prod = dc.astype(F32) * ctx_r[x, h].astype(F32)
                sum_lay = jnp.sum(prod[HD:], axis=0, keepdims=True)
                sum_all = jnp.sum(prod[:HD], axis=0, keepdims=True) + sum_lay
                dz_all = probs * (dot(val, dc, 0, 0) - sum_all)
                dz_lay = probs * (dot(val[HD:], dc[HD:], 0, 0) - sum_lay)
                ds_t, ds_l = dz_all.astype(BF16), dz_lay.astype(BF16)
                dv = dot(dc, low_p, 1, 1)
                dq_t = dot(key[:HD], ds_t) * (1.0 / math.sqrt(HD))
                dq_l = dot(key[HD:], ds_l) * (1.0 / math.sqrt(LHD))
                dk_t = dot(q[:HD], ds_t, 1, 1)
                dk_l = dot(q[HD:], ds_l, 1, 1)
                for m, (top, bot) in enumerate(((dq_t, dq_l), (dk_t, dk_l), (dv[:HD], dv[HD:]))):
                    dp_t[pl.ds(m * p.ct + h * HD, HD)] = top.astype(BF16)
                    dp_l[pl.ds(m * p.cl + h * LHD, LHD)] = bot.astype(BF16)
            gb_t[k] = dot(ones, dp_t[...], 1, 1)[:8]
            gb_l[k] = dot(ones, dp_l[...], 1, 1)[:8]
            acc_t[...] += dot(w[:, : 3 * p.ct], dp_t[...])
            acc_l[...] += dot(wl[:, : 3 * p.cl], dp_l[...])
            grad = jnp.concatenate(
                [dot(xT, dp_t[...], 1, 1), dot(daT, ctx_s[...], 1, 1)], axis=1
            ).astype(BF16)
            if not exact_t:
                grad = dot(spt[...], grad, 0, 0).astype(BF16)
            staged[k] = grad
            fill = p.cols - p.lay_cols
            grad_l = jnp.concatenate(
                [
                    dot(lT, dp_l[...], 1, 1),
                    dot(dalT, ctx_l[...], 1, 1),
                    gfl_refs[c][g_at].astype(F32),
                    jnp.zeros((p.wl, fill), F32),
                ],
                axis=1,
            ).astype(BF16)
            staged_l[k] = dot(spl[...], grad_l, 0, 0).astype(BF16)
            rest = p.ra - p.half_a
            slot = lambda d, y, z: high.at[y, at_k, z] if d else low.at[at_k, y, z]
            slices = [(0, p.ra, 0, p.half_a, 0)]
            if rest:
                slices.append((1, p.ra, p.half_a, rest, 0))
            store_slots(p, staged.at[k], slot, my_dp, sem_out.at[0], slices)
            store_slots(p, staged_l.at[k], slot, my_dp, sem_out.at[1], [(1, p.rl, 0, p.rl, rest)])
        if last:
            gt = prev_refs[2][...] + acc_t[...].T
            gl = prev_refs[3][...] + acc_l[...].T
            out_a[:, pl.ds(0, p.wt)] = gt.astype(BF16)
            out_a[:, pl.ds(p.wt, p.wl)] = gl.astype(BF16)
            half = p.wl // 2
            bins = bin_rows.shape[0]
            levels = lax.broadcasted_iota(jnp.int32, (bins, 1), 0).astype(F32)
            for m in range(2):
                row = itr[1 + 2 * m : 2 + 2 * m, :] * 128.0 + itr[2 + 2 * m : 3 + 2 * m, :]
                hot = (levels == row).astype(F32).astype(BF16)
                part = gl[:, m * half : (m + 1) * half]
                top = part.astype(BF16)
                rest_part = (part - top.astype(F32)).astype(BF16)
                both = dot(hot, jnp.concatenate([top, rest_part], axis=1))
                bin_rows[:, pl.ds(m * half, half)] = (both[:, :half] + both[:, half:]).astype(BF16)
            if p.per % 16:
                pltpu.make_async_copy(bin_rows, out_b, sem_bin).start()
            else:
                for r in range(p.total):
                    z, y, x, c = r // 8, (r // 4) % 2, (r // 2) % 2, r % 2
                    at = ((r // n_t) ^ my_dp) * n_t + ((r % n_t) ^ my_t)
                    pltpu.make_async_copy(
                        bin_rows.at[pl.ds(pl.multiple_of(at * p.per, 16), p.per)],
                        out_b.at[c, y, x, z],
                        sem_bin,
                    ).start()
            wait_for(bin_rows, sem_bin)
        else:
            out_a[...] = acc_t[...]
            out_b[...] = acc_l[...]
        wait_for(staged, sem_out.at[0])
        wait_for(staged_l, sem_out.at[1])

    half_b = p.ra + p.rl - p.half_a
    slots_out = []
    for c in range(n_core):
        held = sum(1 for member in xs if member[0] == c)
        slots_out += [
            shape((held, 2, p.far, p.half_a, p.cols), BF16),
            shape((2, held, p.far, half_b, p.cols), BF16),
        ]
    outs = slots_out + [
        shape((nb, 8, 3 * p.ct), F32),
        shape((nb, 8, 3 * p.cl), F32),
    ]
    args = [me2, x_low, lay_low, ints, ints_t, da_t, da_l, spread_t, spread_l]
    specs = [SM] + [VM] * 8 + [ANY] + [VM] * (4 + n_core + n_prev)
    args += [*arrays, *gfls, *prev]
    if last:
        bins = p.per * p.total
        slots = (bins,) if p.per % 16 else (2, 2, 2, p.far, p.per)
        outs += [shape((rows, p.wt + p.wl), BF16), shape((*slots, p.wl), BF16)]
    else:
        outs += [shape((p.wt, rows), F32), shape((p.wl, rows), F32)]
    scratch = [
        pltpu.VMEM((nb, p.wt, p.cols), BF16),
        pltpu.VMEM((nb, padded_t, p.cols), BF16),
        pltpu.VMEM((nb, padded_l, p.cols), BF16),
        pltpu.VMEM((p.wt, rows), F32),
        pltpu.VMEM((p.wl, rows), F32),
        pltpu.VMEM((nh, hw, rows), BF16),
        pltpu.VMEM((p.ct, rows), BF16),
        pltpu.VMEM((p.cl, rows), BF16),
        pltpu.VMEM((3 * p.ct, rows), BF16),
        pltpu.VMEM((3 * p.cl, rows), BF16),
        pltpu.VMEM((p.per * p.total, p.wl), BF16),
        pltpu.SemaphoreType.DMA((nb,)),
        pltpu.SemaphoreType.DMA((2,)),
        pltpu.SemaphoreType.DMA,
    ]
    out_specs = [ANY] * (2 * n_core) + [VM] * 3 + [ANY if last else VM]
    return kernel_call(body, outs, specs, out_specs, scratch, args)


def tie(*groups):
    leaves, tree = jax.tree.flatten(groups)
    return jax.tree.unflatten(tree, lax.optimization_barrier(leaves))


def after(values, *others):
    return tie(values, *others)[0]


def line_of(shard, total):
    return [shard] + [xor_send(shard, total, 8 * r) for r in range(1, total // 8)]


def line_doubled(shard, total, others):
    line = [shard]
    while 8 * len(line) < total:
        held = jnp.stack(line)
        if len(line) > 1:
            held = after(held, others)
        theirs = xor_send(held, total, 8 * len(line))
        line = line + [theirs[z] for z in range(len(line))]
    return line


def halves_of(line, half):
    low = jnp.stack([member[:half] for member in line])
    high = jnp.stack([member[half:] for member in line])
    return low, high


def add_low(mine, theirs):
    return to_low(mine.astype(F32) + theirs.astype(F32))


def reduce_second(mine, got):
    send = [add_low(mine[k][1], got[k][1]) for k in range(2)]
    keep = [add_low(mine[k][0], got[k][0]) for k in range(2)]
    return send, keep


def reduce_line_parts(keep, got):
    return [
        jnp.concatenate([add_low(keep[k][z], got[k][z]) for k in range(2)], axis=0)
        for z in range(keep[0].shape[0])
    ]


def send_line(line, total):
    return line[:1] + [xor_send(line[z], total, 8 * z) for z in range(1, len(line))]


def add_line(line):
    out = line[0].astype(F32)
    for member in line[1:]:
        out = out + member.astype(F32)
    return out


def update_all(factor, matrices, flat, grads):
    states = [member for group in (*matrices, *flat) for member in group]

    def body(*refs):
        factor_ref, grads = refs[0], refs[1:7]
        ins, outs = refs[7:25], refs[25:]
        scale = factor_ref[0, 0]
        for k in range(6):
            w, m, v = (ins[3 * k + j][...] for j in range(3))
            results = adamw_step(
                w, m, v, grads[k][...].astype(F32) * scale, WEIGHT_DECAY if k < 4 else 0.0, LEARN_RATES[k]
            )
            for j in range(3):
                outs[3 * k + j][...] = results[j]

    return list(
        kernel_call(
            body,
            [shape(v.shape, F32) for v in states],
            [SM] + [VM] * 24,
            [VM] * 18,
            [],
            (factor.reshape(1, 1), *grads, *states),
        )
    )


def relative(blocks, me):
    total = blocks.shape[0]
    step = 1
    while step < total:
        pairs = blocks.reshape(total // (2 * step), 2, step, *blocks.shape[1:])
        swapped = jnp.stack([pairs[:, 1], pairs[:, 0]], axis=1)
        blocks = jnp.where((me // step) % 2 == 0, pairs, swapped).reshape(blocks.shape)
        step = step * 2
    return blocks


def on_device(
    text_in,
    layout_in,
    segment_ids,
    box_bins,
    text_cot,
    layout_cot,
    attend_text,
    attend_text_mean,
    attend_text_square,
    feed_text,
    feed_text_mean,
    feed_text_square,
    attend_layout,
    attend_layout_mean,
    attend_layout_square,
    feed_layout,
    feed_layout_mean,
    feed_layout_square,
    vectors,
    vectors_mean,
    vectors_square,
    tables,
    tables_mean,
    tables_square,
):
    n_dp, n_t = lax.axis_size("dp"), lax.axis_size("tensor")
    total = n_dp * n_t
    t_pos = lax.axis_index("tensor")
    pages, quarter, wt = text_in.shape
    wl = layout_in.shape[1] // quarter
    d_own, dl_own = attend_text.shape[0], attend_layout.shape[0]
    ct, cl = attend_text.shape[2], attend_layout.shape[2]
    ht, hl = feed_text.shape[2], feed_layout.shape[2]


    p = Plan(n_dp, n_t, quarter, wt, wl, ct, cl, ht, hl, tables.shape[0] // wl)
    me = lax.axis_index("dp") * n_t + t_pos
    me2 = jnp.stack([lax.axis_index("dp"), t_pos]).astype(jnp.int32)
    lay_cols = p.lay_cols

    def pad_rows(values, count):
        return jnp.pad(values, ((0, count - values.shape[0]), (0, 0)))

    lay_pack = jnp.concatenate(
        [
            to_low(attend_layout).reshape(dl_own, 4 * cl),
            to_low(feed_layout).reshape(dl_own, 2 * hl),
        ],
        axis=1,
    )
    lay_pack = jnp.pad(lay_pack, ((0, p.rl - dl_own), (0, p.cols - lay_cols)))
    attend_pack = jnp.concatenate(
        [pad_rows(to_low(attend_text).reshape(d_own, p.cols), p.ra), lay_pack]
    )
    low_feed = to_low(feed_text)
    feed_pack = jnp.concatenate(
        [pad_rows(low_feed[:, 0], p.ra), pad_rows(low_feed[:, 1], p.ra)]
    )
    bins = box_bins.reshape(pages, quarter, 2)
    digits = jnp.stack(
        [segment_ids, bins[..., 0] // 128, bins[..., 0] % 128, bins[..., 1] // 128, bins[..., 1] % 128],
        axis=-1,
    )
    packed_in = jnp.concatenate(
        [
            text_in,
            layout_in.reshape(pages, quarter, wl),
            jnp.pad(to_low(digits), ((0, 0), (0, 0), (0, 59))),
        ],
        axis=2,
    )
    packed_cot = jnp.concatenate([text_cot, layout_cot.reshape(pages, quarter, wl)], axis=2)

    def blocks_of(values):
        return [lax.dynamic_index_in_dim(values, t_pos ^ r, 0, keepdims=False) for r in range(n_t)]

    def send_blocks(blocks):
        return [blocks[0]] + [xor_send(blocks[r], total, r) for r in range(1, n_t)]

    def page_of(values):
        return send_blocks(blocks_of(values))

    def send_rows(page):
        return send_blocks(page.reshape(n_t, quarter, page.shape[-1]))

    def pages_of(blocks):
        out = jnp.zeros((n_t,) + blocks[0].shape, blocks[0].dtype)
        for r in range(n_t):
            out = lax.dynamic_update_slice(out, blocks[r][None], (t_pos ^ r, 0, 0))
        return out

    send = lambda values, distance: xor_send(values, total, distance)
    packed_cot = blocks_of(packed_cot)

    line_a = line_of(attend_pack, total)
    xin = page_of(packed_in)
    low, high = halves_of(line_a, p.half_a)
    line_f = line_doubled(feed_pack, total, line_a)
    low0, high0 = jnp.stack([low, send(low, 2)]), jnp.stack([high, send(high, 4)])
    low4, high2 = send(low0, 4), send(high0, 2)
    low1, high1 = send(low0, 1), send(high0, 1)
    late_vectors, late_tables = after((vectors, tables), low0, high0)
    parts = split_vectors(late_vectors, [wt, wl], [n_t * ht, n_t * hl])
    biases, vecs, bins_in = [], [], []
    for s, width in ((0, ct), (1, cl)):
        vec, hidden = parts[s]
        biases.append(
            jnp.concatenate(
                [
                    vec[0].reshape(n_t, 1, width),
                    jnp.zeros((n_t, 1, width), F32),
                    vec[1].reshape(n_t, 1, width),
                ],
                axis=2,
            )
        )
        vecs.append(jnp.stack(vec))
        bins_in.append(hidden.reshape(n_t, 1, -1))
    table_rows = to_low(late_tables.reshape(-1, wl))
    spread_t = p.spread(d_own, p.ra) if p.ra != d_own else jnp.zeros((16, 128), BF16)
    spread_l = p.spread(dl_own, p.rl)

    flow, fhigh = halves_of(after(line_f, low0, high0), p.ra)
    flow, fhigh = after((flow, fhigh), low4, high2)
    att_fix = (biases[0], biases[1], vecs[0], vecs[1], spread_t, spread_l)
    low5, high3 = send(low4, 1), send(high2, 1)
    flow_x, fhigh_y = send(flow, 2), send(fhigh, 4)
    (w_all0, w_lay0, qkv0, ctx0, lse0, *row_state) = attend_forward(
        p, me2, ((0, 0),), (*after(xin, bins_in, packed_cot), table_rows), *att_fix, [low0, low4, high0, high2]
    )
    row_state, qkv0, low5, high3, low1, high1, flow_x, fhigh_y = tie(
        row_state, qkv0, low5, high3, low1, high1, flow_x, fhigh_y
    )
    flow0, fhigh0 = jnp.stack([flow, flow_x]), jnp.stack([fhigh, fhigh_y])
    row_state = after(row_state, flow0, fhigh0)
    flow4, fhigh2 = send(flow0, 4), send(fhigh0, 2)
    flow1, fhigh1 = send(flow0, 1), send(fhigh0, 1)
    (w_all1, w_lay1, qkv1, ctx1, lse1, n1t, i1t, h_t, n1l, i1l, h_l) = attend_forward(
        p, me2, ((1, 0), (1, 1), (0, 1)), row_state, *att_fix,
        [low0, low4, high0, high2, low1, low5, high1, high3],
    )
    x_low, lay_low, _, ints, ints_t = row_state[:5]
    n1t, n1l, h_t, h_l, w_lay1, flow4, fhigh2, packed_cot = tie(
        n1t, n1l, h_t, h_l, w_lay1, flow4, fhigh2, packed_cot
    )
    flow5, fhigh3 = send(flow4, 1), send(fhigh2, 1)
    cots = send_blocks(packed_cot)
    (g_t0, gp_t0, g_l0, gp_l0, acc_t, acc_l) = feed_forward(
        p, me2, [flow0, flow4, fhigh0, fhigh2], (w_lay0, w_lay1), h_t, h_l, bins_in[0], bins_in[1], spread_t
    )
    acc_t, acc_l, flow5, fhigh3, flow1, fhigh1, cots = tie(
        acc_t, acc_l, flow5, fhigh3, flow1, fhigh1, cots
    )
    (gf_low1, gf_high1, gfl1, dbt1, dbl1, df_t, df_l, gv2t, gv2l, acc_t, acc_l, *out_rows) = feed_middle(
        p, me2, [flow1, flow5, fhigh1, fhigh3], w_lay1, h_t, h_l, bins_in[0], bins_in[1], spread_t,
        (acc_t, acc_l, n1t, n1l, *cots, vecs[0], vecs[1]),
    )
    rows_out = send_blocks(out_rows)
    got = [send(gf_low1, 1), send(gf_high1, 1)]
    (gf_low0, gf_high0, gfl0, dbt0, dbl0, dr1t, dr1l, da_t, da_l, gv1t, gv1l) = feed_backward(
        p, me2, [flow0, flow4, fhigh0, fhigh2], (w_lay0, w_lay1), h_t, h_l, df_t, df_l, g_t0, gp_t0, g_l0, gp_l0, spread_t,
        (acc_t, acc_l, n1t, i1t, n1l, i1l, vecs[0], vecs[1])
    )
    got, rows_out, gf_low0, gf_high0, gfl0, dbt0, dbl0, dr1t, dr1l, da_t, da_l, gv1t, gv1l = tie(
        got, rows_out, gf_low0, gf_high0, gfl0, dbt0, dbl0, dr1t, dr1l, da_t, da_l, gv1t, gv1l
    )
    next_f = [add_low(gf_low0[1], got[0][1]), add_low(gf_high0[1], got[1][1])]
    da_t, got_feed = after(da_t, next_f), got
    got_f = [send(next_f[0], 2), send(next_f[1], 4)]
    att_args = (x_low, lay_low, ints, ints_t, da_t, da_l, spread_t, spread_l)
    first_arrays, arrays = (w_all0, w_lay0, qkv0, ctx0, lse0), (w_all1, w_lay1, qkv1, ctx1, lse1)
    (low_x1, high_x1, ga_low1, ga_high1, gb_t1, gb_l1, acc_t, acc_l) = attend_backward(
        p, me2, ((1, 0, 0), (1, 1, 1), (0, 2, 1)), arrays, (gfl0, gfl1), *att_args, (), False
    )
    got_f, low_x1, high_x1, ga_low1, ga_high1, gb_t1, gb_l1, acc_t, acc_l = tie(
        got_f, low_x1, high_x1, ga_low1, ga_high1, gb_t1, gb_l1, acc_t, acc_l
    )
    stay = after((gf_low0, gf_high0, got_feed[0], got_feed[1]), got_f)
    keep_f = [add_low(stay[k][0], stay[2 + k][0]) for k in range(2)]
    next_f = [add_low(keep_f[k][1], got_f[k][1]) for k in range(2)]
    keep_f = [add_low(keep_f[k][0], got_f[k][0]) for k in range(2)]
    acc_t = after(acc_t, next_f)
    got = [send(ga_low1, 1), send(ga_high1, 1)]
    got_f = [send(next_f[0], 4), send(next_f[1], 2)]
    (low_x0, high_x0, gb_t00, gb_l00, grad_rows, table_grad) = attend_backward(
        p, me2, ((0, 0, 0),), first_arrays, (gfl0,), *att_args, (acc_t, acc_l, dr1t, dr1l), True
    )
    got, got_f, low_x0, high_x0, gb_t00, gb_l00, grad_rows, table_grad = tie(
        got, got_f, low_x0, high_x0, gb_t00, gb_l00, grad_rows, table_grad
    )
    if p.per % 16:
        table_grad = relative(table_grad.reshape(total, p.per, wl), me)
        table_grad = table_grad.reshape(p.far, 2, 2, 2, p.per, wl).transpose(3, 1, 2, 0, 4, 5)
    table_got = send(table_grad[1], 1)
    low_x1 = add_low(low_x1[0], got[0][1])
    got_low = send(low_x1, 2)
    rest = p.ra - p.half_a
    spare = high_x0.shape[-2] - rest - p.per
    edges = ((0, 0), (0, 0), (0, 0), (rest, spare), (lay_cols, p.cols - lay_cols - wl))
    table_sum = jnp.pad(add_low(table_grad[0], after(table_got, low_x1)), edges)
    both = [jnp.concatenate([high_x0[y], high_x1[y]]) for y in range(2)]
    next_high = to_low(both[1].astype(F32) + got[1][1].astype(F32) + table_sum[1].astype(F32))
    got_high = send(next_high, 4)
    line_f = send_line(reduce_line_parts(keep_f, after(got_f, next_high)), total)
    low = to_low(low_x0[0].astype(F32) + got[0][0].astype(F32) + got_low.astype(F32))
    got_low = send(low[1], 4)
    high = to_low(
        both[0].astype(F32)
        + got[1][0].astype(F32)
        + table_sum[0].astype(F32)
        + got_high.astype(F32)
    )
    got_high = send(high[1], 2)
    pieces = (gb_t1, gb_l1, gb_t00, gb_l00, dbt0, dbt1, dbl0, dbl1, gv1t, gv1l, gv2t, gv2l)
    (gb_t1, gb_l1, gb_t00, gb_l00, dbt0, dbt1, dbl0, dbl1, gv1t, gv1l, gv2t, gv2l) = after(
        pieces, next_high
    )
    gb_t0 = jnp.concatenate([gb_t00, gb_t1[2:]])
    gb_l0 = jnp.concatenate([gb_l00, gb_l1[2:]])
    feed_sum = add_line(after(line_f, low, high))
    line_a = reduce_line_parts((low[0], high[0]), (got_low, got_high))
    rows_out, grad_rows = after((rows_out, grad_rows), line_a)
    late_pos = after(t_pos, next_high)
    line_a = send_line(line_a, total)
    rows_grad = send_rows(grad_rows)
    feed_sum = after(feed_sum, line_a[1])
    rows_out, rows_grad = pages_of(rows_out), pages_of(rows_grad)
    row_outputs = (
        rows_out[:, :, :wt],
        rows_out[:, :, wt:].reshape(pages, quarter * wl),
        rows_grad[:, :, :wt].astype(F32),
        rows_grad[:, :, wt:].astype(F32).reshape(pages, quarter * wl),
    )
    attend_sum = add_line(after(line_a, row_outputs[:2]))

    def by_block(odd, even):
        both = jnp.stack([even[0], odd[0], even[1], odd[1]]).reshape(n_t, -1)
        order = jnp.arange(n_t) ^ late_pos
        hot = order[:, None] == jnp.arange(n_t)[None, :]
        return jnp.sum(jnp.where(hot[:, :, None], both[None], 0.0), axis=1).reshape(-1)

    gv_t, gv_l = gv2t + gv1t, gv2l + gv1l
    vector_grad = jnp.concatenate(
        [
            by_block(gb_t1[:, 0, : ct], gb_t0[:, 0, : ct]),
            by_block(gb_t1[:, 0, 2 * ct :], gb_t0[:, 0, 2 * ct :]),
            gv_t[2:].reshape(-1),
            by_block(dbt1, dbt0),
            by_block(gb_l1[:, 0, : cl], gb_l0[:, 0, : cl]),
            by_block(gb_l1[:, 0, 2 * cl :], gb_l0[:, 0, 2 * cl :]),
            gv_l[2:].reshape(-1),
            by_block(dbl1, dbl0),
        ]
    )
    own_sq = jnp.sum(feed_sum * feed_sum) + jnp.sum(attend_sum * attend_sum)
    n_vec = vector_grad.shape[0]
    summed = jnp.pad(vector_grad, (0, round_up(n_vec + 1, 1024) - n_vec)).reshape(-1, 128)
    spot = (lax.broadcasted_iota(jnp.int32, summed.shape, 0) == n_vec // 128) & (
        lax.broadcasted_iota(jnp.int32, summed.shape, 1) == n_vec % 128
    )
    summed = jnp.where(spot, own_sq, summed)
    spread_table = to_low(attend_sum[p.ra : p.ra + p.per, lay_cols : lay_cols + wl])
    distance = total // 2
    while distance:
        other = send(summed, distance)
        theirs = send(after(spread_table, summed), distance)
        summed = summed + other
        bit = (me // distance) % 2
        spread_table = jnp.where(
            bit == 0, jnp.stack([spread_table, theirs]), jnp.stack([theirs, spread_table])
        )
        distance = distance // 2
    deep = spread_table.ndim - 2
    order = tuple(range(deep - 1, -1, -1)) + (deep, deep + 1)
    table_grad = spread_table.transpose(order).reshape(-1, 128)
    vector_grad = summed
    all_sq = jnp.sum(jnp.where(spot, 0.0, summed * summed))
    shared_sq = all_sq + summed[n_vec // 128, n_vec % 128]
    clip_norm = jnp.sqrt(shared_sq)
    factor = jnp.minimum(1.0, CLIP_NORM / (clip_norm + 1e-06))
    flat = [
        [v.reshape(-1, 128) for v in group]
        for group in ((vectors, vectors_mean, vectors_square), (tables, tables_mean, tables_square))
    ]
    lay_sum = attend_sum[p.ra : p.ra + dl_own]
    grads = (
        attend_sum[:d_own].reshape(d_own, 4, ct),
        jnp.stack([feed_sum[:d_own], feed_sum[p.ra : p.ra + d_own]], axis=1),
        lay_sum[:, : 4 * cl].reshape(dl_own, 4, cl),
        lay_sum[:, 4 * cl : lay_cols].reshape(dl_own, 2, hl),
        vector_grad[: n_vec // 128],
        table_grad,
    )
    matrices = (
        (attend_text, attend_text_mean, attend_text_square),
        (feed_text, feed_text_mean, feed_text_square),
        (attend_layout, attend_layout_mean, attend_layout_square),
        (feed_layout, feed_layout_mean, feed_layout_square),
    )
    updated = update_all(factor, matrices, flat, grads)
    updated[12:] = [v.reshape(-1) for v in updated[12:]]
    return (
        *row_outputs,
        *updated,
        clip_norm,
    )


def solution(mesh):
    rows3, rows2, cols3 = P("dp", "tensor", None), P("dp", "tensor"), P("dp", None, "tensor")
    in_specs = (rows3, rows2, rows2, rows2, rows3, rows2) + (cols3,) * 12 + (P(),) * 6
    out_specs = (rows3, rows2, rows3, rows2) + (cols3,) * 12 + (P(),) * 7
    return jax.shard_map(
        on_device, mesh=mesh, in_specs=in_specs, out_specs=out_specs, check_vma=False
    )
```
